32 devices in a mesh: dp: 4 (over y, x), space: 8 (over z, core).
Axes of the slice: x: 2, y: 2, z: 4, core: 2. Of those that a mesh axis runs over, the one named last changes fastest.
Arguments:
- block_input: bfloat16 [4, 2304, 8, 192], P('dp', 'space'), may hold values from -6 to 6
- cotangent: bfloat16 [4, 2304, 8, 192], P('dp', 'space'), may hold values from -6 to 6
- params: float32 [1216512], P(('dp', 'space')), as said below
- send_rows: int32 [4, 8, 8, 288], P('dp', None, 'space'), may hold values from 0 to 2303, as said below
- window_band: int32 [4, 256], P('dp', 'space'), may hold values from 0 to 19
- level_count: int32 [4, 2304], P('dp', 'space'), may hold values from 1 to 8
Outputs:
- block_output: bfloat16 [4, 2304, 8, 192], P('dp', 'space')
- input_grad: float32 [4, 2304, 8, 192], P('dp', 'space')
- param_grad: float32 [1216512], P(('dp', 'space'))
The draws below stay inside these ranges and needn't reach their ends.
Inputs may be any that keep to these rules, and one draw needn't show every extreme that they name: For each sample and each source device e, the entries send_rows[s, :, e, :] are a permutation of 0 to 2303. `params`: laid out in the order of the statement's segments; the padding is unused.
All inputs are finite; a program needn't handle non-finite values.
Results may differ from the reference program's by a relative error of at most 0.013.
The reference program's roundings to bfloat16 on the way count: a program that leaves them out, or rounds other values in their place, can miss the bound.
Values may be sent and summed in bfloat16 or wider, within the bound.
No kernel may reach another device: no remote copies, remote signals or barrier semaphores. Data moves between devices by JAX's collectives and lax.ppermute only.
A program may use at most 192 MiB of HBM per device.

```python
import jax
import jax.numpy as jnp
from jax import lax

D = 192
HEADS = 6
HEAD_DIM = 32
FF = 768
LEVELS = 8
WIN = 72
LAT_BANDS = 20
COL_DEV = 288
TOK_DEV = 2304
PER_PEER = 288
UNIT_DEV = 32
SAMPLES = 4
COLUMNS = 2304
UNITS = 256
PARAMS = 1216512
N_SPACE = 8


def segment_table():
    return [(D, 0.2, 1.0), (D, 0.3, 0.0), (D * 3 * D, D ** (-0.5), 0.0), (D * D, (D / 8.0) ** (-0.5), 0.0), (D, 0.3, 0.0), (D, 0.2, 1.0), (D, 0.3, 0.0), (D * 3 * D, D ** (-0.5), 0.0), (D * D, (D / 2.0) ** (-0.5), 0.0), (D, 0.3, 0.0), (D, 0.2, 1.0), (D, 0.3, 0.0), (D * FF, D ** (-0.5), 0.0), (FF, 0.3, 0.0), (FF * D, FF ** (-0.5), 0.0), (D, 0.3, 0.0), (LAT_BANDS * HEADS * WIN * WIN, 1.0, 0.0)]


def segment_scales():
    scales = []
    offsets = []
    filled = 0
    for entry_size, spread, center in segment_table():
        scales.append(jnp.full((entry_size,), spread, jnp.float32))
        offsets.append(jnp.full((entry_size,), center, jnp.float32))
        filled = filled + entry_size
    scales.append(jnp.ones((PARAMS - filled,), jnp.float32))
    offsets.append(jnp.zeros((PARAMS - filled,), jnp.float32))
    return (jnp.concatenate(scales), jnp.concatenate(offsets))


def draw_params(key, part):
    key = jax.random.fold_in(key, 7)
    noise = jax.random.normal(key, (PARAMS,), jnp.float32)
    scales, offsets = segment_scales()
    return noise * scales + offsets


def draw_send_rows(key, part):
    key = jax.random.fold_in(key, 11)
    base = jnp.broadcast_to(jnp.arange(TOK_DEV, dtype=jnp.int32), (SAMPLES, N_SPACE, TOK_DEV))
    shuffled = jax.random.permutation(key, base, axis=2, independent=True)
    return shuffled.reshape(SAMPLES, N_SPACE, N_SPACE, PER_PEER).transpose(0, 2, 1, 3)


def set_ends(array, own_key, low, high):
    longest = array.shape.index(max(array.shape))
    spots = []
    for shift in (0, 1):
        where = [jax.random.randint(jax.random.fold_in(own_key, axis), (), 0, length) for axis, length in enumerate(array.shape)]
        where[longest] = (where[longest] + shift) % array.shape[longest]
        spots.append(tuple(where))
    return array.at[spots[0]].set(low).at[spots[1]].set(high)


def level_of(own_key, dims, shards, low, high):
    loudness = 1.0
    for dim, shards_of in shards:
        steps = jax.random.uniform(jax.random.fold_in(jax.random.fold_in(own_key, 6), dim), (shards_of,), jnp.float32, low / len(shards), high / len(shards))
        loudness = loudness * jnp.repeat(jnp.exp(steps), dims[dim] // shards_of).reshape((-1,) + (1,) * (len(dims) - 1 - dim))
    return loudness


def normal_values(own_key, shape, scale, limit, cuts=(), kind=jnp.bfloat16):
    array = jax.random.normal(own_key, shape, jnp.float32) * scale
    if len(cuts) > 0:
        array = level_of(own_key, shape, cuts, -0.22, 0.18) * array
    return jnp.clip(array, min=-limit, max=limit).astype(kind)


def setup_inputs(seed: int = 0) -> dict:
    streams_of = jax.random.split(jax.random.key(seed), 7)
    block_input = normal_values(streams_of[0], (SAMPLES, COLUMNS, LEVELS, D), 1.0, 6.0, ((0, 4), (1, 8)))
    cotangent = normal_values(streams_of[1], (SAMPLES, COLUMNS, LEVELS, D), 1.0, 6.0, ((0, 4), (1, 8)))
    params = draw_params(jax.random.fold_in(streams_of[6], 71), 0)
    send_rows = draw_send_rows(jax.random.fold_in(streams_of[6], 71), 0)
    window_band = set_ends(jax.random.randint(streams_of[4], (SAMPLES, UNITS), 0, LAT_BANDS), jax.random.fold_in(streams_of[4], 1), 0, LAT_BANDS - 1).astype(jnp.int32)
    level_count = set_ends(jax.random.randint(streams_of[5], (SAMPLES, COLUMNS), 1, LEVELS + 1), jax.random.fold_in(streams_of[5], 1), 1, LEVELS).astype(jnp.int32)
    return {"block_input": block_input, "cotangent": cotangent, "params": params, "send_rows": send_rows, "window_band": window_band, "level_count": level_count}


@jax.custom_vjp
def low(v):
    return lax.optimization_barrier(v.astype(jnp.bfloat16)).astype(jnp.float32)

@jax.custom_vjp
def low_back(v):
    return v

def low_keep(v):
    return (low(v), None)

def low_pass(kept, grad):
    return (grad,)

def back_keep(v):
    return (v, None)

def back_low(kept, grad):
    return (low(grad),)
low.defvjp(low_keep, low_pass)
low_back.defvjp(back_keep, back_low)
norm_eps = 1e-05
highest = lax.Precision.HIGHEST

def param_layout():
    return [('norm1_gain', (D,)), ('norm1_shift', (D,)), ('qkv1', (D, 3 * D)), ('proj1', (D, D)), ('proj1_bias', (D,)), ('norm2_gain', (D,)), ('norm2_shift', (D,)), ('qkv2', (D, 3 * D)), ('proj2', (D, D)), ('proj2_bias', (D,)), ('norm3_gain', (D,)), ('norm3_shift', (D,)), ('mlp_in', (D, FF)), ('mlp_in_bias', (FF,)), ('mlp_out', (FF, D)), ('mlp_out_bias', (D,)), ('earth_bias', (LAT_BANDS, HEADS, WIN, WIN))]

def unpack_params(flat_values):
    pieces = {}
    offset = 0
    for entry_name, entry_shape in param_layout():
        entry_size = 1
        for extent in entry_shape:
            entry_size = entry_size * extent
        pieces[entry_name] = flat_values[offset:offset + entry_size].reshape(entry_shape)
        offset = offset + entry_size
    return pieces

def layer_norm(rows_in, norm_gain, norm_shift):
    row_mean = lax.optimization_barrier(jnp.mean(rows_in, axis=-1, keepdims=True))
    centered = rows_in - row_mean
    row_var = lax.optimization_barrier(jnp.mean(centered * centered, axis=-1, keepdims=True))
    return centered * lax.rsqrt(row_var + norm_eps) * norm_gain + norm_shift

def window_block(pieces, tokens, band_rows):
    score_scale = HEAD_DIM ** (-0.5)
    normed = low(layer_norm(tokens, pieces['norm1_gain'], pieces['norm1_shift']))
    packed = jnp.dot(normed, pieces['qkv1'], precision=highest).reshape(-1, WIN, 3, HEADS, HEAD_DIM)
    query_rows = low_back(low(packed[:, :, 0]))
    key_rows = low_back(low(packed[:, :, 1]))
    value_rows = low_back(low(packed[:, :, 2]))
    scores = jnp.einsum('uqhe,ukhe->uhqk', query_rows, key_rows, precision=highest) * score_scale
    scores = low_back(scores + pieces['earth_bias'][band_rows])
    attn_prob = jax.nn.softmax(scores, axis=-1)
    mixed_heads = jnp.einsum('uhqk,ukhe->uqhe', low(attn_prob), value_rows, precision=highest)
    mixed_heads = low_back(low(mixed_heads.reshape(-1, D)))
    return jnp.dot(mixed_heads, pieces['proj1'], precision=highest) + pieces['proj1_bias']

def column_block(pieces, rows_in, level_rows):
    score_scale = HEAD_DIM ** (-0.5)
    normed = low(layer_norm(rows_in, pieces['norm2_gain'], pieces['norm2_shift']))
    packed = jnp.dot(normed, pieces['qkv2'], precision=highest).reshape(-1, LEVELS, 3, HEADS, HEAD_DIM)
    query_rows = low_back(low(packed[:, :, 0]))
    key_rows = low_back(low(packed[:, :, 1]))
    value_rows = low_back(low(packed[:, :, 2]))
    scores = jnp.einsum('cqhe,ckhe->hqkc', query_rows, key_rows, precision=highest) * score_scale
    valid_keys = jnp.arange(LEVELS, dtype=jnp.int32)[:, None] < level_rows[None, :]
    scores = low_back(jnp.where(valid_keys, scores, -jnp.inf))
    attn_prob = jax.nn.softmax(scores, axis=2)
    mixed_heads = jnp.einsum('hqkc,ckhe->cqhe', low(attn_prob), value_rows, precision=highest)
    mixed_heads = low_back(low(mixed_heads.reshape(-1, D)))
    middle = rows_in + low_back(jnp.dot(mixed_heads, pieces['proj2'], precision=highest) + pieces['proj2_bias'])
    normed3 = low(layer_norm(middle, pieces['norm3_gain'], pieces['norm3_shift']))
    pre_gelu = low_back(jnp.dot(normed3, pieces['mlp_in'], precision=highest) + pieces['mlp_in_bias'])
    activation = low(jax.nn.gelu(pre_gelu))
    return middle + low_back(jnp.dot(activation, pieces['mlp_out'], precision=highest) + pieces['mlp_out_bias'])

def sample_forward(flat_params, sample_in, routes, band_rows, level_rows):
    pieces = unpack_params(low(flat_params))
    tokens = sample_in.reshape(-1, D)
    order = (jnp.arange(N_SPACE, dtype=jnp.int32)[None, :, None] * TOK_DEV + routes).reshape(-1)
    shifted = low_back(tokens[order])
    window_step = jax.checkpoint(window_block)
    window_out = lax.map(lambda block_pair: window_step(pieces, block_pair[0], block_pair[1]), (shifted.reshape(N_SPACE, UNIT_DEV * WIN, D), band_rows.reshape(N_SPACE, UNIT_DEV)))
    branch = jnp.zeros_like(tokens).at[order].set(window_out.reshape(-1, D))
    after_window = tokens + low_back(low(branch))
    column_step = jax.checkpoint(column_block)
    column_out = lax.map(lambda block_pair: column_step(pieces, block_pair[0], block_pair[1]), (after_window.reshape(N_SPACE, TOK_DEV, D), level_rows.reshape(N_SPACE, COL_DEV)))
    return column_out.reshape(sample_in.shape)

def reference(block_input, cotangent, params, send_rows, window_band, level_count):

    def one_sample(total, sample):
        sample_in, sample_cot, routes, band_rows, level_rows = sample

        def forward(rows_in, flat_values):
            return sample_forward(flat_values, rows_in, routes, band_rows, level_rows)
        output, pullback = jax.vjp(forward, sample_in, params)
        input_part, param_part = pullback(sample_cot)
        return (total + param_part, (output.astype(jnp.bfloat16), input_part))
    total, outputs = lax.scan(one_sample, jnp.zeros_like(params), (block_input.astype(jnp.float32), cotangent.astype(jnp.float32), send_rows, window_band, level_count))
    return (outputs[0], outputs[1], total)
```

```python
import math

import jax
import jax.numpy as jnp
from jax import lax
from jax.sharding import PartitionSpec as P

D = 192
HEADS = 6
HEAD_DIM = 32
FF = 768
LEVELS = 8
WIN = 72
LAT_BANDS = 20


norm_eps = 1e-05


def param_layout():
    return [
        ("norm1_gain", (D,)),
        ("norm1_shift", (D,)),
        ("qkv1", (D, 3 * D)),
        ("proj1", (D, D)),
        ("proj1_bias", (D,)),
        ("norm2_gain", (D,)),
        ("norm2_shift", (D,)),
        ("qkv2", (D, 3 * D)),
        ("proj2", (D, D)),
        ("proj2_bias", (D,)),
        ("norm3_gain", (D,)),
        ("norm3_shift", (D,)),
        ("mlp_in", (D, FF)),
        ("mlp_in_bias", (FF,)),
        ("mlp_out", (FF, D)),
        ("mlp_out_bias", (D,)),
        ("earth_bias", (LAT_BANDS, HEADS, WIN, WIN)),
    ]


def unpack_params(flat_values):
    pieces = {}
    offset = 0
    for entry_name, entry_shape in param_layout():
        entry_size = 1
        for extent in entry_shape:
            entry_size = entry_size * extent
        pieces[entry_name] = flat_values[offset : offset + entry_size].reshape(entry_shape)
        offset = offset + entry_size
    return pieces


def layer_norm(rows_in, norm_gain, norm_shift):
    row_mean = jnp.mean(rows_in, axis=-1, keepdims=True)
    centered = rows_in - row_mean
    row_var = jnp.mean(centered * centered, axis=-1, keepdims=True)
    return centered * lax.rsqrt(row_var + norm_eps) * norm_gain + norm_shift


def plain_product(left, right):
    return jnp.dot(left, right, preferred_element_type=jnp.float32)


def left_product(left, right):
    return lax.dot_general(
        left, right, (((0,), (0,)), ((), ())), preferred_element_type=jnp.float32
    )


def right_product(left, right):
    return lax.dot_general(
        left, right, (((1,), (1,)), ((), ())), preferred_element_type=jnp.float32
    )


def as_float(value):
    return value.astype(jnp.float32)


def window_forward(pieces, shifted, selector):
    score_scale = HEAD_DIM ** (-0.5)
    normed, norm_back = jax.vjp(
        layer_norm,
        as_float(shifted),
        as_float(pieces["norm1_gain"]),
        as_float(pieces["norm1_shift"]),
    )
    normed_bf = normed.astype(jnp.bfloat16)
    packed = (
        plain_product(normed_bf, pieces["qkv1"])
        .astype(jnp.bfloat16)
        .reshape(-1, WIN, 3, HEADS, HEAD_DIM)
    )
    bias_rows = plain_product(selector, pieces["earth_bias"].reshape(LAT_BANDS, -1)).reshape(
        -1, HEADS, WIN, WIN
    )
    scores = (
        jnp.einsum(
            "uqhe,ukhe->uhqk", packed[:, :, 0], packed[:, :, 1], preferred_element_type=jnp.float32
        )
        * score_scale
        + bias_rows
    )
    attn_prob = jax.nn.softmax(scores, axis=-1)
    attn_bf = attn_prob.astype(jnp.bfloat16)
    mixed_heads = (
        jnp.einsum("uhqk,ukhe->uqhe", attn_bf, packed[:, :, 2], preferred_element_type=jnp.float32)
        .reshape(-1, D)
        .astype(jnp.bfloat16)
    )
    window_out = plain_product(mixed_heads, pieces["proj1"]) + as_float(pieces["proj1_bias"])
    return (window_out, (norm_back, normed_bf, packed, attn_prob, attn_bf, mixed_heads))


def window_backward(pieces, saved, grad_out, selector):
    score_scale = HEAD_DIM ** (-0.5)
    norm_back, normed_bf, packed, attn_prob, attn_bf, mixed_heads = saved
    gradient = {}
    gradient["proj1"] = left_product(mixed_heads, grad_out)
    gradient["proj1_bias"] = jnp.sum(as_float(grad_out), axis=0)
    grad_mixed = (
        right_product(grad_out, pieces["proj1"])
        .astype(jnp.bfloat16)
        .reshape(-1, WIN, HEADS, HEAD_DIM)
    )
    grad_prob = jnp.einsum(
        "uqhe,ukhe->uhqk", grad_mixed, packed[:, :, 2], preferred_element_type=jnp.float32
    )
    grad_value = jnp.einsum(
        "uhqk,uqhe->ukhe", attn_bf, grad_mixed, preferred_element_type=jnp.float32
    )
    grad_scores = (
        attn_prob * (grad_prob - jnp.sum(attn_prob * grad_prob, axis=-1, keepdims=True))
    ).astype(jnp.bfloat16)
    gradient["earth_bias"] = left_product(
        selector, grad_scores.reshape(selector.shape[0], -1)
    ).reshape(LAT_BANDS, HEADS, WIN, WIN)
    grad_query = (
        jnp.einsum(
            "uhqk,ukhe->uqhe", grad_scores, packed[:, :, 1], preferred_element_type=jnp.float32
        )
        * score_scale
    )
    grad_key = (
        jnp.einsum(
            "uhqk,uqhe->ukhe", grad_scores, packed[:, :, 0], preferred_element_type=jnp.float32
        )
        * score_scale
    )
    grad_packed = (
        jnp.stack([grad_query, grad_key, grad_value], axis=2)
        .astype(jnp.bfloat16)
        .reshape(-1, 3 * D)
    )
    gradient["qkv1"] = left_product(normed_bf, grad_packed)
    grad_tokens, gradient["norm1_gain"], gradient["norm1_shift"] = norm_back(
        right_product(grad_packed, pieces["qkv1"])
    )
    return (grad_tokens, gradient)


def column_forward(pieces, after_window, level_rows):
    score_scale = HEAD_DIM ** (-0.5)
    normed, norm2_back = jax.vjp(
        layer_norm, after_window, as_float(pieces["norm2_gain"]), as_float(pieces["norm2_shift"])
    )
    normed_bf = normed.astype(jnp.bfloat16)
    packed = (
        plain_product(normed_bf, pieces["qkv2"])
        .astype(jnp.bfloat16)
        .reshape(-1, LEVELS, 3, HEADS, HEAD_DIM)
    )
    scores = (
        jnp.einsum(
            "cqhe,ckhe->hqkc", packed[:, :, 0], packed[:, :, 1], preferred_element_type=jnp.float32
        )
        * score_scale
    )
    valid_keys = jnp.arange(LEVELS, dtype=jnp.int32)[:, None] < level_rows[None, :]
    scores = jnp.where(valid_keys, scores, -jnp.inf)
    attn_prob = jax.nn.softmax(scores, axis=2)
    attn_bf = attn_prob.astype(jnp.bfloat16)
    mixed_heads = (
        jnp.einsum("hqkc,ckhe->cqhe", attn_bf, packed[:, :, 2], preferred_element_type=jnp.float32)
        .reshape(-1, D)
        .astype(jnp.bfloat16)
    )
    middle = after_window + (
        plain_product(mixed_heads, pieces["proj2"]) + as_float(pieces["proj2_bias"])
    )
    normed3, norm3_back = jax.vjp(
        layer_norm, middle, as_float(pieces["norm3_gain"]), as_float(pieces["norm3_shift"])
    )
    normed3_bf = normed3.astype(jnp.bfloat16)
    pre_gelu = plain_product(normed3_bf, pieces["mlp_in"]) + as_float(pieces["mlp_in_bias"])
    activation, gelu_back = jax.vjp(jax.nn.gelu, pre_gelu)
    active_bf = activation.astype(jnp.bfloat16)
    output = middle + (
        plain_product(active_bf, pieces["mlp_out"]) + as_float(pieces["mlp_out_bias"])
    )
    saved = (
        norm2_back,
        normed_bf,
        packed,
        attn_prob,
        attn_bf,
        mixed_heads,
        norm3_back,
        normed3_bf,
        gelu_back,
        active_bf,
    )
    return (output, saved)


def column_backward(pieces, saved, grad_out):
    score_scale = HEAD_DIM ** (-0.5)
    (
        norm2_back,
        normed_bf,
        packed,
        attn_prob,
        attn_bf,
        mixed_heads,
        norm3_back,
        normed3_bf,
        gelu_back,
        active_bf,
    ) = saved
    gradient = {}
    grad_mlp = grad_out.astype(jnp.bfloat16)
    gradient["mlp_out"] = left_product(active_bf, grad_mlp)
    gradient["mlp_out_bias"] = jnp.sum(as_float(grad_mlp), axis=0)
    grad_pre = gelu_back(right_product(grad_mlp, pieces["mlp_out"]))[0].astype(jnp.bfloat16)
    gradient["mlp_in"] = left_product(normed3_bf, grad_pre)
    gradient["mlp_in_bias"] = jnp.sum(as_float(grad_pre), axis=0)
    grad_norm3, gradient["norm3_gain"], gradient["norm3_shift"] = norm3_back(
        right_product(grad_pre, pieces["mlp_in"])
    )
    grad_middle = grad_out + grad_norm3
    grad_attn = grad_middle.astype(jnp.bfloat16)
    gradient["proj2"] = left_product(mixed_heads, grad_attn)
    gradient["proj2_bias"] = jnp.sum(as_float(grad_attn), axis=0)
    grad_mixed = (
        right_product(grad_attn, pieces["proj2"])
        .astype(jnp.bfloat16)
        .reshape(-1, LEVELS, HEADS, HEAD_DIM)
    )
    grad_prob = jnp.einsum(
        "cqhe,ckhe->hqkc", grad_mixed, packed[:, :, 2], preferred_element_type=jnp.float32
    )
    grad_value = jnp.einsum(
        "hqkc,cqhe->ckhe", attn_bf, grad_mixed, preferred_element_type=jnp.float32
    )
    grad_scores = (
        attn_prob * (grad_prob - jnp.sum(attn_prob * grad_prob, axis=2, keepdims=True))
    ).astype(jnp.bfloat16)
    grad_query = (
        jnp.einsum(
            "hqkc,ckhe->cqhe", grad_scores, packed[:, :, 1], preferred_element_type=jnp.float32
        )
        * score_scale
    )
    grad_key = (
        jnp.einsum(
            "hqkc,cqhe->ckhe", grad_scores, packed[:, :, 0], preferred_element_type=jnp.float32
        )
        * score_scale
    )
    grad_packed = (
        jnp.stack([grad_query, grad_key, grad_value], axis=2)
        .astype(jnp.bfloat16)
        .reshape(-1, 3 * D)
    )
    gradient["qkv2"] = left_product(normed_bf, grad_packed)
    grad_norm2, gradient["norm2_gain"], gradient["norm2_shift"] = norm2_back(
        right_product(grad_packed, pieces["qkv2"])
    )
    return (grad_middle + grad_norm2, gradient)


def body(block_input, cotangent, params, send_rows, window_band, level_count):
    model_width = block_input.shape[-1]
    rows_dev = block_input.shape[1] * block_input.shape[2]
    n_space, per_peer = send_rows.shape[1], send_rows.shape[3]
    group = WIN // math.gcd(per_peer, WIN)
    if n_space % group:
        group = n_space
    dest = n_space // group
    per_dest = group * per_peer // WIN
    member_groups = [[first + k for k in range(group)] for first in range(0, n_space, group)]
    me = lax.axis_index("space")
    flat_in = block_input[0].reshape(rows_dev, model_width)
    routes = send_rows[0, :, 0, :]
    route_flat = routes.reshape(-1)
    level_rows = level_count[0]

    def exchange(value):
        return lax.all_to_all(
            value, "space", split_axis=0, concat_axis=0, tiled=True, axis_index_groups=member_groups
        )

    def to_windows(rows):
        picked = rows[route_flat]
        if group > 1:
            moved = exchange(picked).reshape(group, dest, per_peer, model_width)
            picked = moved.transpose(1, 0, 2, 3).reshape(rows_dev, model_width)
        return picked

    def from_windows(rows):
        if group > 1:
            moved = rows.reshape(dest, group, per_peer, model_width).transpose(1, 0, 2, 3)
            rows = exchange(moved.reshape(rows_dev, model_width))
        return jnp.zeros((rows_dev, model_width), rows.dtype).at[route_flat].set(rows)

    all_bands = lax.all_gather(window_band[0], "space", axis=0)
    bands = lax.dynamic_slice(
        all_bands, ((me % group) * dest, (me // group) * per_dest), (dest, per_dest)
    ).reshape(-1)
    selector = (bands[:, None] == jnp.arange(LAT_BANDS, dtype=jnp.int32)[None, :]).astype(
        jnp.bfloat16
    )
    gathered = lax.all_gather(params.astype(jnp.bfloat16), ("dp", "space"), axis=0, tiled=True)
    pieces = unpack_params(gathered)
    shifted = to_windows(flat_in)
    window_out, window_saved = window_forward(pieces, shifted, selector)
    branch = from_windows(window_out.astype(jnp.bfloat16))
    after_window = as_float(flat_in) + as_float(branch)
    output, column_saved = column_forward(pieces, after_window, level_rows)
    grad_after, column_grads = column_backward(
        pieces, column_saved, as_float(cotangent[0].reshape(rows_dev, model_width))
    )
    grad_window = to_windows(grad_after.astype(jnp.bfloat16))
    grad_shifted, window_grads = window_backward(pieces, window_saved, grad_window, selector)
    input_grad = grad_after + as_float(from_windows(grad_shifted.astype(jnp.bfloat16)))
    gradient = dict(column_grads)
    gradient.update(window_grads)
    flat_grad = jnp.concatenate(
        [gradient[entry_name].reshape(-1) for entry_name, entry_shape in param_layout()]
    )
    flat_grad = jnp.pad(flat_grad, (0, gathered.shape[0] - flat_grad.shape[0]))
    owned = lax.psum_scatter(flat_grad, ("dp", "space"), scatter_dimension=0, tiled=True)
    return (
        output.astype(jnp.bfloat16).reshape(block_input.shape),
        input_grad.reshape(block_input.shape),
        owned,
    )


def solution(mesh):
    return jax.shard_map(
        body,
        mesh=mesh,
        in_specs=(
            P("dp", "space", None, None),
            P("dp", "space", None, None),
            P(("dp", "space")),
            P("dp", None, "space", None),
            P("dp", "space"),
            P("dp", "space"),
        ),
        out_specs=(P("dp", "space", None, None), P("dp", "space", None, None), P(("dp", "space"))),
        check_vma=False,
    )
```

```python
import functools
import math

import jax
import jax.numpy as jnp
from jax import lax
from jax.experimental import pallas as pl
from jax.experimental.pallas import tpu as pltpu
from jax.sharding import PartitionSpec as P

D = 192
HEADS = 6
HEAD_DIM = 32
FF = 768
LEVELS = 8
WIN = 72
LAT_BANDS = 20
LANES = 128
HALF = LANES // 2
KEYS = 80
SCALE = HEAD_DIM ** (-0.5)
LOG2E = math.log2(math.e)
F32 = jnp.float32
BF16 = jnp.bfloat16
VMEM_LIMIT = 58 << 20

norm_eps = 1e-05


def param_layout():
    return [
        ("norm1_gain", (D,)),
        ("norm1_shift", (D,)),
        ("qkv1", (D, 3 * D)),
        ("proj1", (D, D)),
        ("proj1_bias", (D,)),
        ("norm2_gain", (D,)),
        ("norm2_shift", (D,)),
        ("qkv2", (D, 3 * D)),
        ("proj2", (D, D)),
        ("proj2_bias", (D,)),
        ("norm3_gain", (D,)),
        ("norm3_shift", (D,)),
        ("mlp_in", (D, FF)),
        ("mlp_in_bias", (FF,)),
        ("mlp_out", (FF, D)),
        ("mlp_out_bias", (D,)),
        ("earth_bias", (LAT_BANDS, HEADS, WIN, WIN)),
    ]


def param_offsets():
    offsets = {}
    filled = 0
    for entry_name, entry_shape in param_layout():
        offsets[entry_name] = filled
        filled += math.prod(entry_shape)
    return offsets


OFFSET = param_offsets()
BIAS_ROW, BIAS_LANE = divmod(OFFSET["earth_bias"], LANES)
BIAS_ROWS = LAT_BANDS * HEADS * WIN
WIDE = LANES // math.gcd(WIN, LANES)
DENSE = WIN // math.gcd(WIN, LANES)
PERIODS = -(-(BIAS_ROWS // WIDE + 1) // 8) * 8
COL_LO = (OFFSET["norm2_gain"] // LANES) // 8 * 8
COL_HI = -(-BIAS_ROW // 8) * 8 + 8
BIAS_LO = BIAS_ROW // 8 * 8


def mm(left, right):
    return lax.dot_general(left, right, (((1,), (0,)), ((), ())), preferred_element_type=F32)


def mt(left, right):
    return lax.dot_general(left, right, (((1,), (1,)), ((), ())), preferred_element_type=F32)


def lane_ids(rows):
    return lax.broadcasted_iota(jnp.int32, (rows, LANES), 1)


def rows_at(start, count, stride):
    return pl.ds(start, count) if stride == 1 else pl.ds(start, count, stride=stride)


def read_matrix(dense, first_row, name, matrix):
    rows, width = dict(param_layout())[name]
    halves = width // HALF
    step = 1 + halves % 2
    count, stride = rows // step, halves * step // 2
    low = lane_ids(count) < HALF
    for part in range(step):
        for chunk in range(-(-halves // 2)):
            unit = OFFSET[name] // HALF + part * halves + 2 * chunk
            row = unit // 2 - first_row
            value = dense[rows_at(row, count, stride), :]
            if unit % 2:
                after = dense[rows_at(row + 1, count, stride), :]
                value = pltpu.roll(jnp.where(low, after, value), HALF, 1)
            matrix[chunk, rows_at(part, count, step), :] = value


def write_matrix(dense, first_row, name, matrix):
    rows, width = dict(param_layout())[name]
    halves = width // HALF
    step = 1 + halves % 2
    count, stride = rows // step, halves * step // 2
    lane = lane_ids(count)
    for part in range(step):
        piece = 0
        while piece < halves:
            unit = OFFSET[name] // HALF + part * halves + piece
            where_to = rows_at(unit // 2 - first_row, count, stride)
            chunk = piece // 2
            value = matrix[chunk, rows_at(part, count, step), :]
            if unit % 2 == piece % 2 == 0 and piece + 1 < halves:
                dense[where_to, :] = value
                piece += 2
                continue
            if unit % 2 != piece % 2:
                value = pltpu.roll(value, HALF, 1)
            mine = lane < HALF if unit % 2 == 0 else lane >= HALF
            dense[where_to, :] = jnp.where(mine, value, dense[where_to, :])
            piece += 1


def joined(matrix, width):
    chunks = [matrix[k] for k in range(-(-width // LANES))]
    return jnp.concatenate(chunks, axis=1)[:, :width]


def split_into(matrix, value):
    width = value.shape[1]
    for k in range(-(-width // LANES)):
        end = min(width, (k + 1) * LANES)
        matrix[k, :, : end - k * LANES] = value[:, k * LANES : end]


def read_vector(dense, first_row, name):
    size = dict(param_layout())[name][0]
    unit = OFFSET[name] // HALF
    row = unit // 2 - first_row
    turned = dense[row : row + 8, :].T
    pieces = []
    for k in range(size // HALF):
        spot = unit % 2 + k
        pieces.append(turned[spot % 2 * HALF : (spot % 2 + 1) * HALF, spot // 2 : spot // 2 + 1])
    return jnp.concatenate(pieces, axis=0)


def write_vector(dense, first_row, name, sums):
    size = dict(param_layout())[name][0]
    line = jnp.sum(sums.T, axis=0, keepdims=True)
    lane = lane_ids(1)
    for k in range(size // HALF):
        unit = OFFSET[name] // HALF + k
        row = unit // 2 - first_row
        if size % LANES and k == size // HALF - 1:
            tail = line[:, k * HALF :]
            piece = jnp.concatenate([tail, tail], axis=1)
        else:
            piece = line[:, k // 2 * LANES : (k // 2 + 1) * LANES]
            if unit % 2 != k % 2:
                piece = pltpu.roll(piece, HALF, 1)
        mine = lane < HALF if unit % 2 == 0 else lane >= HALF
        dense[row : row + 1, :] = jnp.where(mine, piece, dense[row : row + 1, :])


def read_bias(dense, wide):
    lane = lane_ids(PERIODS)
    for j in range(WIDE):
        row, first = divmod(BIAS_LANE + j * WIN, LANES)
        value = dense[pl.ds(BIAS_ROW + row, PERIODS, stride=DENSE), :]
        if first + WIN > LANES:
            after = dense[pl.ds(BIAS_ROW + row + 1, PERIODS, stride=DENSE), :]
            value = jnp.where(lane < first, after, value)
        if first:
            value = pltpu.roll(value, LANES - first, 1)
        wide[pl.ds(j, PERIODS, stride=WIDE), :] = value


def write_bias(wide, dense, first_row):
    lane = lane_ids(PERIODS)
    for i in range(DENSE):
        begin = i * LANES - BIAS_LANE
        line = begin // WIN
        value = None
        while line * WIN < begin + LANES:
            shift = line * WIN - begin
            piece = wide[pl.ds(WIDE + line, PERIODS, stride=WIDE), :]
            if shift % LANES:
                piece = pltpu.roll(piece, shift % LANES, 1)
            value = piece if value is None else jnp.where(lane >= shift, piece, value)
            line += 1
        dense[pl.ds(BIAS_ROW - first_row + i, PERIODS, stride=DENSE), :] = value


def norm_parts(rows_in):
    mean = jnp.mean(rows_in, axis=0, keepdims=True)
    centered = rows_in - mean
    var = jnp.mean(centered * centered, axis=0, keepdims=True)
    scale = lax.rsqrt(var + norm_eps)
    return centered * scale, scale


def norm_back(grad, unit, scale, gain):
    scaled = grad * gain
    first = jnp.mean(scaled, axis=0, keepdims=True)
    second = jnp.mean(scaled * unit, axis=0, keepdims=True)
    return scale * (scaled - first - unit * second)


def lane_fold(value):
    total = value[:, :LANES]
    for k in range(1, value.shape[1] // LANES):
        total = total + value[:, k * LANES : (k + 1) * LANES]
    return total


def head_rows(h):
    return slice(h * HEAD_DIM, (h + 1) * HEAD_DIM)


def head_lanes(h):
    return slice(h * LANES, (h + 1) * LANES)


def diagonal(full):
    return jnp.concatenate([full[head_rows(h), head_lanes(h)] for h in range(HEADS)], axis=0)


def scatter_heads(block, rows_in):
    for h in range(HEADS):
        block[head_rows(h), head_lanes(h)] = rows_in[head_rows(h), :]


def chooser(first, rows, slots):
    ids = lax.broadcasted_iota(jnp.int32, (rows, slots.shape[1]), 0) + first
    return jnp.where(ids == slots, 1.0, 0.0).astype(BF16)


def to_slots(rows_t, slots):
    tokens = rows_t.shape[1]
    pick = jnp.concatenate([chooser(k, 256, slots) for k in range(0, tokens, 256)], axis=0)
    return mm(rows_t, pick).astype(BF16)


def from_slots(slot_rows, slots, first, rows):
    return mt(slot_rows, chooser(first, rows, slots))


def call(kernel, grid, ins, outs, scratch, name, scalars=0):
    in_specs = [s for _, s in ins]
    spec = pltpu.PrefetchScalarGridSpec(
        num_scalar_prefetch=scalars,
        grid=grid,
        in_specs=in_specs[scalars:],
        out_specs=[s for _, _, s in outs],
        scratch_shapes=scratch,
    )
    return pl.pallas_call(
        kernel,
        grid_spec=spec,
        out_shape=[jax.ShapeDtypeStruct(shape, kind) for shape, kind, _ in outs],
        compiler_params=pltpu.CompilerParams(
            dimension_semantics=("arbitrary",) * len(grid), vmem_limit_bytes=VMEM_LIMIT
        ),
        name=name,
    )(*[a for a, _ in ins])


def whole_block(shape):
    return pl.BlockSpec(shape, lambda *_: (0,) * len(shape))


SLOT_BLOCK = 512
TOKEN_BLOCK = 256


def shift_kernel(x_ref, slots_ref, out_ref, x_t):
    @pl.when(pl.program_id(0) == 0)
    def _():
        x_t[...] = x_ref[...].astype(F32).T.astype(BF16)

    out_ref[...] = to_slots(x_t[...], slots_ref[...])


def shift_call(tokens, slots):
    count, n = tokens.shape[0], slots.shape[1]
    return call(
        shift_kernel,
        (n // SLOT_BLOCK,),
        [
            (tokens, whole_block(tokens.shape)),
            (slots, pl.BlockSpec((1, SLOT_BLOCK), lambda i: (0, i))),
        ],
        [((D, n), BF16, pl.BlockSpec((D, SLOT_BLOCK), lambda i: (0, i)))],
        [pltpu.VMEM((D, count), BF16)],
        "shift",
    )[0]


def load_dense(me_ref, parts, blocks, dense, sem, order):
    copies = []
    first = 0
    for part in parts:
        copies.append(pltpu.make_async_copy(part, blocks.at[pl.ds(first, part.shape[0])], sem))
        first += part.shape[0]
    for copy in copies:
        copy.start()
    for copy in copies:
        copy.wait()
    shards, rows = blocks.shape[0], blocks.shape[1]
    for shard in range(shards):
        spot = position(me_ref[0] ^ shard, order)
        dense[shard * rows : (shard + 1) * rows, :] = blocks[spot].astype(F32)
    if dense.shape[0] > shards * rows:
        dense[shards * rows :, :] = jnp.zeros((dense.shape[0] - shards * rows, LANES), F32)


def position(relative, order):
    spot = 0
    for place, bit in enumerate(reversed(order)):
        spot = spot + ((relative >> bit) & 1) * (1 << place)
    return spot


def window_forward_kernel(me_ref, band_ref, *refs, parts, order, steps, fused):
    ins = refs[:parts]
    refs = refs[parts:]
    if fused:
        shifted_ref, slots_ref, x_ref = refs[:3]
        refs = refs[3:]
    else:
        shifted_ref, refs = refs[0], refs[1:]
    (
        out_ref,
        qkv_ref,
        mixed_ref,
        prob_ref,
        weights_ref,
        column_ref,
        vec,
        blocks,
        dense,
        wide,
        bias,
        mat,
        qkv_t,
        proj_t,
        spread,
        y_all,
        sem,
    ) = refs
    step = pl.program_id(0)

    @pl.when(step == 0)
    def _():
        load_dense(me_ref, ins, blocks, dense, sem, order)
        column_ref[...] = dense[COL_LO:COL_HI, :]
        read_matrix(dense, 0, "qkv1", mat)
        weights_ref[:, : 3 * D] = joined(mat, 3 * D).astype(BF16)
        qkv_t[...] = joined(mat, 3 * D).T.astype(BF16)
        read_matrix(dense, 0, "proj1", mat)
        weights_ref[:, 3 * D :] = joined(mat, D).astype(BF16)
        proj_t[...] = joined(mat, D).T.astype(BF16)
        vec[:, 0:1] = read_vector(dense, 0, "norm1_gain")
        vec[:, 1:2] = read_vector(dense, 0, "norm1_shift")
        vec[:, 2:3] = read_vector(dense, 0, "proj1_bias")
        read_bias(dense, wide)
        wide[BIAS_ROWS:, :] = jnp.zeros((wide.shape[0] - BIAS_ROWS, LANES), F32)

        def turn(k, _):
            block = wide[pl.ds(pl.multiple_of(k * WIN, 8), LANES), :].T
            bias[k, :WIN, :] = block[:WIN].astype(BF16)
            return 0

        lax.fori_loop(0, LAT_BANDS * HEADS, turn, 0)
        bias[:, WIN:, :] = jnp.full((LAT_BANDS * HEADS, KEYS - WIN, LANES), -jnp.inf, BF16)
        spread[...] = jnp.zeros_like(spread)

    @pl.when(step < steps)
    def _():
        per_step = SLOT_BLOCK // LANES
        unit, _ = norm_parts(shifted_ref[...].astype(F32))
        normed = (unit * vec[:, 0:1] + vec[:, 1:2]).astype(BF16)
        qkv = mm(qkv_t[...], normed).astype(BF16)
        qkv_ref[...] = qkv
        mixed = []
        for w in range(per_step):
            lanes = slice(w * LANES, (w + 1) * LANES)
            band = band_ref[step * per_step + w]
            scatter_heads(spread.at[w], qkv[:D, lanes])
            scores = mm(qkv[D : 2 * D, lanes].T[:KEYS], spread[w])
            probs = []
            for h in range(HEADS):
                score = scores[:, head_lanes(h)] * SCALE + bias[band * HEADS + h].astype(F32)
                grown = jnp.exp(score - jnp.max(score, axis=0, keepdims=True))
                probs.append(
                    (grown * (1.0 / jnp.sum(grown, axis=0, keepdims=True))).astype(BF16)
                )
            prob = jnp.concatenate(probs, axis=1)
            prob_ref[w] = prob
            tall = jnp.concatenate([prob, jnp.zeros((LANES - KEYS, HEADS * LANES), BF16)], axis=0)
            mixed.append(diagonal(mm(qkv[2 * D :, lanes], tall)))
        mixed = jnp.concatenate(mixed, axis=1).astype(BF16)
        mixed_ref[...] = mixed
        result = (mm(proj_t[...], mixed) + vec[:, 2:3]).astype(BF16)
        if fused:
            y_all[:, pl.ds(pl.multiple_of(step * SLOT_BLOCK, SLOT_BLOCK), SLOT_BLOCK)] = result
        else:
            out_ref[...] = result

    if fused:

        @pl.when(step >= steps)
        def _():
            branch = from_slots(
                y_all[...], slots_ref[...], (step - steps) * TOKEN_BLOCK, TOKEN_BLOCK
            )
            out_ref[...] = x_ref[...].astype(F32).T + branch


def window_forward_call(me, bands, parts, order, shifted, tokens, slots, fused):
    n = shifted.shape[1]
    steps = n // SLOT_BLOCK
    per_step = SLOT_BLOCK // LANES
    shards, rows = sum(p.shape[0] for p in parts), parts[0].shape[1]
    flat_rows = max(shards * rows, BIAS_ROW + DENSE * PERIODS + 8)
    slot_block = lambda r: pl.BlockSpec((r, SLOT_BLOCK), lambda i, *_: (0, jnp.minimum(i, steps - 1)))
    ins = [(me, None), (bands, None)]
    ins += [(p, pl.BlockSpec(memory_space=pl.ANY)) for p in parts]
    ins += [(shifted, slot_block(D))]
    if fused:
        count = tokens.shape[0]
        late = lambda i: jnp.maximum(i - steps, 0)
        ins += [
            (slots, whole_block(slots.shape)),
            (tokens, pl.BlockSpec((TOKEN_BLOCK, D), lambda i, *_: (late(i), 0))),
        ]
        first = ((D, count), F32, pl.BlockSpec((D, TOKEN_BLOCK), lambda i, *_: (0, late(i))))
        grid = steps + count // TOKEN_BLOCK
    else:
        first = ((D, n), BF16, slot_block(D))
        grid = steps
    outs = [
        first,
        ((3 * D, n), BF16, slot_block(3 * D)),
        ((D, n), BF16, slot_block(D)),
        (
            (n // LANES, KEYS, HEADS * LANES),
            BF16,
            pl.BlockSpec(
                (per_step, KEYS, HEADS * LANES), lambda i, *_: (jnp.minimum(i, steps - 1), 0, 0)
            ),
        ),
        ((D, 4 * D), BF16, whole_block((D, 4 * D))),
        ((COL_HI - COL_LO, LANES), F32, whole_block((COL_HI - COL_LO, LANES))),
        ((D, LANES), F32, whole_block((D, LANES))),
    ]
    scratch = [
        pltpu.VMEM((shards, rows, LANES), BF16),
        pltpu.VMEM((flat_rows, LANES), F32),
        pltpu.VMEM((WIDE * PERIODS + LANES, LANES), F32),
        pltpu.VMEM((LAT_BANDS * HEADS, KEYS, LANES), BF16),
        pltpu.VMEM((5, D, LANES), F32),
        pltpu.VMEM((3 * D, D), BF16),
        pltpu.VMEM((D, D), BF16),
        pltpu.VMEM((per_step, D, HEADS * LANES), BF16),
        pltpu.VMEM((D, n), BF16),
        pltpu.SemaphoreType.DMA,
    ]
    kernel = functools.partial(
        window_forward_kernel, parts=len(parts), order=order, steps=steps, fused=fused
    )
    return call(kernel, (grid,), ins, outs, scratch, "window_forward", scalars=2)


COLUMN_BLOCK = 768
COLUMN_VECTORS = (
    "norm2_gain",
    "norm2_shift",
    "proj2_bias",
    "norm3_gain",
    "norm3_shift",
    "mlp_out_bias",
)
COLUMN_MATRICES = ("qkv2", "proj2", "mlp_in", "mlp_out")


def column_kernel(
    dense,
    x_ref,
    cot_ref,
    count_ref,
    out_ref,
    after_ref,
    branch_ref,
    grad_ref,
    mat,
    tall,
    w_qkv,
    w_proj,
    w_in,
    w_out,
    t_qkv,
    t_proj,
    t_in,
    t_out,
    vec,
    fvec,
    n2_s,
    dqkv_s,
    mixed_s,
    attn_s,
    n3_s,
    dpre_s,
    act_s,
    cot_s,
    sums,
    fsums,
    spread,
):
    step = pl.program_id(0)

    @pl.when(step == 0)
    def _():
        for name, plain, turned in (
            ("qkv2", w_qkv, t_qkv),
            ("proj2", w_proj, t_proj),
            ("mlp_in", w_in, t_in),
            ("mlp_out", w_out, t_out),
        ):
            rows, width = plain.shape
            source = tall if rows == FF else mat
            read_matrix(dense, COL_LO, name, source)
            plain[...] = joined(source, width).astype(BF16)
            turned[...] = joined(source, width).T.astype(BF16)
        for k, name in enumerate(COLUMN_VECTORS):
            vec[:, k : k + 1] = read_vector(dense, COL_LO, name)
        fvec[:, 0:1] = read_vector(dense, COL_LO, "mlp_in_bias")
        sums[...] = jnp.zeros_like(sums)
        fsums[...] = jnp.zeros_like(fsums)
        spread[...] = jnp.zeros_like(spread)

    groups = COLUMN_BLOCK // LANES
    cols = pl.ds(pl.multiple_of(step * COLUMN_BLOCK, COLUMN_BLOCK), COLUMN_BLOCK)
    x = x_ref[...]
    gain2, shift2, bias2, gain3, shift3, bias_out = [vec[:, k : k + 1] for k in range(6)]
    unit2, scale2 = norm_parts(x)
    n2 = (unit2 * gain2 + shift2).astype(BF16)
    n2_s[:, cols] = n2
    qkv = mm(t_qkv[...], n2).astype(BF16)
    key_id = lax.broadcasted_iota(jnp.int32, (LANES, LANES), 0)
    query_id = lax.broadcasted_iota(jnp.int32, (LANES, LANES), 1)
    same = key_id // LEVELS == query_id // LEVELS
    level = key_id % LEVELS
    probs, tall_probs, mixed = {}, {}, []
    for g in range(groups):
        lanes = slice(g * LANES, (g + 1) * LANES)
        valid = jnp.logical_and(same, level < count_ref[:, lanes])
        scatter_heads(spread.at[0, g], qkv[:D, lanes])
        scores = mm(qkv[D : 2 * D, lanes].T, spread[0, g])
        rounded = []
        for h in range(HEADS):
            score = jnp.where(valid, scores[:, head_lanes(h)] * SCALE, -jnp.inf)
            grown = jnp.exp(score - jnp.max(score, axis=0, keepdims=True))
            prob = grown * (1.0 / jnp.sum(grown, axis=0, keepdims=True))
            probs[g, h] = prob
            rounded.append(prob.astype(BF16))
        tall_probs[g] = jnp.concatenate(rounded, axis=1)
        mixed.append(diagonal(mm(qkv[2 * D :, lanes], tall_probs[g])))
    mixed = jnp.concatenate(mixed, axis=1).astype(BF16)
    mixed_s[:, cols] = mixed
    middle = x + (mm(t_proj[...], mixed) + bias2)
    unit3, scale3 = norm_parts(middle)
    n3 = (unit3 * gain3 + shift3).astype(BF16)
    n3_s[:, cols] = n3
    pre = mm(t_in[...], n3) + fvec[:, 0:1]
    root = math.sqrt(2.0 / math.pi)
    square = pre * pre
    share = 0.5 + 0.5 * jnp.tanh(pre * (root + (root * 0.044715) * square))
    act = pre * share
    slope = share + act * (1.0 - share) * (2.0 * root + (6.0 * root * 0.044715) * square)
    act = act.astype(BF16)
    act_s[:, cols] = act
    output = middle + (mm(t_out[...], act) + bias_out)
    out_ref[...] = output.T.astype(BF16)

    cot = cot_ref[...].astype(F32).T
    cot_bf = cot.astype(BF16)
    cot_s[:, cols] = cot_bf
    dpre = (mm(w_out[...], cot_bf) * slope).astype(BF16)
    dpre_s[:, cols] = dpre
    dn3 = mm(w_in[...], dpre)
    dmiddle = cot + norm_back(dn3, unit3, scale3, gain3)
    dattn = dmiddle.astype(BF16)
    attn_s[:, cols] = dattn
    dmixed = mm(w_proj[...], dattn).astype(BF16)
    dq, dk, dv = [], [], []
    for g in range(groups):
        lanes = slice(g * LANES, (g + 1) * LANES)
        scatter_heads(spread.at[1, g], dmixed[:, lanes])
        dprobs = mm(qkv[2 * D :, lanes].T, spread[1, g])
        dscores = []
        for h in range(HEADS):
            prob, dprob = probs[g, h], dprobs[:, head_lanes(h)]
            dscores.append(
                (prob * (dprob - jnp.sum(prob * dprob, axis=0, keepdims=True))).astype(BF16)
            )
        dscores = jnp.concatenate(dscores, axis=1)
        dq.append(diagonal(mm(qkv[D : 2 * D, lanes], dscores)) * SCALE)
        dk.append(mt(spread[0, g], dscores) * SCALE)
        dv.append(mt(spread[1, g], tall_probs[g]))
    dqkv = jnp.concatenate([jnp.concatenate(d, axis=1) for d in (dq, dk, dv)], axis=0).astype(BF16)
    dqkv_s[:, cols] = dqkv
    dn2 = mm(w_qkv[...], dqkv)
    dafter = dmiddle + norm_back(dn2, unit2, scale2, gain2)
    after_ref[...] = dafter
    branch_ref[...] = dafter.astype(BF16)
    for k, value in enumerate(
        (dn2 * unit2, dn2, dattn.astype(F32), dn3 * unit3, dn3, cot_bf.astype(F32))
    ):
        sums[k] += lane_fold(value)
    fsums[...] += lane_fold(dpre.astype(F32))

    @pl.when(step == pl.num_programs(0) - 1)
    def _():
        grad_ref[...] = jnp.zeros_like(grad_ref)
        split_into(mat, mt(n2_s[...], dqkv_s[...]))
        write_matrix(grad_ref, COL_LO, "qkv2", mat)
        split_into(mat, mt(mixed_s[...], attn_s[...]))
        write_matrix(grad_ref, COL_LO, "proj2", mat)
        split_into(mat, mt(n3_s[...], dpre_s[...]))
        write_matrix(grad_ref, COL_LO, "mlp_in", mat)
        split_into(tall, mt(act_s[...], cot_s[...]))
        write_matrix(grad_ref, COL_LO, "mlp_out", tall)
        for k, name in enumerate(COLUMN_VECTORS):
            write_vector(grad_ref, COL_LO, name, sums[k])
        write_vector(grad_ref, COL_LO, "mlp_in_bias", fsums[...])


def column_call(dense, after_t, cotangent, counts):
    n = after_t.shape[1]
    feature = lambda r: pl.BlockSpec((r, COLUMN_BLOCK), lambda i: (0, i))
    token = pl.BlockSpec((COLUMN_BLOCK, D), lambda i: (i, 0))
    keep = lambda r: pltpu.VMEM((r, n), BF16)
    return call(
        column_kernel,
        (n // COLUMN_BLOCK,),
        [
            (dense, whole_block(dense.shape)),
            (after_t, feature(D)),
            (cotangent, token),
            (counts, feature(1)),
        ],
        [
            ((n, D), BF16, token),
            ((D, n), F32, feature(D)),
            ((D, n), BF16, feature(D)),
            (dense.shape, F32, whole_block(dense.shape)),
        ],
        [
            pltpu.VMEM((FF // LANES, D, LANES), F32),
            pltpu.VMEM((2, FF, LANES), F32),
            pltpu.VMEM((D, 3 * D), BF16),
            pltpu.VMEM((D, D), BF16),
            pltpu.VMEM((D, FF), BF16),
            pltpu.VMEM((FF, D), BF16),
            pltpu.VMEM((3 * D, D), BF16),
            pltpu.VMEM((D, D), BF16),
            pltpu.VMEM((FF, D), BF16),
            pltpu.VMEM((D, FF), BF16),
            pltpu.VMEM((D, LANES), F32),
            pltpu.VMEM((FF, LANES), F32),
            keep(D),
            keep(3 * D),
            keep(D),
            keep(D),
            keep(D),
            keep(FF),
            keep(FF),
            keep(D),
            pltpu.VMEM((6, D, LANES), F32),
            pltpu.VMEM((FF, LANES), F32),
            pltpu.VMEM((2, COLUMN_BLOCK // LANES, D, HEADS * LANES), BF16),
        ],
        "column",
    )


def window_backward_kernel(me_ref, band_ref, *refs, order, fused):
    if fused:
        slots_ref, refs = refs[0], refs[1:]
    (
        grad_ref,
        weights_ref,
        vec,
        column_ref,
        shifted_ref,
        qkv_ref,
        mixed_ref,
        prob_ref,
        out_ref,
        keep_ref,
        send_ref,
        total,
        kept,
        wide,
        dense,
        mat,
        blocks,
        spread,
        normed_s,
        dqkv_s,
        mixed_s,
        grad_s,
        sums,
        sem,
    ) = refs
    step = pl.program_id(0)
    per_step = SLOT_BLOCK // LANES

    @pl.when(step == 0)
    def _():
        total[...] = jnp.zeros_like(total)
        sums[...] = jnp.zeros_like(sums)
        spread[...] = jnp.zeros_like(spread)

    cols = pl.ds(pl.multiple_of(step * SLOT_BLOCK, SLOT_BLOCK), SLOT_BLOCK)
    if fused:
        grad = to_slots(grad_ref[...], slots_ref[...])
    else:
        grad = grad_ref[...]
    grad_s[:, cols] = grad
    mixed_s[:, cols] = mixed_ref[...]
    dmixed = mm(weights_ref[:, 3 * D :], grad).astype(BF16)
    qkv = qkv_ref[...]
    dq, dk, dv = [], [], []
    for w in range(per_step):
        lanes = slice(w * LANES, (w + 1) * LANES)
        scatter_heads(spread.at[0, w], qkv[:D, lanes])
        scatter_heads(spread.at[1, w], dmixed[:, lanes])
        dprobs = mm(qkv[2 * D :, lanes].T[:KEYS], spread[1, w])
        dscores = []
        for h in range(HEADS):
            prob = prob_ref[w, :, head_lanes(h)].astype(F32)
            dprob = dprobs[:, head_lanes(h)]
            dscore = (prob * (dprob - jnp.sum(prob * dprob, axis=0, keepdims=True))).astype(BF16)
            dscores.append(dscore)
        for h in range(HEADS):
            kept[w, h] = dscores[h].astype(F32)
        blank = jnp.zeros((LANES - KEYS, HEADS * LANES), BF16)
        dscores = jnp.concatenate([jnp.concatenate(dscores, axis=1), blank], axis=0)
        probs = jnp.concatenate([prob_ref[w], blank], axis=0)
        dq.append(diagonal(mm(qkv[D : 2 * D, lanes], dscores)) * SCALE)
        dk.append(mt(spread[0, w], dscores) * SCALE)
        dv.append(mt(spread[1, w], probs))
    dqkv = jnp.concatenate([jnp.concatenate(d, axis=1) for d in (dq, dk, dv)], axis=0).astype(BF16)
    dqkv_s[:, cols] = dqkv

    def add(w, _):
        total[band_ref[step * per_step + w]] += kept[w]
        return 0

    lax.fori_loop(0, per_step, add, 0)
    unit, scale = norm_parts(shifted_ref[...].astype(F32))
    normed_s[:, cols] = (unit * vec[:, 0:1] + vec[:, 1:2]).astype(BF16)
    dnormed = mm(weights_ref[:, : 3 * D], dqkv)
    out_ref[...] = norm_back(dnormed, unit, scale, vec[:, 0:1]).astype(BF16)
    for k, value in enumerate((dnormed * unit, dnormed, grad.astype(F32))):
        sums[k] += lane_fold(value)

    @pl.when(step == pl.num_programs(0) - 1)
    def _():
        wide[:WIDE, :] = jnp.zeros((WIDE, LANES), F32)
        wide[WIDE + BIAS_ROWS :, :] = jnp.zeros((wide.shape[0] - WIDE - BIAS_ROWS, LANES), F32)

        def turn(k, _):
            for h in range(HEADS):
                spot = pl.multiple_of(WIDE + (k * HEADS + h) * WIN, 8)
                wide[pl.ds(spot, WIN), :KEYS] = total[k, h].T[:WIN]
            return 0

        lax.fori_loop(0, LAT_BANDS, turn, 0)
        dense[:COL_LO, :] = jnp.zeros((COL_LO, LANES), F32)
        write_bias(wide, dense, 0)
        covered = BIAS_ROW + DENSE * PERIODS
        dense[covered:, :] = jnp.zeros((dense.shape[0] - covered, LANES), F32)
        both = column_ref[COL_HI - COL_LO - 16 :, :]
        rows = lax.broadcasted_iota(jnp.int32, both.shape, 0) + (COL_HI - 16)
        lane = lane_ids(16)
        start = rows * LANES + lane < OFFSET["earth_bias"]
        dense[COL_LO : COL_HI - 16, :] = column_ref[: COL_HI - COL_LO - 16, :]
        dense[COL_HI - 16 : COL_HI, :] = jnp.where(start, both, dense[COL_HI - 16 : COL_HI, :])
        split_into(mat, mt(normed_s[...], dqkv_s[...]))
        write_matrix(dense, 0, "qkv1", mat)
        split_into(mat, mt(mixed_s[...], grad_s[...]))
        write_matrix(dense, 0, "proj1", mat)
        for k, name in enumerate(("norm1_gain", "norm1_shift", "proj1_bias")):
            write_vector(dense, 0, name, sums[k])
        shards, rows = blocks.shape[0], blocks.shape[1]
        for shard in range(shards):
            spot = position(me_ref[0] ^ shard, order)
            blocks[spot] = dense[shard * rows : (shard + 1) * rows, :].astype(BF16)
        first = pltpu.make_async_copy(blocks.at[pl.ds(0, shards // 2)], keep_ref, sem.at[0])
        second = pltpu.make_async_copy(
            blocks.at[pl.ds(shards // 2, shards // 2)], send_ref, sem.at[1]
        )
        first.start()
        second.start()
        first.wait()
        second.wait()


def window_backward_call(
    me, bands, order, shards, rows, slots, grad, weights, vec, column_grad, shifted, qkv, mixed, prob, fused
):
    n = shifted.shape[1]
    per_step = SLOT_BLOCK // LANES
    slot_block = lambda r: pl.BlockSpec((r, SLOT_BLOCK), lambda i, *_: (0, i))
    ins = [(me, None), (bands, None)]
    if fused:
        ins += [(slots, slot_block(1)), (grad, whole_block(grad.shape))]
    else:
        ins += [(grad, slot_block(D))]
    ins += [
        (weights, whole_block(weights.shape)),
        (vec, whole_block(vec.shape)),
        (column_grad, whole_block(column_grad.shape)),
        (shifted, slot_block(D)),
        (qkv, slot_block(3 * D)),
        (mixed, slot_block(D)),
        (
            prob,
            pl.BlockSpec((per_step, KEYS, HEADS * LANES), lambda i, *_: (i, 0, 0)),
        ),
    ]
    flat_rows = max(shards * rows, BIAS_ROW + DENSE * PERIODS + 8)
    outs = [
        ((D, n), BF16, slot_block(D)),
        ((shards // 2, rows, LANES), BF16, pl.BlockSpec(memory_space=pl.ANY)),
        ((shards // 2, rows, LANES), BF16, pl.BlockSpec(memory_space=pl.ANY)),
    ]
    scratch = [
        pltpu.VMEM((LAT_BANDS, HEADS, KEYS, LANES), F32),
        pltpu.VMEM((per_step, HEADS, KEYS, LANES), F32),
        pltpu.VMEM((WIDE * (PERIODS + 2), LANES), F32),
        pltpu.VMEM((flat_rows, LANES), F32),
        pltpu.VMEM((5, D, LANES), F32),
        pltpu.VMEM((shards, rows, LANES), BF16),
        pltpu.VMEM((2, per_step, D, HEADS * LANES), BF16),
        pltpu.VMEM((D, n), BF16),
        pltpu.VMEM((3 * D, n), BF16),
        pltpu.VMEM((D, n), BF16),
        pltpu.VMEM((D, n), BF16),
        pltpu.VMEM((3, D, LANES), F32),
        pltpu.SemaphoreType.DMA((2,)),
    ]
    kernel = functools.partial(window_backward_kernel, order=order, fused=fused)
    return call(kernel, (n // SLOT_BLOCK,), ins, outs, scratch, "window_backward", scalars=2)


def finish_kernel(shift_ref, slots_ref, after_ref, out_ref):
    first = pl.program_id(0) * TOKEN_BLOCK
    back = from_slots(shift_ref[...], slots_ref[...], first, TOKEN_BLOCK)
    out_ref[...] = (after_ref[...] + back).T


def finish_call(grad_shifted, slots, after_t):
    n = after_t.shape[1]
    return call(
        finish_kernel,
        (n // TOKEN_BLOCK,),
        [
            (grad_shifted, whole_block(grad_shifted.shape)),
            (slots, whole_block(slots.shape)),
            (after_t, pl.BlockSpec((D, TOKEN_BLOCK), lambda i: (0, i))),
        ],
        [((n, D), F32, pl.BlockSpec((TOKEN_BLOCK, D), lambda i: (i, 0)))],
        [],
        "finish",
    )[0]


def body(block_input, cotangent, params, send_rows, window_band, level_count):
    model_width = block_input.shape[-1]
    rows_dev = block_input.shape[1] * block_input.shape[2]
    n_space, per_peer = send_rows.shape[1], send_rows.shape[3]
    devices = lax.axis_size(("dp", "space"))
    group = WIN // math.gcd(per_peer, WIN)
    if n_space % group:
        group = n_space
    fused = group == 1
    dest = n_space // group
    per_dest = group * per_peer // WIN
    member_groups = [[first + k for k in range(group)] for first in range(0, n_space, group)]
    place = lax.axis_index("space")
    index = lax.axis_index(("dp", "space"))
    me = index.astype(jnp.int32).reshape(1)
    bits = devices.bit_length() - 1
    order = [0] + list(range(bits - 1, 0, -1))

    def swap(value, bit):
        pairs = [(k, k ^ (1 << bit)) for k in range(devices)]
        return lax.ppermute(value, ("dp", "space"), pairs)

    def exchange(value):
        return lax.all_to_all(
            value, "space", split_axis=0, concat_axis=0, tiled=True, axis_index_groups=member_groups
        )

    def to_windows(rows):
        moved = exchange(rows[route_flat]).reshape(group, dest, per_peer, model_width)
        windows = moved.transpose(1, 0, 2, 3).reshape(-1, WIN, model_width)
        windows = jnp.pad(windows, ((0, 0), (0, LANES - WIN), (0, 0)))
        return windows.reshape(-1, model_width).T

    def from_windows(rows_t):
        rows = rows_t.T.reshape(-1, LANES, model_width)[:, :WIN]
        moved = rows.reshape(dest, group, per_peer, model_width).transpose(1, 0, 2, 3)
        rows = exchange(moved.reshape(rows_dev, model_width))
        return jnp.zeros((rows_dev, model_width), rows.dtype).at[route_flat].set(rows)

    shard_rows = params.shape[0] // LANES
    held = [params.astype(BF16).reshape(1, shard_rows, LANES)]
    for bit in reversed(order):
        held = held + [swap(part, bit) for part in held]
        if sum(part.shape[0] for part in held) <= devices // 4:
            held = [jnp.concatenate(held, axis=0)]

    flat_in = block_input[0].reshape(rows_dev, model_width)
    routes = send_rows[0, :, 0, :]
    route_flat = routes.reshape(-1)
    slots = jnp.pad(
        routes.reshape(-1, WIN), ((0, 0), (0, LANES - WIN)), constant_values=-1
    ).reshape(1, -1)
    if fused:
        bands = lax.all_to_all(
            window_band[0].reshape(n_space, per_dest), "space", split_axis=0, concat_axis=0, tiled=True
        ).reshape(-1)
        shifted = shift_call(flat_in, slots)
    else:
        all_bands = lax.all_gather(window_band[0], "space", axis=0)
        bands = lax.dynamic_slice(
            all_bands, ((place % group) * dest, (place // group) * per_dest), (dest, per_dest)
        ).reshape(-1)
        shifted = to_windows(flat_in)
    first, qkv, mixed, prob, weights, column_rows, vec = window_forward_call(
        me, bands, held, order, shifted, flat_in, slots, fused
    )
    if fused:
        after_t = first
    else:
        after_t = (flat_in.astype(F32) + from_windows(first).astype(F32)).T
    counts = jnp.repeat(level_count[0], LEVELS).reshape(1, -1)
    output, grad_after, grad_branch, column_grad = column_call(
        column_rows, after_t, cotangent[0].reshape(rows_dev, model_width), counts
    )
    if not fused:
        grad_branch = to_windows(grad_branch.T)
    grad_shifted, keep, send = window_backward_call(
        me, bands, order, devices, shard_rows, slots, grad_branch, weights, vec, column_grad,
        shifted, qkv, mixed, prob, fused
    )
    if fused:
        input_grad = finish_call(grad_shifted, slots, grad_after)
    else:
        input_grad = grad_after.T + from_windows(grad_shifted).astype(F32)
    total = keep.astype(F32) + swap(send, order[0]).astype(F32)
    for bit in order[1:]:
        half = total.shape[0] // 2
        total = total[:half] + swap(total[half:].astype(BF16), bit).astype(F32)
    return (
        output.reshape(block_input.shape),
        input_grad.reshape(block_input.shape),
        total.reshape(-1),
    )


def solution(mesh):
    return jax.shard_map(
        body,
        mesh=mesh,
        in_specs=(
            P("dp", "space", None, None),
            P("dp", "space", None, None),
            P(("dp", "space")),
            P("dp", None, "space", None),
            P("dp", "space"),
            P("dp", "space"),
        ),
        out_specs=(P("dp", "space", None, None), P("dp", "space", None, None), P(("dp", "space"))),
        check_vma=False,
    )
```

```python
import functools
import math

import jax
import jax.numpy as jnp
from jax import lax
from jax.experimental import pallas as pl
from jax.experimental.pallas import tpu as pltpu
from jax.sharding import PartitionSpec as P

D = 192
HEADS = 6
HEAD_DIM = 32
FF = 768
LEVELS = 8
WIN = 72
LAT_BANDS = 20
LANES = 128
HALF = LANES // 2
KEYS = 80
SCALE = HEAD_DIM ** (-0.5)
LOG2E = math.log2(math.e)
F32 = jnp.float32
BF16 = jnp.bfloat16
VMEM_LIMIT = 58 << 20

norm_eps = 1e-05


def param_layout():
    return [
        ("norm1_gain", (D,)),
        ("norm1_shift", (D,)),
        ("qkv1", (D, 3 * D)),
        ("proj1", (D, D)),
        ("proj1_bias", (D,)),
        ("norm2_gain", (D,)),
        ("norm2_shift", (D,)),
        ("qkv2", (D, 3 * D)),
        ("proj2", (D, D)),
        ("proj2_bias", (D,)),
        ("norm3_gain", (D,)),
        ("norm3_shift", (D,)),
        ("mlp_in", (D, FF)),
        ("mlp_in_bias", (FF,)),
        ("mlp_out", (FF, D)),
        ("mlp_out_bias", (D,)),
        ("earth_bias", (LAT_BANDS, HEADS, WIN, WIN)),
    ]


def param_offsets():
    offsets = {}
    filled = 0
    for entry_name, entry_shape in param_layout():
        offsets[entry_name] = filled
        filled += math.prod(entry_shape)
    return offsets


OFFSET = param_offsets()
BIAS_ROW, BIAS_LANE = divmod(OFFSET["earth_bias"], LANES)
BIAS_ROWS = LAT_BANDS * HEADS * WIN
WIDE = LANES // math.gcd(WIN, LANES)
DENSE = WIN // math.gcd(WIN, LANES)
PERIODS = -(-(BIAS_ROWS // WIDE + 1) // 8) * 8
COL_LO = (OFFSET["norm2_gain"] // LANES) // 8 * 8
COL_HI = -(-BIAS_ROW // 8) * 8 + 8
BIAS_LO = BIAS_ROW // 8 * 8


def mm(left, right):
    return lax.dot_general(left, right, (((1,), (0,)), ((), ())), preferred_element_type=F32)


def mt(left, right):
    return lax.dot_general(left, right, (((1,), (1,)), ((), ())), preferred_element_type=F32)


def lane_ids(rows):
    return lax.broadcasted_iota(jnp.int32, (rows, LANES), 1)


def rows_at(start, count, stride):
    return pl.ds(start, count) if stride == 1 else pl.ds(start, count, stride=stride)


def read_matrix(dense, first_row, name, matrix):
    rows, width = dict(param_layout())[name]
    halves = width // HALF
    step = 1 + halves % 2
    count, stride = rows // step, halves * step // 2
    low = lane_ids(count) < HALF
    for part in range(step):
        for chunk in range(-(-halves // 2)):
            unit = OFFSET[name] // HALF + part * halves + 2 * chunk
            row = unit // 2 - first_row
            value = dense[rows_at(row, count, stride), :]
            if unit % 2:
                after = dense[rows_at(row + 1, count, stride), :]
                value = pltpu.roll(jnp.where(low, after, value), HALF, 1)
            matrix[chunk, rows_at(part, count, step), :] = value


def write_matrix(dense, first_row, name, matrix):
    rows, width = dict(param_layout())[name]
    halves = width // HALF
    step = 1 + halves % 2
    count, stride = rows // step, halves * step // 2
    lane = lane_ids(count)
    for part in range(step):
        piece = 0
        while piece < halves:
            unit = OFFSET[name] // HALF + part * halves + piece
            where_to = rows_at(unit // 2 - first_row, count, stride)
            chunk = piece // 2
            value = matrix[chunk, rows_at(part, count, step), :]
            if unit % 2 == piece % 2 == 0 and piece + 1 < halves:
                dense[where_to, :] = value
                piece += 2
                continue
            if unit % 2 != piece % 2:
                value = pltpu.roll(value, HALF, 1)
            mine = lane < HALF if unit % 2 == 0 else lane >= HALF
            dense[where_to, :] = jnp.where(mine, value, dense[where_to, :])
            piece += 1


def joined(matrix, width):
    chunks = [matrix[k] for k in range(-(-width // LANES))]
    return jnp.concatenate(chunks, axis=1)[:, :width]


def split_into(matrix, value):
    width = value.shape[1]
    for k in range(-(-width // LANES)):
        end = min(width, (k + 1) * LANES)
        matrix[k, :, : end - k * LANES] = value[:, k * LANES : end]


def read_vector(dense, first_row, name):
    size = dict(param_layout())[name][0]
    unit = OFFSET[name] // HALF
    row = unit // 2 - first_row
    turned = dense[row : row + 8, :].T
    pieces = []
    for k in range(size // HALF):
        spot = unit % 2 + k
        pieces.append(turned[spot % 2 * HALF : (spot % 2 + 1) * HALF, spot // 2 : spot // 2 + 1])
    return jnp.concatenate(pieces, axis=0)


def write_vector(dense, first_row, name, sums):
    size = dict(param_layout())[name][0]
    line = jnp.sum(sums.T, axis=0, keepdims=True)
    lane = lane_ids(1)
    for k in range(size // HALF):
        unit = OFFSET[name] // HALF + k
        row = unit // 2 - first_row
        if size % LANES and k == size // HALF - 1:
            tail = line[:, k * HALF :]
            piece = jnp.concatenate([tail, tail], axis=1)
        else:
            piece = line[:, k // 2 * LANES : (k // 2 + 1) * LANES]
            if unit % 2 != k % 2:
                piece = pltpu.roll(piece, HALF, 1)
        mine = lane < HALF if unit % 2 == 0 else lane >= HALF
        dense[row : row + 1, :] = jnp.where(mine, piece, dense[row : row + 1, :])


def read_bias(dense, wide):
    lane = lane_ids(PERIODS)
    for j in range(WIDE):
        row, first = divmod(BIAS_LANE + j * WIN, LANES)
        value = dense[pl.ds(BIAS_ROW + row, PERIODS, stride=DENSE), :]
        if first + WIN > LANES:
            after = dense[pl.ds(BIAS_ROW + row + 1, PERIODS, stride=DENSE), :]
            value = jnp.where(lane < first, after, value)
        if first:
            value = pltpu.roll(value, LANES - first, 1)
        wide[pl.ds(j, PERIODS, stride=WIDE), :] = value


def write_bias(wide, dense, first_row):
    lane = lane_ids(PERIODS)
    for i in range(DENSE):
        begin = i * LANES - BIAS_LANE
        line = begin // WIN
        value = None
        while line * WIN < begin + LANES:
            shift = line * WIN - begin
            piece = wide[pl.ds(WIDE + line, PERIODS, stride=WIDE), :]
            if shift % LANES:
                piece = pltpu.roll(piece, shift % LANES, 1)
            value = piece if value is None else jnp.where(lane >= shift, piece, value)
            line += 1
        dense[pl.ds(BIAS_ROW - first_row + i, PERIODS, stride=DENSE), :] = value


def norm_parts(rows_in):
    mean = jnp.mean(rows_in, axis=0, keepdims=True)
    centered = rows_in - mean
    var = jnp.mean(centered * centered, axis=0, keepdims=True)
    scale = lax.rsqrt(var + norm_eps)
    return centered * scale, scale


def norm_back(grad, unit, scale, gain):
    scaled = grad * gain
    first = jnp.mean(scaled, axis=0, keepdims=True)
    second = jnp.mean(scaled * unit, axis=0, keepdims=True)
    return scale * (scaled - first - unit * second)


def lane_fold(value):
    total = value[:, :LANES]
    for k in range(1, value.shape[1] // LANES):
        total = total + value[:, k * LANES : (k + 1) * LANES]
    return total


def head_rows(h):
    return slice(h * HEAD_DIM, (h + 1) * HEAD_DIM)


def head_lanes(h):
    return slice(h * LANES, (h + 1) * LANES)


def diagonal(full):
    return jnp.concatenate([full[head_rows(h), head_lanes(h)] for h in range(HEADS)], axis=0)


def scatter_heads(block, rows_in):
    for h in range(HEADS):
        block[head_rows(h), head_lanes(h)] = rows_in[head_rows(h), :]


def chooser(first, slots):
    ids = lax.broadcasted_iota(jnp.int32, (PICK, slots.shape[1]), 0).astype(F32).astype(BF16)
    near = jnp.clip(slots - first, -1, PICK).astype(F32).astype(BF16)
    return jnp.where(ids == near, jnp.ones((), BF16), jnp.zeros((), BF16))


def to_slots(rows_t, slots):
    tokens = rows_t.shape[1]
    pick = jnp.concatenate([chooser(k, slots) for k in range(0, tokens, PICK)], axis=0)
    return mm(rows_t, pick).astype(BF16)


def from_slots(slot_rows, slots, first, rows):
    return jnp.concatenate(
        [mt(slot_rows, chooser(first + k, slots)) for k in range(0, rows, PICK)], axis=1
    )


def call(kernel, grid, ins, outs, scratch, name, macs, scalars=0):
    in_specs = [s for _, s in ins]
    spec = pltpu.PrefetchScalarGridSpec(
        num_scalar_prefetch=scalars,
        grid=grid,
        in_specs=in_specs[scalars:],
        out_specs=[s for _, _, s in outs],
        scratch_shapes=scratch,
    )
    return pl.pallas_call(
        kernel,
        grid_spec=spec,
        out_shape=[jax.ShapeDtypeStruct(shape, kind) for shape, kind, _ in outs],
        compiler_params=pltpu.CompilerParams(
            dimension_semantics=("arbitrary",) * len(grid), vmem_limit_bytes=VMEM_LIMIT
        ),
        cost_estimate=pl.CostEstimate(
            flops=2 * macs,
            transcendentals=0,
            bytes_accessed=sum(a.size * a.dtype.itemsize for a, _ in ins)
            + sum(math.prod(shape) * jnp.dtype(kind).itemsize for shape, kind, _ in outs),
        ),
        name=name,
    )(*[a for a, _ in ins])


def padded_rows(rows):
    return -(-(rows + 1) // 8) * 8


def whole_block(shape):
    return pl.BlockSpec(shape, lambda *_: (0,) * len(shape))


SLOT_BLOCK = 1024
TURNS = 12
PICK = 256
TOKEN_BLOCK = 768


def shift_kernel(x_ref, slots_ref, out_ref, x_t):
    @pl.when(pl.program_id(0) == 0)
    def _():
        x_t[...] = x_ref[...].astype(F32).T.astype(BF16)

    out_ref[...] = to_slots(x_t[...], slots_ref[...])


def shift_call(tokens, slots):
    count, n = tokens.shape[0], slots.shape[1]
    return call(
        shift_kernel,
        (n // SLOT_BLOCK,),
        [
            (tokens, whole_block(tokens.shape)),
            (slots, pl.BlockSpec((1, SLOT_BLOCK), lambda i: (0, i))),
        ],
        [((D, n), BF16, pl.BlockSpec((D, SLOT_BLOCK), lambda i: (0, i)))],
        [pltpu.VMEM((D, count), BF16)],
        "shift",
        D * count * n,
    )[0]


def load_dense(me_ref, parts, plan, blocks, dense, sem, order, rows):
    copies = []
    for part, first, spot, count, row in plan:
        copies.append(
            pltpu.make_async_copy(
                parts[part].at[pl.ds(first, count)],
                blocks.at[pl.ds(spot, count), pl.ds(row, parts[part].shape[1])],
                sem,
            )
        )
    for copy in copies:
        copy.start()
    for copy in copies:
        copy.wait()
    shards = blocks.shape[0]
    for shard in range(shards):
        spot = position(me_ref[0] ^ shard, order)
        dense[shard * rows : (shard + 1) * rows, :] = blocks[spot, :rows, :].astype(F32)
    if dense.shape[0] > shards * rows:
        dense[shards * rows :, :] = jnp.zeros((dense.shape[0] - shards * rows, LANES), F32)


def position(relative, order):
    spot = 0
    for place, bit in enumerate(reversed(order)):
        spot = spot + ((relative >> bit) & 1) * (1 << place)
    return spot


def band_of(table, window, me_ref, space, steps):
    if not space:
        return table[0, window]
    each = steps * (SLOT_BLOCK // LANES) // space
    return table[window // each, me_ref[0] % space * each + window % each]


def window_forward_kernel(me_ref, band_ref, *refs, parts, plan, order, rows, steps, space):
    fused = space > 0
    ins = refs[:parts]
    refs = refs[parts:]
    if fused:
        shifted_ref, slots_ref, x_ref = refs[:3]
        refs = refs[3:]
    else:
        shifted_ref, refs = refs[0], refs[1:]
    (
        out_ref,
        qkv_ref,
        mixed_ref,
        prob_ref,
        weights_ref,
        column_ref,
        vec,
        table_ref,
        blocks,
        dense,
        wide,
        bias,
        mat,
        qkv_t,
        proj_t,
        spread,
        y_all,
        band_s,
        sem,
    ) = refs
    step = pl.program_id(0)

    @pl.when(step == 0)
    def _():
        load_dense(me_ref, ins, plan, blocks, dense, sem, order, rows)
        if fused:
            lines = []
            for source in range(space):
                shard = me_ref[0] // space * space + source
                tile = blocks[position(me_ref[0] ^ shard, order), rows // 8 * 8 : rows // 8 * 8 + 8, :]
                lines.append(tile.astype(F32)[rows % 8 : rows % 8 + 1])
            table_ref[...] = jnp.concatenate(lines, axis=0).astype(jnp.int32)
            copy = pltpu.make_async_copy(table_ref, band_s, sem)
            copy.start()
            copy.wait()
        column_ref[...] = dense[COL_LO:COL_HI, :]
        read_matrix(dense, 0, "qkv1", mat)
        weights_ref[:, : 3 * D] = joined(mat, 3 * D).astype(BF16)
        qkv_t[...] = joined(mat, 3 * D).T.astype(BF16)
        read_matrix(dense, 0, "proj1", mat)
        weights_ref[:, 3 * D :] = joined(mat, D).astype(BF16)
        proj_t[...] = joined(mat, D).T.astype(BF16)
        vec[:, 0:1] = read_vector(dense, 0, "norm1_gain")
        vec[:, 1:2] = read_vector(dense, 0, "norm1_shift")
        vec[:, 2:3] = read_vector(dense, 0, "proj1_bias")
        read_bias(dense, wide)
        wide[BIAS_ROWS:, :] = jnp.zeros((wide.shape[0] - BIAS_ROWS, LANES), F32)

        def turn(k, _):
            for j in range(TURNS):
                spot = pl.multiple_of((k * TURNS + j) * WIN, 8)
                bias[k * TURNS + j, :WIN, :] = wide[pl.ds(spot, LANES), :].T[:WIN].astype(BF16)
            return 0

        lax.fori_loop(0, LAT_BANDS * HEADS // TURNS, turn, 0)
        bias[:, WIN:, :] = jnp.full((LAT_BANDS * HEADS, KEYS - WIN, LANES), -jnp.inf, BF16)
        spread[...] = jnp.zeros_like(spread)

    @pl.when(step < steps)
    def _():
        per_step = SLOT_BLOCK // LANES
        unit, _ = norm_parts(shifted_ref[...].astype(F32))
        normed = (unit * vec[:, 0:1] + vec[:, 1:2]).astype(BF16)
        qkv = mm(qkv_t[...], normed).astype(BF16)
        qkv_ref[...] = qkv
        mixed = []
        for w in range(per_step):
            lanes = slice(w * LANES, (w + 1) * LANES)
            band = band_of(band_s if fused else band_ref, step * per_step + w, me_ref, space, steps)
            scatter_heads(spread.at[w], qkv[:D, lanes])
            scores = mm(qkv[D : 2 * D, lanes].T[:KEYS], spread[w])
            probs = []
            for h in range(HEADS):
                score = scores[:, head_lanes(h)] * SCALE + bias[band * HEADS + h].astype(F32)
                grown = jnp.exp(score - jnp.max(score, axis=0, keepdims=True))
                probs.append(
                    (grown * (1.0 / jnp.sum(grown, axis=0, keepdims=True))).astype(BF16)
                )
            prob = jnp.concatenate(probs, axis=1)
            prob_ref[w] = prob
            tall = jnp.concatenate([prob, jnp.zeros((LANES - KEYS, HEADS * LANES), BF16)], axis=0)
            mixed.append(diagonal(mm(qkv[2 * D :, lanes], tall)))
        mixed = jnp.concatenate(mixed, axis=1).astype(BF16)
        mixed_ref[...] = mixed
        result = (mm(proj_t[...], mixed) + vec[:, 2:3]).astype(BF16)
        if fused:
            y_all[:, pl.ds(pl.multiple_of(step * SLOT_BLOCK, SLOT_BLOCK), SLOT_BLOCK)] = result
        else:
            out_ref[...] = result

    if fused:

        @pl.when(step >= steps)
        def _():
            branch = from_slots(
                y_all[...], slots_ref[...], (step - steps) * TOKEN_BLOCK, TOKEN_BLOCK
            )
            out_ref[...] = x_ref[...].astype(F32).T + branch


def window_forward_call(me, bands, parts, plan, order, shards, rows, shifted, tokens, slots, space):
    fused = space > 0
    n = shifted.shape[1]
    steps = n // SLOT_BLOCK
    per_step = SLOT_BLOCK // LANES
    padded = padded_rows(rows)
    flat_rows = max(shards * rows, BIAS_ROW + DENSE * PERIODS + 8)
    slot_block = lambda r: pl.BlockSpec((r, SLOT_BLOCK), lambda i, *_: (0, jnp.minimum(i, steps - 1)))
    ins = [(me, None), (bands, None)]
    ins += [(p, pl.BlockSpec(memory_space=pl.ANY)) for p in parts]
    ins += [(shifted, slot_block(D))]
    if fused:
        count = tokens.shape[0]
        late = lambda i: jnp.maximum(i - steps, 0)
        ins += [
            (slots, whole_block(slots.shape)),
            (tokens, pl.BlockSpec((TOKEN_BLOCK, D), lambda i, *_: (late(i), 0))),
        ]
        first = ((D, count), F32, pl.BlockSpec((D, TOKEN_BLOCK), lambda i, *_: (0, late(i))))
        grid = steps + count // TOKEN_BLOCK
    else:
        first = ((D, n), BF16, slot_block(D))
        grid = steps
    outs = [
        first,
        ((3 * D, n), BF16, slot_block(3 * D)),
        ((D, n), BF16, slot_block(D)),
        (
            (n // LANES, KEYS, HEADS * LANES),
            BF16,
            pl.BlockSpec(
                (per_step, KEYS, HEADS * LANES), lambda i, *_: (jnp.minimum(i, steps - 1), 0, 0)
            ),
        ),
        ((D, 4 * D), BF16, whole_block((D, 4 * D))),
        ((COL_HI - COL_LO, LANES), F32, whole_block((COL_HI - COL_LO, LANES))),
        ((D, LANES), F32, whole_block((D, LANES))),
        ((max(space, 1), LANES), jnp.int32, whole_block((max(space, 1), LANES))),
    ]
    scratch = [
        pltpu.VMEM((shards, padded, LANES), BF16),
        pltpu.VMEM((flat_rows, LANES), F32),
        pltpu.VMEM((WIDE * PERIODS + LANES, LANES), F32),
        pltpu.VMEM((LAT_BANDS * HEADS, KEYS, LANES), BF16),
        pltpu.VMEM((5, D, LANES), F32),
        pltpu.VMEM((3 * D, D), BF16),
        pltpu.VMEM((D, D), BF16),
        pltpu.VMEM((per_step, D, HEADS * LANES), BF16),
        pltpu.VMEM((D, n), BF16),
        pltpu.SMEM((max(space, 1), LANES), jnp.int32),
        pltpu.SemaphoreType.DMA,
    ]
    kernel = functools.partial(
        window_forward_kernel,
        parts=len(parts),
        plan=plan,
        order=order,
        rows=rows,
        steps=steps,
        space=space,
    )
    return call(kernel, (grid,), ins, outs, scratch, "window_forward", 12 * D * D * n, scalars=2)


COLUMN_BLOCK = 768
COLUMN_VECTORS = (
    "norm2_gain",
    "norm2_shift",
    "proj2_bias",
    "norm3_gain",
    "norm3_shift",
    "mlp_out_bias",
)
COLUMN_MATRICES = ("qkv2", "proj2", "mlp_in", "mlp_out")


def column_kernel(
    dense,
    x_ref,
    cot_ref,
    count_ref,
    out_ref,
    after_ref,
    branch_ref,
    grad_ref,
    mat,
    tall,
    w_qkv,
    w_proj,
    w_in,
    w_out,
    t_qkv,
    t_proj,
    t_in,
    t_out,
    vec,
    fvec,
    n2_s,
    dqkv_s,
    mixed_s,
    attn_s,
    n3_s,
    dpre_s,
    act_s,
    cot_s,
    sums,
    fsums,
    spread,
):
    step = pl.program_id(0)

    @pl.when(step == 0)
    def _():
        for name, plain, turned in (
            ("qkv2", w_qkv, t_qkv),
            ("proj2", w_proj, t_proj),
            ("mlp_in", w_in, t_in),
            ("mlp_out", w_out, t_out),
        ):
            rows, width = plain.shape
            source = tall if rows == FF else mat
            read_matrix(dense, COL_LO, name, source)
            plain[...] = joined(source, width).astype(BF16)
            turned[...] = joined(source, width).T.astype(BF16)
        for k, name in enumerate(COLUMN_VECTORS):
            vec[:, k : k + 1] = read_vector(dense, COL_LO, name)
        fvec[:, 0:1] = read_vector(dense, COL_LO, "mlp_in_bias")
        sums[...] = jnp.zeros_like(sums)
        fsums[...] = jnp.zeros_like(fsums)
        spread[...] = jnp.zeros_like(spread)

    groups = COLUMN_BLOCK // LANES
    cols = pl.ds(pl.multiple_of(step * COLUMN_BLOCK, COLUMN_BLOCK), COLUMN_BLOCK)
    x = x_ref[...]
    gain2, shift2, bias2, gain3, shift3, bias_out = [vec[:, k : k + 1] for k in range(6)]
    unit2, scale2 = norm_parts(x)
    n2 = (unit2 * gain2 + shift2).astype(BF16)
    n2_s[:, cols] = n2
    qkv = mm(t_qkv[...], n2).astype(BF16)
    key_id = lax.broadcasted_iota(jnp.int32, (LANES, LANES), 0)
    query_id = lax.broadcasted_iota(jnp.int32, (LANES, LANES), 1)
    same = key_id // LEVELS == query_id // LEVELS
    level = key_id % LEVELS
    probs, tall_probs, mixed = {}, {}, []
    for g in range(groups):
        lanes = slice(g * LANES, (g + 1) * LANES)
        valid = jnp.logical_and(same, level < count_ref[:, lanes])
        scatter_heads(spread.at[0, g], qkv[:D, lanes])
        scores = mm(qkv[D : 2 * D, lanes].T, spread[0, g])
        rounded = []
        for h in range(HEADS):
            score = jnp.where(valid, scores[:, head_lanes(h)] * SCALE, -jnp.inf)
            grown = jnp.exp(score - jnp.max(score, axis=0, keepdims=True))
            prob = grown * (1.0 / jnp.sum(grown, axis=0, keepdims=True))
            probs[g, h] = prob
            rounded.append(prob.astype(BF16))
        tall_probs[g] = jnp.concatenate(rounded, axis=1)
        mixed.append(diagonal(mm(qkv[2 * D :, lanes], tall_probs[g])))
    mixed = jnp.concatenate(mixed, axis=1).astype(BF16)
    mixed_s[:, cols] = mixed
    middle = x + (mm(t_proj[...], mixed) + bias2)
    unit3, scale3 = norm_parts(middle)
    n3 = (unit3 * gain3 + shift3).astype(BF16)
    n3_s[:, cols] = n3
    pre = mm(t_in[...], n3) + fvec[:, 0:1]
    root = math.sqrt(2.0 / math.pi)
    square = pre * pre
    share = 0.5 + 0.5 * jnp.tanh(pre * (root + (root * 0.044715) * square))
    act = pre * share
    slope = share + act * (1.0 - share) * (2.0 * root + (6.0 * root * 0.044715) * square)
    act = act.astype(BF16)
    act_s[:, cols] = act
    output = middle + (mm(t_out[...], act) + bias_out)
    out_ref[...] = output.T.astype(BF16)

    cot = cot_ref[...].astype(F32).T
    cot_bf = cot.astype(BF16)
    cot_s[:, cols] = cot_bf
    dpre = (mm(w_out[...], cot_bf) * slope).astype(BF16)
    dpre_s[:, cols] = dpre
    dn3 = mm(w_in[...], dpre)
    dmiddle = cot + norm_back(dn3, unit3, scale3, gain3)
    dattn = dmiddle.astype(BF16)
    attn_s[:, cols] = dattn
    dmixed = mm(w_proj[...], dattn).astype(BF16)
    dq, dk, dv = [], [], []
    for g in range(groups):
        lanes = slice(g * LANES, (g + 1) * LANES)
        scatter_heads(spread.at[1, g], dmixed[:, lanes])
        dprobs = mm(qkv[2 * D :, lanes].T, spread[1, g])
        dscores = []
        for h in range(HEADS):
            prob, dprob = probs[g, h], dprobs[:, head_lanes(h)]
            dscores.append(
                (prob * (dprob - jnp.sum(prob * dprob, axis=0, keepdims=True))).astype(BF16)
            )
        dscores = jnp.concatenate(dscores, axis=1)
        dq.append(diagonal(mm(qkv[D : 2 * D, lanes], dscores)) * SCALE)
        dk.append(mt(spread[0, g], dscores) * SCALE)
        dv.append(mt(spread[1, g], tall_probs[g]))
    dqkv = jnp.concatenate([jnp.concatenate(d, axis=1) for d in (dq, dk, dv)], axis=0).astype(BF16)
    dqkv_s[:, cols] = dqkv
    dn2 = mm(w_qkv[...], dqkv)
    dafter = dmiddle + norm_back(dn2, unit2, scale2, gain2)
    after_ref[...] = dafter
    branch_ref[...] = dafter.astype(BF16)
    for k, value in enumerate(
        (dn2 * unit2, dn2, dattn.astype(F32), dn3 * unit3, dn3, cot_bf.astype(F32))
    ):
        sums[k] += lane_fold(value)
    fsums[...] += lane_fold(dpre.astype(F32))

    @pl.when(step == pl.num_programs(0) - 1)
    def _():
        grad_ref[...] = jnp.zeros_like(grad_ref)
        split_into(mat, mt(n2_s[...], dqkv_s[...]))
        write_matrix(grad_ref, COL_LO, "qkv2", mat)
        split_into(mat, mt(mixed_s[...], attn_s[...]))
        write_matrix(grad_ref, COL_LO, "proj2", mat)
        split_into(mat, mt(n3_s[...], dpre_s[...]))
        write_matrix(grad_ref, COL_LO, "mlp_in", mat)
        split_into(tall, mt(act_s[...], cot_s[...]))
        write_matrix(grad_ref, COL_LO, "mlp_out", tall)
        for k, name in enumerate(COLUMN_VECTORS):
            write_vector(grad_ref, COL_LO, name, sums[k])
        write_vector(grad_ref, COL_LO, "mlp_in_bias", fsums[...])


def column_call(dense, after_t, cotangent, counts):
    n = after_t.shape[1]
    feature = lambda r: pl.BlockSpec((r, COLUMN_BLOCK), lambda i: (0, i))
    token = pl.BlockSpec((COLUMN_BLOCK, D), lambda i: (i, 0))
    keep = lambda r: pltpu.VMEM((r, n), BF16)
    return call(
        column_kernel,
        (n // COLUMN_BLOCK,),
        [
            (dense, whole_block(dense.shape)),
            (after_t, feature(D)),
            (cotangent, token),
            (counts, feature(1)),
        ],
        [
            ((n, D), BF16, token),
            ((D, n), F32, feature(D)),
            ((D, n), BF16, feature(D)),
            (dense.shape, F32, whole_block(dense.shape)),
        ],
        [
            pltpu.VMEM((FF // LANES, D, LANES), F32),
            pltpu.VMEM((2, FF, LANES), F32),
            pltpu.VMEM((D, 3 * D), BF16),
            pltpu.VMEM((D, D), BF16),
            pltpu.VMEM((D, FF), BF16),
            pltpu.VMEM((FF, D), BF16),
            pltpu.VMEM((3 * D, D), BF16),
            pltpu.VMEM((D, D), BF16),
            pltpu.VMEM((FF, D), BF16),
            pltpu.VMEM((D, FF), BF16),
            pltpu.VMEM((D, LANES), F32),
            pltpu.VMEM((FF, LANES), F32),
            keep(D),
            keep(3 * D),
            keep(D),
            keep(D),
            keep(D),
            keep(FF),
            keep(FF),
            keep(D),
            pltpu.VMEM((6, D, LANES), F32),
            pltpu.VMEM((FF, LANES), F32),
            pltpu.VMEM((2, COLUMN_BLOCK // LANES, D, HEADS * LANES), BF16),
        ],
        "column",
        40 * D * D * n,
    )


def window_backward_kernel(me_ref, band_ref, *refs, order, shard_rows, space):
    fused = space > 0
    if fused:
        slots_ref, refs = refs[0], refs[1:]
    (
        grad_ref,
        weights_ref,
        vec,
        column_ref,
        shifted_ref,
        qkv_ref,
        mixed_ref,
        prob_ref,
        out_ref,
        keep_ref,
        send_ref,
        total,
        kept,
        wide,
        dense,
        mat,
        blocks,
        spread,
        normed_s,
        dqkv_s,
        mixed_s,
        grad_s,
        sums,
        sem,
    ) = refs
    step = pl.program_id(0)
    per_step = SLOT_BLOCK // LANES

    @pl.when(step == 0)
    def _():
        total[...] = jnp.zeros_like(total)
        sums[...] = jnp.zeros_like(sums)
        spread[...] = jnp.zeros_like(spread)

    cols = pl.ds(pl.multiple_of(step * SLOT_BLOCK, SLOT_BLOCK), SLOT_BLOCK)
    if fused:
        grad = to_slots(grad_ref[...], slots_ref[...])
    else:
        grad = grad_ref[...]
    grad_s[:, cols] = grad
    mixed_s[:, cols] = mixed_ref[...]
    dmixed = mm(weights_ref[:, 3 * D :], grad).astype(BF16)
    qkv = qkv_ref[...]
    dq, dk, dv = [], [], []
    for w in range(per_step):
        lanes = slice(w * LANES, (w + 1) * LANES)
        scatter_heads(spread.at[0, w], qkv[:D, lanes])
        scatter_heads(spread.at[1, w], dmixed[:, lanes])
        dprobs = mm(qkv[2 * D :, lanes].T[:KEYS], spread[1, w])
        dscores = []
        for h in range(HEADS):
            prob = prob_ref[w, :, head_lanes(h)].astype(F32)
            dprob = dprobs[:, head_lanes(h)]
            dscore = (prob * (dprob - jnp.sum(prob * dprob, axis=0, keepdims=True))).astype(BF16)
            dscores.append(dscore)
        for h in range(HEADS):
            kept[w, h] = dscores[h].astype(F32)
        blank = jnp.zeros((LANES - KEYS, HEADS * LANES), BF16)
        dscores = jnp.concatenate([jnp.concatenate(dscores, axis=1), blank], axis=0)
        probs = jnp.concatenate([prob_ref[w], blank], axis=0)
        dq.append(diagonal(mm(qkv[D : 2 * D, lanes], dscores)) * SCALE)
        dk.append(mt(spread[0, w], dscores) * SCALE)
        dv.append(mt(spread[1, w], probs))
    dqkv = jnp.concatenate([jnp.concatenate(d, axis=1) for d in (dq, dk, dv)], axis=0).astype(BF16)
    dqkv_s[:, cols] = dqkv

    def add(w, _):
        band = band_of(band_ref, step * per_step + w, me_ref, space, pl.num_programs(0))
        total[band] += kept[w]
        return 0

    lax.fori_loop(0, per_step, add, 0)
    unit, scale = norm_parts(shifted_ref[...].astype(F32))
    normed_s[:, cols] = (unit * vec[:, 0:1] + vec[:, 1:2]).astype(BF16)
    dnormed = mm(weights_ref[:, : 3 * D], dqkv)
    out_ref[...] = norm_back(dnormed, unit, scale, vec[:, 0:1]).astype(BF16)
    for k, value in enumerate((dnormed * unit, dnormed, grad.astype(F32))):
        sums[k] += lane_fold(value)

    @pl.when(step == pl.num_programs(0) - 1)
    def _():
        wide[:WIDE, :] = jnp.zeros((WIDE, LANES), F32)
        wide[WIDE + BIAS_ROWS :, :] = jnp.zeros((wide.shape[0] - WIDE - BIAS_ROWS, LANES), F32)

        def turn(k, _):
            for h in range(HEADS):
                spot = pl.multiple_of(WIDE + (k * HEADS + h) * WIN, 8)
                wide[pl.ds(spot, WIN), :KEYS] = total[k, h].T[:WIN]
            return 0

        lax.fori_loop(0, LAT_BANDS, turn, 0)
        dense[:COL_LO, :] = jnp.zeros((COL_LO, LANES), F32)
        write_bias(wide, dense, 0)
        covered = BIAS_ROW + DENSE * PERIODS
        dense[covered:, :] = jnp.zeros((dense.shape[0] - covered, LANES), F32)
        both = column_ref[COL_HI - COL_LO - 16 :, :]
        rows = lax.broadcasted_iota(jnp.int32, both.shape, 0) + (COL_HI - 16)
        lane = lane_ids(16)
        start = rows * LANES + lane < OFFSET["earth_bias"]
        dense[COL_LO : COL_HI - 16, :] = column_ref[: COL_HI - COL_LO - 16, :]
        dense[COL_HI - 16 : COL_HI, :] = jnp.where(start, both, dense[COL_HI - 16 : COL_HI, :])
        split_into(mat, mt(normed_s[...], dqkv_s[...]))
        write_matrix(dense, 0, "qkv1", mat)
        split_into(mat, mt(mixed_s[...], grad_s[...]))
        write_matrix(dense, 0, "proj1", mat)
        for k, name in enumerate(("norm1_gain", "norm1_shift", "proj1_bias")):
            write_vector(dense, 0, name, sums[k])
        shards, rows = blocks.shape[0], shard_rows
        for shard in range(shards):
            spot = position(me_ref[0] ^ shard, order)
            blocks[spot, :rows, :] = dense[shard * rows : (shard + 1) * rows, :].astype(BF16)
        first = pltpu.make_async_copy(blocks.at[pl.ds(0, shards // 2)], keep_ref, sem.at[0])
        second = pltpu.make_async_copy(
            blocks.at[pl.ds(shards // 2, shards // 2)], send_ref, sem.at[1]
        )
        first.start()
        second.start()
        first.wait()
        second.wait()


def window_backward_call(
    me, bands, order, shards, rows, slots, grad, weights, vec, column_grad, shifted, qkv, mixed, prob, space
):
    fused = space > 0
    padded = padded_rows(rows)
    n = shifted.shape[1]
    per_step = SLOT_BLOCK // LANES
    slot_block = lambda r: pl.BlockSpec((r, SLOT_BLOCK), lambda i, *_: (0, i))
    ins = [(me, None), (bands, None)]
    if fused:
        ins += [(slots, slot_block(1)), (grad, whole_block(grad.shape))]
    else:
        ins += [(grad, slot_block(D))]
    ins += [
        (weights, whole_block(weights.shape)),
        (vec, whole_block(vec.shape)),
        (column_grad, whole_block(column_grad.shape)),
        (shifted, slot_block(D)),
        (qkv, slot_block(3 * D)),
        (mixed, slot_block(D)),
        (
            prob,
            pl.BlockSpec((per_step, KEYS, HEADS * LANES), lambda i, *_: (i, 0, 0)),
        ),
    ]
    flat_rows = max(shards * rows, BIAS_ROW + DENSE * PERIODS + 8)
    outs = [
        ((D, n), BF16, slot_block(D)),
        ((shards // 2, padded, LANES), BF16, pl.BlockSpec(memory_space=pl.ANY)),
        ((shards // 2, padded, LANES), BF16, pl.BlockSpec(memory_space=pl.ANY)),
    ]
    scratch = [
        pltpu.VMEM((LAT_BANDS, HEADS, KEYS, LANES), F32),
        pltpu.VMEM((per_step, HEADS, KEYS, LANES), F32),
        pltpu.VMEM((WIDE * (PERIODS + 2), LANES), F32),
        pltpu.VMEM((flat_rows, LANES), F32),
        pltpu.VMEM((5, D, LANES), F32),
        pltpu.VMEM((shards, padded, LANES), BF16),
        pltpu.VMEM((2, per_step, D, HEADS * LANES), BF16),
        pltpu.VMEM((D, n), BF16),
        pltpu.VMEM((3 * D, n), BF16),
        pltpu.VMEM((D, n), BF16),
        pltpu.VMEM((D, n), BF16),
        pltpu.VMEM((3, D, LANES), F32),
        pltpu.SemaphoreType.DMA((2,)),
    ]
    kernel = functools.partial(
        window_backward_kernel, order=order, shard_rows=rows, space=space
    )
    return call(kernel, (n // SLOT_BLOCK,), ins, outs, scratch, "window_backward", 24 * D * D * n, scalars=2)


def finish_kernel(shift_ref, slots_ref, after_ref, out_ref):
    first = pl.program_id(0) * TOKEN_BLOCK
    back = from_slots(shift_ref[...], slots_ref[...], first, TOKEN_BLOCK)
    out_ref[...] = (after_ref[...] + back).T


def finish_call(grad_shifted, slots, after_t):
    n = after_t.shape[1]
    return call(
        finish_kernel,
        (n // TOKEN_BLOCK,),
        [
            (grad_shifted, whole_block(grad_shifted.shape)),
            (slots, whole_block(slots.shape)),
            (after_t, pl.BlockSpec((D, TOKEN_BLOCK), lambda i: (0, i))),
        ],
        [((n, D), F32, pl.BlockSpec((TOKEN_BLOCK, D), lambda i: (i, 0)))],
        [],
        "finish",
        D * n * slots.shape[1],
    )[0]


def body(block_input, cotangent, params, send_rows, window_band, level_count):
    model_width = block_input.shape[-1]
    rows_dev = block_input.shape[1] * block_input.shape[2]
    n_space, per_peer = send_rows.shape[1], send_rows.shape[3]
    devices = lax.axis_size(("dp", "space"))
    group = WIN // math.gcd(per_peer, WIN)
    if n_space % group:
        group = n_space
    fused = group == 1
    dest = n_space // group
    per_dest = group * per_peer // WIN
    member_groups = [[first + k for k in range(group)] for first in range(0, n_space, group)]
    place = lax.axis_index("space")
    index = lax.axis_index(("dp", "space"))
    me = index.astype(jnp.int32).reshape(1)
    bits = devices.bit_length() - 1
    order = [0] + list(range(bits - 1, 0, -1))

    def swap(value, bit):
        pairs = [(k, k ^ (1 << bit)) for k in range(devices)]
        return lax.ppermute(value, ("dp", "space"), pairs)

    def exchange(value):
        return lax.all_to_all(
            value, "space", split_axis=0, concat_axis=0, tiled=True, axis_index_groups=member_groups
        )

    def to_windows(rows):
        moved = exchange(rows[route_flat]).reshape(group, dest, per_peer, model_width)
        windows = moved.transpose(1, 0, 2, 3).reshape(-1, WIN, model_width)
        windows = jnp.pad(windows, ((0, 0), (0, LANES - WIN), (0, 0)))
        return windows.reshape(-1, model_width).T

    def from_windows(rows_t):
        rows = rows_t.T.reshape(-1, LANES, model_width)[:, :WIN]
        moved = rows.reshape(dest, group, per_peer, model_width).transpose(1, 0, 2, 3)
        rows = exchange(moved.reshape(rows_dev, model_width))
        return jnp.zeros((rows_dev, model_width), rows.dtype).at[route_flat].set(rows)

    flat_in = block_input[0].reshape(rows_dev, model_width)
    routes = send_rows[0, :, 0, :]
    route_flat = routes.reshape(-1)
    slots = jnp.pad(
        routes.reshape(-1, WIN), ((0, 0), (0, LANES - WIN)), constant_values=-1
    ).reshape(1, -1)
    if fused:
        bands = jnp.zeros((1, LANES), jnp.int32)
    else:
        all_bands = lax.all_gather(window_band[0], "space", axis=0)
        bands = lax.dynamic_slice(
            all_bands, ((place % group) * dest, (place // group) * per_dest), (dest, per_dest)
        ).reshape(1, -1)
        shifted = to_windows(flat_in)

    shard_rows = params.shape[0] // LANES
    padded = padded_rows(shard_rows)
    band_row = jnp.pad(window_band[0].astype(BF16), (0, LANES - window_band.shape[1]))
    held = jnp.concatenate(
        [
            params.astype(BF16).reshape(shard_rows, LANES),
            band_row.reshape(1, LANES),
            jnp.zeros((padded - shard_rows - 1, LANES), BF16),
        ],
        axis=0,
    ).reshape(1, padded, LANES)
    for bit in reversed(order[3:]):
        held = jnp.concatenate([held, swap(held, bit)], axis=0)
    top, next_top = order[1], order[2]
    cut = padded // 16 * 8
    upper, lower = held[:, :cut], held[:, cut:]
    upper = jnp.concatenate([upper, swap(upper, next_top)], axis=0)
    lower = jnp.concatenate([lower, swap(lower, top)], axis=0)
    if fused:
        upper, lower, slots = lax.optimization_barrier((upper, lower, slots))
        shifted = shift_call(flat_in, slots)
    parts = [upper, swap(upper, top), lower, swap(lower, next_top)]
    if fused:
        parts, shifted = lax.optimization_barrier((parts, shifted))
    parts = parts + [swap(part, order[0]) for part in parts]
    few = devices // 8
    plan = []
    for core in range(2):
        base = core * 4 * few
        plan += [(4 * core, 0, base, 2 * few, 0), (4 * core + 1, 0, base + 2 * few, 2 * few, 0)]
        for part, spot in ((2, 0), (3, few)):
            plan += [
                (4 * core + part, 0, base + spot, few, cut),
                (4 * core + part, few, base + spot + 2 * few, few, cut),
            ]
    space = n_space if fused else 0
    first, qkv, mixed, prob, weights, column_rows, vec, table = window_forward_call(
        me, bands, parts, plan, order, devices, shard_rows, shifted, flat_in, slots, space
    )
    if fused:
        bands = table
    if fused:
        after_t = first
    else:
        after_t = (flat_in.astype(F32) + from_windows(first).astype(F32)).T
    counts = jnp.repeat(level_count[0], LEVELS).reshape(1, -1)
    output, grad_after, grad_branch, column_grad = column_call(
        column_rows, after_t, cotangent[0].reshape(rows_dev, model_width), counts
    )
    if not fused:
        grad_branch = to_windows(grad_branch.T)
    grad_shifted, keep, send = window_backward_call(
        me, bands, order, devices, shard_rows, slots, grad_branch, weights, vec, column_grad,
        shifted, qkv, mixed, prob, space
    )
    total = keep.astype(F32) + swap(send, order[0]).astype(F32)
    total, grad_shifted = lax.optimization_barrier((total, grad_shifted))
    if fused:
        input_grad = finish_call(grad_shifted, slots, grad_after)
    else:
        input_grad = grad_after.T + from_windows(grad_shifted).astype(F32)

    def fold(kept, sent, bit):
        return kept + swap(sent.astype(BF16), bit).astype(F32)

    upper = total[:, :cut]
    lower = total[:, cut:].reshape(2, 2, few, padded - cut, LANES)
    upper = fold(upper[: 2 * few], upper[2 * few :], top)
    lower = fold(lower[:, 0], lower[:, 1], next_top)
    upper, lower, input_grad = lax.optimization_barrier((upper, lower, input_grad))
    upper = fold(upper[:few], upper[few:], next_top)
    lower = fold(lower[0], lower[1], top)
    total = jnp.concatenate([upper, lower], axis=1)
    for bit in order[3:]:
        half = total.shape[0] // 2
        total = fold(total[:half], total[half:], bit)
    total = total[0, :shard_rows]
    return (
        output.reshape(block_input.shape),
        input_grad.reshape(block_input.shape),
        total.reshape(-1),
    )


def solution(mesh):
    return jax.shard_map(
        body,
        mesh=mesh,
        in_specs=(
            P("dp", "space", None, None),
            P("dp", "space", None, None),
            P(("dp", "space")),
            P("dp", None, "space", None),
            P("dp", "space"),
            P("dp", "space"),
        ),
        out_specs=(P("dp", "space", None, None), P("dp", "space", None, None), P(("dp", "space"))),
        check_vma=False,
    )
```

```python
import functools
import math

import jax
import jax.numpy as jnp
from jax import lax
from jax.experimental import pallas as pl
from jax.experimental.pallas import tpu as pltpu
from jax.sharding import PartitionSpec as P

D = 192
HEADS = 6
HEAD_DIM = 32
FF = 768
LEVELS = 8
WIN = 72
LAT_BANDS = 20
LANES = 128
HALF = LANES // 2
KEYS = 80
SCALE = HEAD_DIM ** (-0.5)
LOG2E = math.log2(math.e)
F32 = jnp.float32
BF16 = jnp.bfloat16
VMEM_LIMIT = 58 << 20

norm_eps = 1e-05


def param_layout():
    return [
        ("norm1_gain", (D,)),
        ("norm1_shift", (D,)),
        ("qkv1", (D, 3 * D)),
        ("proj1", (D, D)),
        ("proj1_bias", (D,)),
        ("norm2_gain", (D,)),
        ("norm2_shift", (D,)),
        ("qkv2", (D, 3 * D)),
        ("proj2", (D, D)),
        ("proj2_bias", (D,)),
        ("norm3_gain", (D,)),
        ("norm3_shift", (D,)),
        ("mlp_in", (D, FF)),
        ("mlp_in_bias", (FF,)),
        ("mlp_out", (FF, D)),
        ("mlp_out_bias", (D,)),
        ("earth_bias", (LAT_BANDS, HEADS, WIN, WIN)),
    ]


def param_offsets():
    offsets = {}
    filled = 0
    for entry_name, entry_shape in param_layout():
        offsets[entry_name] = filled
        filled += math.prod(entry_shape)
    return offsets


OFFSET = param_offsets()
BIAS_ROW, BIAS_LANE = divmod(OFFSET["earth_bias"], LANES)
BIAS_ROWS = LAT_BANDS * HEADS * WIN
WIDE = LANES // math.gcd(WIN, LANES)
DENSE = WIN // math.gcd(WIN, LANES)
PERIODS = -(-(BIAS_ROWS // WIDE + 1) // 8) * 8
COL_LO = (OFFSET["norm2_gain"] // LANES) // 8 * 8
COL_HI = -(-BIAS_ROW // 8) * 8 + 8
BIAS_LO = BIAS_ROW // 8 * 8


def mm(left, right):
    return lax.dot_general(left, right, (((1,), (0,)), ((), ())), preferred_element_type=F32)


def mt(left, right):
    return lax.dot_general(left, right, (((1,), (1,)), ((), ())), preferred_element_type=F32)


def lane_ids(rows):
    return lax.broadcasted_iota(jnp.int32, (rows, LANES), 1)


def rows_at(start, count, stride):
    return pl.ds(start, count) if stride == 1 else pl.ds(start, count, stride=stride)


def read_matrix(dense, first_row, name, matrix):
    rows, width = dict(param_layout())[name]
    halves = width // HALF
    step = 1 + halves % 2
    count, stride = rows // step, halves * step // 2
    low = lane_ids(count) < HALF
    for part in range(step):
        for chunk in range(-(-halves // 2)):
            unit = OFFSET[name] // HALF + part * halves + 2 * chunk
            row = unit // 2 - first_row
            value = dense[rows_at(row, count, stride), :]
            if unit % 2:
                after = dense[rows_at(row + 1, count, stride), :]
                value = pltpu.roll(jnp.where(low, after, value), HALF, 1)
            matrix[chunk, rows_at(part, count, step), :] = value


def write_matrix(dense, first_row, name, matrix):
    rows, width = dict(param_layout())[name]
    halves = width // HALF
    step = 1 + halves % 2
    count, stride = rows // step, halves * step // 2
    lane = lane_ids(count)
    for part in range(step):
        piece = 0
        while piece < halves:
            unit = OFFSET[name] // HALF + part * halves + piece
            where_to = rows_at(unit // 2 - first_row, count, stride)
            chunk = piece // 2
            value = matrix[chunk, rows_at(part, count, step), :]
            if unit % 2 == piece % 2 == 0 and piece + 1 < halves:
                dense[where_to, :] = value
                piece += 2
                continue
            if unit % 2 != piece % 2:
                value = pltpu.roll(value, HALF, 1)
            mine = lane < HALF if unit % 2 == 0 else lane >= HALF
            dense[where_to, :] = jnp.where(mine, value, dense[where_to, :])
            piece += 1


def joined(matrix, width):
    chunks = [matrix[k] for k in range(-(-width // LANES))]
    return jnp.concatenate(chunks, axis=1)[:, :width]


def split_into(matrix, value):
    width = value.shape[1]
    for k in range(-(-width // LANES)):
        end = min(width, (k + 1) * LANES)
        matrix[k, :, : end - k * LANES] = value[:, k * LANES : end]


def read_vector(dense, first_row, name):
    size = dict(param_layout())[name][0]
    unit = OFFSET[name] // HALF
    row = unit // 2 - first_row
    turned = dense[row : row + 8, :].T
    pieces = []
    for k in range(size // HALF):
        spot = unit % 2 + k
        pieces.append(turned[spot % 2 * HALF : (spot % 2 + 1) * HALF, spot // 2 : spot // 2 + 1])
    return jnp.concatenate(pieces, axis=0)


def write_vector(dense, first_row, name, sums):
    size = dict(param_layout())[name][0]
    line = jnp.sum(sums.T, axis=0, keepdims=True)
    lane = lane_ids(1)
    for k in range(size // HALF):
        unit = OFFSET[name] // HALF + k
        row = unit // 2 - first_row
        if size % LANES and k == size // HALF - 1:
            tail = line[:, k * HALF :]
            piece = jnp.concatenate([tail, tail], axis=1)
        else:
            piece = line[:, k // 2 * LANES : (k // 2 + 1) * LANES]
            if unit % 2 != k % 2:
                piece = pltpu.roll(piece, HALF, 1)
        mine = lane < HALF if unit % 2 == 0 else lane >= HALF
        dense[row : row + 1, :] = jnp.where(mine, piece, dense[row : row + 1, :])


def read_bias(dense, wide):
    lane = lane_ids(PERIODS)
    for j in range(WIDE):
        row, first = divmod(BIAS_LANE + j * WIN, LANES)
        value = dense[pl.ds(BIAS_ROW + row, PERIODS, stride=DENSE), :]
        if first + WIN > LANES:
            after = dense[pl.ds(BIAS_ROW + row + 1, PERIODS, stride=DENSE), :]
            value = jnp.where(lane < first, after, value)
        if first:
            value = pltpu.roll(value, LANES - first, 1)
        wide[pl.ds(j, PERIODS, stride=WIDE), :] = value


def write_bias(wide, dense, first_row):
    lane = lane_ids(PERIODS)
    for i in range(DENSE):
        begin = i * LANES - BIAS_LANE
        line = begin // WIN
        value = None
        while line * WIN < begin + LANES:
            shift = line * WIN - begin
            piece = wide[pl.ds(WIDE + line, PERIODS, stride=WIDE), :]
            if shift % LANES:
                piece = pltpu.roll(piece, shift % LANES, 1)
            value = piece if value is None else jnp.where(lane >= shift, piece, value)
            line += 1
        dense[pl.ds(BIAS_ROW - first_row + i, PERIODS, stride=DENSE), :] = value


def norm_parts(rows_in):
    mean = jnp.mean(rows_in, axis=0, keepdims=True)
    centered = rows_in - mean
    var = jnp.mean(centered * centered, axis=0, keepdims=True)
    scale = lax.rsqrt(var + norm_eps)
    return centered * scale, scale


def norm_back(grad, unit, scale, gain):
    scaled = grad * gain
    first = jnp.mean(scaled, axis=0, keepdims=True)
    second = jnp.mean(scaled * unit, axis=0, keepdims=True)
    return scale * (scaled - first - unit * second)


def lane_fold(value):
    total = value[:, :LANES]
    for k in range(1, value.shape[1] // LANES):
        total = total + value[:, k * LANES : (k + 1) * LANES]
    return total


def head_rows(h):
    return slice(h * HEAD_DIM, (h + 1) * HEAD_DIM)


def head_lanes(h):
    return slice(h * LANES, (h + 1) * LANES)


def interleave(parts):
    parts = list(parts)
    live, started = [], 0
    while live or started < len(parts):
        if started < len(parts):
            live.append(parts[started])
            started += 1
        live = [part for part in live if next(part, live) is None]


def own_column(full, bits):
    heads = []
    for h in range(HEADS):
        tiles = [full[k * LEVELS : (k + 1) * LEVELS, head_lanes(h)] for k in range(LANES // LEVELS)]
        for bit in bits:
            tiles = [jnp.where(bit, b, a) for a, b in zip(tiles[::2], tiles[1::2])]
        heads.append(tiles[0])
    return jnp.concatenate(heads, axis=1)


def all_columns(own, same):
    pair = jnp.concatenate([own, own], axis=0).astype(BF16)
    tall = jnp.concatenate([pair] * (LANES // (2 * LEVELS)), axis=0)
    return jnp.concatenate([tall[:, head_lanes(h)] * same for h in range(HEADS)], axis=1)


def blend(rows_in, weights):
    pieces = []
    for h in range(0, HEADS, 2):
        pair = slice(h * HEAD_DIM, (h + 2) * HEAD_DIM)
        both = mm(rows_in[pair], weights[:, h * LANES : (h + 2) * LANES])
        pieces += [both[:HEAD_DIM, :LANES], both[HEAD_DIM:, LANES:]]
    return jnp.concatenate(pieces, axis=0)


def gather_pairs(block, weights):
    pieces = []
    for h in range(0, HEADS, 2):
        lanes = slice(h * LANES, (h + 2) * LANES)
        pieces.append(mt(block[h * HEAD_DIM : (h + 2) * HEAD_DIM, lanes], weights[:, lanes]))
    return jnp.concatenate(pieces, axis=0)


def scatter_heads(block, rows_in):
    for h in range(HEADS):
        block[head_rows(h), head_lanes(h)] = rows_in[head_rows(h), :]


def chooser(first, slots):
    ids = lax.broadcasted_iota(jnp.int32, (PICK, slots.shape[1]), 0).astype(F32).astype(BF16)
    near = jnp.clip(slots - first, -1, PICK).astype(F32).astype(BF16)
    return jnp.where(ids == near, jnp.ones((), BF16), jnp.zeros((), BF16))


def to_slots(rows_t, slots):
    tokens = rows_t.shape[1]
    pick = jnp.concatenate([chooser(k, slots) for k in range(0, tokens, PICK)], axis=0)
    return mm(rows_t, pick).astype(BF16)


def from_slots(slot_rows, slots, first, rows):
    return jnp.concatenate(
        [mt(slot_rows, chooser(first + k, slots)) for k in range(0, rows, PICK)], axis=1
    )


def call(kernel, grid, ins, outs, scratch, name, macs, scalars=0):
    in_specs = [s for _, s in ins]
    spec = pltpu.PrefetchScalarGridSpec(
        num_scalar_prefetch=scalars,
        grid=grid,
        in_specs=in_specs[scalars:],
        out_specs=[s for _, _, s in outs],
        scratch_shapes=scratch,
    )
    return pl.pallas_call(
        kernel,
        grid_spec=spec,
        out_shape=[jax.ShapeDtypeStruct(shape, kind) for shape, kind, _ in outs],
        compiler_params=pltpu.CompilerParams(
            dimension_semantics=("arbitrary",) * len(grid), vmem_limit_bytes=VMEM_LIMIT
        ),
        cost_estimate=pl.CostEstimate(
            flops=2 * macs,
            transcendentals=0,
            bytes_accessed=sum(a.size * a.dtype.itemsize for a, _ in ins)
            + sum(math.prod(shape) * jnp.dtype(kind).itemsize for shape, kind, _ in outs),
        ),
        name=name,
    )(*[a for a, _ in ins])


def padded_rows(rows):
    return -(-(rows + 1) // 8) * 8


def whole_block(shape):
    return pl.BlockSpec(shape, lambda *_: (0,) * len(shape))


SLOT_BLOCK = 1024
TURNS = 12
PICK = 256
TOKEN_BLOCK = 768


def shift_kernel(x_ref, slots_ref, out_ref, x_t):
    @pl.when(pl.program_id(0) == 0)
    def _():
        x_t[...] = x_ref[...].astype(F32).T.astype(BF16)

    out_ref[...] = to_slots(x_t[...], slots_ref[...])


def shift_call(tokens, slots):
    count, n = tokens.shape[0], slots.shape[1]
    return call(
        shift_kernel,
        (n // SLOT_BLOCK,),
        [
            (tokens, whole_block(tokens.shape)),
            (slots, pl.BlockSpec((1, SLOT_BLOCK), lambda i: (0, i))),
        ],
        [((D, n), BF16, pl.BlockSpec((D, SLOT_BLOCK), lambda i: (0, i)))],
        [pltpu.VMEM((D, count), BF16)],
        "shift",
        D * count * n,
    )[0]


def load_dense(me_ref, parts, plan, blocks, dense, sem, order, rows):
    copies = []
    for part, first, spot, count, row in plan:
        copies.append(
            pltpu.make_async_copy(
                parts[part].at[pl.ds(first, count)],
                blocks.at[pl.ds(spot, count), pl.ds(row, parts[part].shape[1])],
                sem,
            )
        )
    for copy in copies:
        copy.start()
    for copy in copies:
        copy.wait()
    shards = blocks.shape[0]
    for shard in range(shards):
        spot = position(me_ref[0] ^ shard, order)
        dense[shard * rows : (shard + 1) * rows, :] = blocks[spot, :rows, :].astype(F32)
    if dense.shape[0] > shards * rows:
        dense[shards * rows :, :] = jnp.zeros((dense.shape[0] - shards * rows, LANES), F32)


def position(relative, order):
    spot = 0
    for place, bit in enumerate(reversed(order)):
        spot = spot + ((relative >> bit) & 1) * (1 << place)
    return spot


def band_of(table, window, me_ref, space, steps):
    if not space:
        return table[0, window]
    each = steps * (SLOT_BLOCK // LANES) // space
    return table[window // each, me_ref[0] % space * each + window % each]


def window_forward_kernel(me_ref, band_ref, *refs, parts, plan, order, rows, steps, space):
    fused = space > 0
    ins = refs[:parts]
    refs = refs[parts:]
    if fused:
        shifted_ref, slots_ref, x_ref = refs[:3]
        refs = refs[3:]
    else:
        shifted_ref, refs = refs[0], refs[1:]
    (
        out_ref,
        qkv_ref,
        mixed_ref,
        prob_ref,
        weights_ref,
        column_ref,
        vec,
        table_ref,
        blocks,
        dense,
        wide,
        bias,
        mat,
        qkv_t,
        proj_t,
        spread,
        y_all,
        band_s,
        sem,
    ) = refs
    step = pl.program_id(0)

    @pl.when(step == 0)
    def _():
        load_dense(me_ref, ins, plan, blocks, dense, sem, order, rows)
        if fused:
            lines = []
            for source in range(space):
                shard = me_ref[0] // space * space + source
                tile = blocks[position(me_ref[0] ^ shard, order), rows // 8 * 8 : rows // 8 * 8 + 8, :]
                lines.append(tile.astype(F32)[rows % 8 : rows % 8 + 1])
            table_ref[...] = jnp.concatenate(lines, axis=0).astype(jnp.int32)
            copy = pltpu.make_async_copy(table_ref, band_s, sem)
            copy.start()
            copy.wait()
        column_ref[...] = dense[COL_LO:COL_HI, :]
        read_matrix(dense, 0, "qkv1", mat)
        weights_ref[:, : 3 * D] = joined(mat, 3 * D).astype(BF16)
        qkv_t[...] = joined(mat, 3 * D).T.astype(BF16)
        read_matrix(dense, 0, "proj1", mat)
        weights_ref[:, 3 * D :] = joined(mat, D).astype(BF16)
        proj_t[...] = joined(mat, D).T.astype(BF16)
        vec[:, 0:1] = read_vector(dense, 0, "norm1_gain")
        vec[:, 1:2] = read_vector(dense, 0, "norm1_shift")
        vec[:, 2:3] = read_vector(dense, 0, "proj1_bias")
        read_bias(dense, wide)
        wide[BIAS_ROWS:, :] = jnp.zeros((wide.shape[0] - BIAS_ROWS, LANES), F32)

        def turn(k, _):
            for j in range(TURNS):
                spot = pl.multiple_of((k * TURNS + j) * WIN, 8)
                bias[k * TURNS + j, :WIN, :] = wide[pl.ds(spot, LANES), :].T[:WIN].astype(BF16)
            return 0

        lax.fori_loop(0, LAT_BANDS * HEADS // TURNS, turn, 0)
        bias[:, WIN:, :] = jnp.full((LAT_BANDS * HEADS, KEYS - WIN, LANES), -jnp.inf, BF16)
        spread[...] = jnp.zeros_like(spread)

    @pl.when(step < steps)
    def _():
        per_step = SLOT_BLOCK // LANES
        unit, _ = norm_parts(shifted_ref[...].astype(F32))
        normed = (unit * vec[:, 0:1] + vec[:, 1:2]).astype(BF16)
        qkv = mm(qkv_t[...], normed).astype(BF16)
        qkv_ref[...] = qkv
        blank = jnp.zeros((LANES - KEYS, HEADS * LANES), BF16)
        scores, probs, mixed = {}, {}, []
        for turn in range(per_step + 2):
            if turn < per_step:
                lanes = slice(turn * LANES, (turn + 1) * LANES)
                scatter_heads(spread.at[turn], qkv[:D, lanes])
                scores[turn] = mm(qkv[D : 2 * D, lanes].T[:KEYS], spread[turn])
            if 1 <= turn <= per_step:
                w = turn - 1
                table = band_s if fused else band_ref
                band = band_of(table, step * per_step + w, me_ref, space, steps)
                heads = []
                for h in range(HEADS):
                    score = scores[w][:, head_lanes(h)] * SCALE + bias[band * HEADS + h].astype(F32)
                    grown = jnp.exp(score - jnp.max(score, axis=0, keepdims=True))
                    heads.append(
                        (grown * (1.0 / jnp.sum(grown, axis=0, keepdims=True))).astype(BF16)
                    )
                probs[w] = jnp.concatenate(heads, axis=1)
                prob_ref[w] = probs[w]
            if turn >= 2:
                w = turn - 2
                tall = jnp.concatenate([probs[w], blank], axis=0)
                mixed.append(blend(qkv[2 * D :, w * LANES : (w + 1) * LANES], tall))
        mixed = jnp.concatenate(mixed, axis=1).astype(BF16)
        mixed_ref[...] = mixed
        result = (mm(proj_t[...], mixed) + vec[:, 2:3]).astype(BF16)
        if fused:
            y_all[:, pl.ds(pl.multiple_of(step * SLOT_BLOCK, SLOT_BLOCK), SLOT_BLOCK)] = result
        else:
            out_ref[...] = result

    if fused:

        @pl.when(step >= steps)
        def _():
            branch = from_slots(
                y_all[...], slots_ref[...], (step - steps) * TOKEN_BLOCK, TOKEN_BLOCK
            )
            out_ref[...] = x_ref[...].astype(F32).T + branch


def window_forward_call(me, bands, parts, plan, order, shards, rows, shifted, tokens, slots, space):
    fused = space > 0
    n = shifted.shape[1]
    steps = n // SLOT_BLOCK
    per_step = SLOT_BLOCK // LANES
    padded = padded_rows(rows)
    flat_rows = max(shards * rows, BIAS_ROW + DENSE * PERIODS + 8)
    slot_block = lambda r: pl.BlockSpec((r, SLOT_BLOCK), lambda i, *_: (0, jnp.minimum(i, steps - 1)))
    ins = [(me, None), (bands, None)]
    ins += [(p, pl.BlockSpec(memory_space=pl.ANY)) for p in parts]
    ins += [(shifted, slot_block(D))]
    if fused:
        count = tokens.shape[0]
        late = lambda i: jnp.maximum(i - steps, 0)
        ins += [
            (slots, whole_block(slots.shape)),
            (tokens, pl.BlockSpec((TOKEN_BLOCK, D), lambda i, *_: (late(i), 0))),
        ]
        first = ((D, count), F32, pl.BlockSpec((D, TOKEN_BLOCK), lambda i, *_: (0, late(i))))
        grid = steps + count // TOKEN_BLOCK
    else:
        first = ((D, n), BF16, slot_block(D))
        grid = steps
    outs = [
        first,
        ((3 * D, n), BF16, slot_block(3 * D)),
        ((D, n), BF16, slot_block(D)),
        (
            (n // LANES, KEYS, HEADS * LANES),
            BF16,
            pl.BlockSpec(
                (per_step, KEYS, HEADS * LANES), lambda i, *_: (jnp.minimum(i, steps - 1), 0, 0)
            ),
        ),
        ((D, 4 * D), BF16, whole_block((D, 4 * D))),
        ((COL_HI - COL_LO, LANES), F32, whole_block((COL_HI - COL_LO, LANES))),
        ((D, LANES), F32, whole_block((D, LANES))),
        ((max(space, 1), LANES), jnp.int32, whole_block((max(space, 1), LANES))),
    ]
    scratch = [
        pltpu.VMEM((shards, padded, LANES), BF16),
        pltpu.VMEM((flat_rows, LANES), F32),
        pltpu.VMEM((WIDE * PERIODS + LANES, LANES), F32),
        pltpu.VMEM((LAT_BANDS * HEADS, KEYS, LANES), BF16),
        pltpu.VMEM((5, D, LANES), F32),
        pltpu.VMEM((3 * D, D), BF16),
        pltpu.VMEM((D, D), BF16),
        pltpu.VMEM((per_step, D, HEADS * LANES), BF16),
        pltpu.VMEM((D, n), BF16),
        pltpu.SMEM((max(space, 1), LANES), jnp.int32),
        pltpu.SemaphoreType.DMA,
    ]
    kernel = functools.partial(
        window_forward_kernel,
        parts=len(parts),
        plan=plan,
        order=order,
        rows=rows,
        steps=steps,
        space=space,
    )
    return call(kernel, (grid,), ins, outs, scratch, "window_forward", 12 * D * D * n, scalars=2)


COLUMN_BLOCK = 768
COLUMN_PART = 768
COLUMN_VECTORS = (
    "norm2_gain",
    "norm2_shift",
    "proj2_bias",
    "norm3_gain",
    "norm3_shift",
    "mlp_out_bias",
)
COLUMN_MATRICES = ("qkv2", "proj2", "mlp_in", "mlp_out")


def column_kernel(
    dense,
    x_ref,
    cot_ref,
    count_ref,
    out_ref,
    after_ref,
    branch_ref,
    grad_ref,
    mat,
    tall,
    w_qkv,
    w_proj,
    w_in,
    w_out,
    t_qkv,
    t_proj,
    t_in,
    t_out,
    vec,
    fvec,
    n2_s,
    dqkv_s,
    mixed_s,
    attn_s,
    n3_s,
    dpre_s,
    act_s,
    cot_s,
    sums,
    fsums,
    spread,
):
    step = pl.program_id(0)

    @pl.when(step == 0)
    def _():
        for name, plain, turned in (
            ("qkv2", w_qkv, t_qkv),
            ("proj2", w_proj, t_proj),
            ("mlp_in", w_in, t_in),
            ("mlp_out", w_out, t_out),
        ):
            rows, width = plain.shape
            source = tall if rows == FF else mat
            read_matrix(dense, COL_LO, name, source)
            plain[...] = joined(source, width).astype(BF16)
            turned[...] = joined(source, width).T.astype(BF16)
        for k, name in enumerate(COLUMN_VECTORS):
            vec[:, k : k + 1] = read_vector(dense, COL_LO, name)
        fvec[:, 0:1] = read_vector(dense, COL_LO, "mlp_in_bias")
        sums[...] = jnp.zeros_like(sums)
        fsums[...] = jnp.zeros_like(fsums)
        spread[...] = jnp.zeros_like(spread)

    gain2, shift2, bias2, gain3, shift3, bias_out = [vec[:, k : k + 1] for k in range(6)]
    key_id = lax.broadcasted_iota(jnp.int32, (LANES, LANES), 0)
    query_id = lax.broadcasted_iota(jnp.int32, (LANES, LANES), 1)
    same = jnp.where(key_id // LEVELS == query_id // LEVELS, 1.0, 0.0).astype(BF16)
    column = lax.broadcasted_iota(jnp.int32, (LEVELS, LANES), 1) // LEVELS
    bits = [(column >> k) & 1 == 1 for k in range(4)]
    level = lax.broadcasted_iota(jnp.int32, (LEVELS, LANES), 0)
    groups = COLUMN_PART // LANES

    def part_steps(part):
        here = slice(part * COLUMN_PART, (part + 1) * COLUMN_PART)
        start = step * COLUMN_BLOCK + part * COLUMN_PART
        cols = pl.ds(pl.multiple_of(start, COLUMN_PART), COLUMN_PART)
        x = x_ref[:, here]
        unit2, scale2 = norm_parts(x)
        n2 = (unit2 * gain2 + shift2).astype(BF16)
        n2_s[:, cols] = n2
        yield
        qkv = mm(t_qkv[...], n2).astype(BF16)
        yield
        scores = []
        for g in range(groups):
            lanes = slice(g * LANES, (g + 1) * LANES)
            scatter_heads(spread.at[0, part * groups + g], qkv[:D, lanes])
            scores.append(own_column(mm(qkv[D : 2 * D, lanes].T, spread[0, part * groups + g]), bits))
        yield
        probs, tall_probs = [], []
        for g in range(groups):
            begin = part * COLUMN_PART + g * LANES
            valid = level < count_ref[:, begin : begin + LANES]
            score = jnp.where(jnp.concatenate([valid] * HEADS, axis=1), scores[g] * SCALE, -jnp.inf)
            grown = jnp.exp(score - jnp.max(score, axis=0, keepdims=True))
            prob = grown * (1.0 / jnp.sum(grown, axis=0, keepdims=True))
            probs.append(prob)
            tall_probs.append(all_columns(prob, same))
        yield
        mixed = [
            blend(qkv[2 * D :, g * LANES : (g + 1) * LANES], tall_probs[g]) for g in range(groups)
        ]
        mixed = jnp.concatenate(mixed, axis=1).astype(BF16)
        mixed_s[:, cols] = mixed
        projected = mm(t_proj[...], mixed)
        yield
        middle = x + (projected + bias2)
        unit3, scale3 = norm_parts(middle)
        n3 = (unit3 * gain3 + shift3).astype(BF16)
        n3_s[:, cols] = n3
        yield
        pre = mm(t_in[...], n3)
        cot = cot_ref[here, :].astype(F32).T
        cot_bf = cot.astype(BF16)
        cot_s[:, cols] = cot_bf
        dact = mm(w_out[...], cot_bf)
        yield
        pre = pre + fvec[:, 0:1]
        root = math.sqrt(2.0 / math.pi)
        square = pre * pre
        share = 0.5 + 0.5 * jnp.tanh(pre * (root + (root * 0.044715) * square))
        act = pre * share
        slope = share + act * (1.0 - share) * (2.0 * root + (6.0 * root * 0.044715) * square)
        act = act.astype(BF16)
        act_s[:, cols] = act
        dpre = (dact * slope).astype(BF16)
        dpre_s[:, cols] = dpre
        yield
        output = middle + (mm(t_out[...], act) + bias_out)
        out_ref[here, :] = output.T.astype(BF16)
        dn3 = mm(w_in[...], dpre)
        yield
        dmiddle = cot + norm_back(dn3, unit3, scale3, gain3)
        dattn = dmiddle.astype(BF16)
        attn_s[:, cols] = dattn
        sums[2] += lane_fold(dattn.astype(F32))
        sums[3] += lane_fold(dn3 * unit3)
        sums[4] += lane_fold(dn3)
        sums[5] += lane_fold(cot_bf.astype(F32))
        fsums[...] += lane_fold(dpre.astype(F32))
        yield
        dmixed = mm(w_proj[...], dattn).astype(BF16)
        dprobs = []
        for g in range(groups):
            lanes = slice(g * LANES, (g + 1) * LANES)
            scatter_heads(spread.at[1, part * groups + g], dmixed[:, lanes])
            dprobs.append(own_column(mm(qkv[2 * D :, lanes].T, spread[1, part * groups + g]), bits))
        yield
        dscores = []
        for prob, dprob in zip(probs, dprobs):
            dscore = prob * (dprob - jnp.sum(prob * dprob, axis=0, keepdims=True))
            dscores.append(all_columns(dscore, same))
        yield
        dq, dk, dv = [], [], []
        for g in range(groups):
            dq.append(blend(qkv[D : 2 * D, g * LANES : (g + 1) * LANES], dscores[g]) * SCALE)
            dk.append(gather_pairs(spread.at[0, part * groups + g], dscores[g]) * SCALE)
            dv.append(gather_pairs(spread.at[1, part * groups + g], tall_probs[g]))
        dqkv = [jnp.concatenate(d, axis=1) for d in (dq, dk, dv)]
        dqkv = jnp.concatenate(dqkv, axis=0).astype(BF16)
        dqkv_s[:, cols] = dqkv
        dn2 = mm(w_qkv[...], dqkv)
        yield
        dafter = dmiddle + norm_back(dn2, unit2, scale2, gain2)
        after_ref[:, here] = dafter
        branch_ref[:, here] = dafter.astype(BF16)
        sums[0] += lane_fold(dn2 * unit2)
        sums[1] += lane_fold(dn2)

    interleave([part_steps(part) for part in range(COLUMN_BLOCK // COLUMN_PART)])

    @pl.when(step == pl.num_programs(0) - 1)
    def _():
        grad_ref[...] = jnp.zeros_like(grad_ref)
        split_into(mat, mt(n2_s[...], dqkv_s[...]))
        write_matrix(grad_ref, COL_LO, "qkv2", mat)
        split_into(mat, mt(mixed_s[...], attn_s[...]))
        write_matrix(grad_ref, COL_LO, "proj2", mat)
        split_into(mat, mt(n3_s[...], dpre_s[...]))
        write_matrix(grad_ref, COL_LO, "mlp_in", mat)
        split_into(tall, mt(act_s[...], cot_s[...]))
        write_matrix(grad_ref, COL_LO, "mlp_out", tall)
        for k, name in enumerate(COLUMN_VECTORS):
            write_vector(grad_ref, COL_LO, name, sums[k])
        write_vector(grad_ref, COL_LO, "mlp_in_bias", fsums[...])


def column_call(dense, after_t, cotangent, counts):
    n = after_t.shape[1]
    feature = lambda r: pl.BlockSpec((r, COLUMN_BLOCK), lambda i: (0, i))
    token = pl.BlockSpec((COLUMN_BLOCK, D), lambda i: (i, 0))
    keep = lambda r: pltpu.VMEM((r, n), BF16)
    return call(
        column_kernel,
        (n // COLUMN_BLOCK,),
        [
            (dense, whole_block(dense.shape)),
            (after_t, feature(D)),
            (cotangent, token),
            (counts, feature(1)),
        ],
        [
            ((n, D), BF16, token),
            ((D, n), F32, feature(D)),
            ((D, n), BF16, feature(D)),
            (dense.shape, F32, whole_block(dense.shape)),
        ],
        [
            pltpu.VMEM((FF // LANES, D, LANES), F32),
            pltpu.VMEM((2, FF, LANES), F32),
            pltpu.VMEM((D, 3 * D), BF16),
            pltpu.VMEM((D, D), BF16),
            pltpu.VMEM((D, FF), BF16),
            pltpu.VMEM((FF, D), BF16),
            pltpu.VMEM((3 * D, D), BF16),
            pltpu.VMEM((D, D), BF16),
            pltpu.VMEM((FF, D), BF16),
            pltpu.VMEM((D, FF), BF16),
            pltpu.VMEM((D, LANES), F32),
            pltpu.VMEM((FF, LANES), F32),
            keep(D),
            keep(3 * D),
            keep(D),
            keep(D),
            keep(D),
            keep(FF),
            keep(FF),
            keep(D),
            pltpu.VMEM((6, D, LANES), F32),
            pltpu.VMEM((FF, LANES), F32),
            pltpu.VMEM((2, COLUMN_BLOCK // LANES, D, HEADS * LANES), BF16),
        ],
        "column",
        40 * D * D * n,
    )


def window_backward_kernel(me_ref, band_ref, *refs, order, shard_rows, space):
    fused = space > 0
    if fused:
        slots_ref, refs = refs[0], refs[1:]
    (
        grad_ref,
        weights_ref,
        vec,
        column_ref,
        shifted_ref,
        qkv_ref,
        mixed_ref,
        prob_ref,
        out_ref,
        keep_ref,
        send_ref,
        total,
        kept,
        wide,
        dense,
        mat,
        blocks,
        spread,
        normed_s,
        dqkv_s,
        mixed_s,
        grad_s,
        sums,
        sem,
    ) = refs
    step = pl.program_id(0)
    per_step = SLOT_BLOCK // LANES

    @pl.when(step == 0)
    def _():
        total[...] = jnp.zeros_like(total)
        sums[...] = jnp.zeros_like(sums)
        spread[...] = jnp.zeros_like(spread)

    cols = pl.ds(pl.multiple_of(step * SLOT_BLOCK, SLOT_BLOCK), SLOT_BLOCK)
    if fused:
        grad = to_slots(grad_ref[...], slots_ref[...])
    else:
        grad = grad_ref[...]
    grad_s[:, cols] = grad
    mixed_s[:, cols] = mixed_ref[...]
    dmixed = mm(weights_ref[:, 3 * D :], grad).astype(BF16)
    qkv = qkv_ref[...]
    blank = jnp.zeros((LANES - KEYS, HEADS * LANES), BF16)
    dq, dk, dv, dprobs, dscores = [], [], [], {}, {}
    for turn in range(per_step + 2):
        if turn < per_step:
            lanes = slice(turn * LANES, (turn + 1) * LANES)
            scatter_heads(spread.at[0, turn], qkv[:D, lanes])
            scatter_heads(spread.at[1, turn], dmixed[:, lanes])
            dprobs[turn] = mm(qkv[2 * D :, lanes].T[:KEYS], spread[1, turn])
        if 1 <= turn <= per_step:
            w = turn - 1
            heads = []
            for h in range(HEADS):
                prob = prob_ref[w, :, head_lanes(h)].astype(F32)
                dprob = dprobs[w][:, head_lanes(h)]
                heads.append(
                    (prob * (dprob - jnp.sum(prob * dprob, axis=0, keepdims=True))).astype(BF16)
                )
            dscores[w] = jnp.concatenate(heads, axis=1)
            kept[w] = dscores[w]
        if turn >= 2:
            w = turn - 2
            tall = jnp.concatenate([dscores[w], blank], axis=0)
            dq.append(blend(qkv[D : 2 * D, w * LANES : (w + 1) * LANES], tall) * SCALE)
            dk.append(gather_pairs(spread.at[0, w], tall) * SCALE)
            tall = jnp.concatenate([prob_ref[w], blank], axis=0)
            dv.append(gather_pairs(spread.at[1, w], tall))
    dqkv = jnp.concatenate([jnp.concatenate(d, axis=1) for d in (dq, dk, dv)], axis=0).astype(BF16)
    dqkv_s[:, cols] = dqkv

    def add(w, _):
        band = band_of(band_ref, step * per_step + w, me_ref, space, pl.num_programs(0))
        for h in range(HEADS):
            total[band, h] += kept[w, :, head_lanes(h)].astype(F32)
        return 0

    lax.fori_loop(0, per_step, add, 0)
    unit, scale = norm_parts(shifted_ref[...].astype(F32))
    normed_s[:, cols] = (unit * vec[:, 0:1] + vec[:, 1:2]).astype(BF16)
    dnormed = mm(weights_ref[:, : 3 * D], dqkv)
    out_ref[...] = norm_back(dnormed, unit, scale, vec[:, 0:1]).astype(BF16)
    for k, value in enumerate((dnormed * unit, dnormed, grad.astype(F32))):
        sums[k] += lane_fold(value)

    @pl.when(step == pl.num_programs(0) - 1)
    def _():
        wide[:WIDE, :] = jnp.zeros((WIDE, LANES), F32)
        wide[WIDE + BIAS_ROWS :, :] = jnp.zeros((wide.shape[0] - WIDE - BIAS_ROWS, LANES), F32)

        def turn(k, _):
            for h in range(HEADS):
                spot = pl.multiple_of(WIDE + (k * HEADS + h) * WIN, 8)
                wide[pl.ds(spot, WIN), :KEYS] = total[k, h].T[:WIN]
            return 0

        lax.fori_loop(0, LAT_BANDS, turn, 0)
        dense[:COL_LO, :] = jnp.zeros((COL_LO, LANES), F32)
        write_bias(wide, dense, 0)
        covered = BIAS_ROW + DENSE * PERIODS
        dense[covered:, :] = jnp.zeros((dense.shape[0] - covered, LANES), F32)
        both = column_ref[COL_HI - COL_LO - 16 :, :]
        rows = lax.broadcasted_iota(jnp.int32, both.shape, 0) + (COL_HI - 16)
        lane = lane_ids(16)
        start = rows * LANES + lane < OFFSET["earth_bias"]
        dense[COL_LO : COL_HI - 16, :] = column_ref[: COL_HI - COL_LO - 16, :]
        dense[COL_HI - 16 : COL_HI, :] = jnp.where(start, both, dense[COL_HI - 16 : COL_HI, :])
        split_into(mat, mt(normed_s[...], dqkv_s[...]))
        write_matrix(dense, 0, "qkv1", mat)
        split_into(mat, mt(mixed_s[...], grad_s[...]))
        write_matrix(dense, 0, "proj1", mat)
        for k, name in enumerate(("norm1_gain", "norm1_shift", "proj1_bias")):
            write_vector(dense, 0, name, sums[k])
        shards, rows = blocks.shape[0], shard_rows
        for shard in range(shards):
            spot = position(me_ref[0] ^ shard, order)
            blocks[spot, :rows, :] = dense[shard * rows : (shard + 1) * rows, :].astype(BF16)
        first = pltpu.make_async_copy(blocks.at[pl.ds(0, shards // 2)], keep_ref, sem.at[0])
        second = pltpu.make_async_copy(
            blocks.at[pl.ds(shards // 2, shards // 2)], send_ref, sem.at[1]
        )
        first.start()
        second.start()
        first.wait()
        second.wait()


def window_backward_call(
    me, bands, order, shards, rows, slots, grad, weights, vec, column_grad, shifted, qkv, mixed, prob, space
):
    fused = space > 0
    padded = padded_rows(rows)
    n = shifted.shape[1]
    per_step = SLOT_BLOCK // LANES
    slot_block = lambda r: pl.BlockSpec((r, SLOT_BLOCK), lambda i, *_: (0, i))
    ins = [(me, None), (bands, None)]
    if fused:
        ins += [(slots, slot_block(1)), (grad, whole_block(grad.shape))]
    else:
        ins += [(grad, slot_block(D))]
    ins += [
        (weights, whole_block(weights.shape)),
        (vec, whole_block(vec.shape)),
        (column_grad, whole_block(column_grad.shape)),
        (shifted, slot_block(D)),
        (qkv, slot_block(3 * D)),
        (mixed, slot_block(D)),
        (
            prob,
            pl.BlockSpec((per_step, KEYS, HEADS * LANES), lambda i, *_: (i, 0, 0)),
        ),
    ]
    flat_rows = max(shards * rows, BIAS_ROW + DENSE * PERIODS + 8)
    outs = [
        ((D, n), BF16, slot_block(D)),
        ((shards // 2, padded, LANES), BF16, pl.BlockSpec(memory_space=pl.ANY)),
        ((shards // 2, padded, LANES), BF16, pl.BlockSpec(memory_space=pl.ANY)),
    ]
    scratch = [
        pltpu.VMEM((LAT_BANDS, HEADS, KEYS, LANES), F32),
        pltpu.VMEM((per_step, KEYS, HEADS * LANES), BF16),
        pltpu.VMEM((WIDE * (PERIODS + 2), LANES), F32),
        pltpu.VMEM((flat_rows, LANES), F32),
        pltpu.VMEM((5, D, LANES), F32),
        pltpu.VMEM((shards, padded, LANES), BF16),
        pltpu.VMEM((2, per_step, D, HEADS * LANES), BF16),
        pltpu.VMEM((D, n), BF16),
        pltpu.VMEM((3 * D, n), BF16),
        pltpu.VMEM((D, n), BF16),
        pltpu.VMEM((D, n), BF16),
        pltpu.VMEM((3, D, LANES), F32),
        pltpu.SemaphoreType.DMA((2,)),
    ]
    kernel = functools.partial(
        window_backward_kernel, order=order, shard_rows=rows, space=space
    )
    return call(kernel, (n // SLOT_BLOCK,), ins, outs, scratch, "window_backward", 24 * D * D * n, scalars=2)


def finish_kernel(shift_ref, slots_ref, after_ref, out_ref):
    first = pl.program_id(0) * TOKEN_BLOCK
    back = from_slots(shift_ref[...], slots_ref[...], first, TOKEN_BLOCK)
    out_ref[...] = (after_ref[...] + back).T


def finish_call(grad_shifted, slots, after_t):
    n = after_t.shape[1]
    return call(
        finish_kernel,
        (n // TOKEN_BLOCK,),
        [
            (grad_shifted, whole_block(grad_shifted.shape)),
            (slots, whole_block(slots.shape)),
            (after_t, pl.BlockSpec((D, TOKEN_BLOCK), lambda i: (0, i))),
        ],
        [((n, D), F32, pl.BlockSpec((TOKEN_BLOCK, D), lambda i: (i, 0)))],
        [],
        "finish",
        D * n * slots.shape[1],
    )[0]


def body(block_input, cotangent, params, send_rows, window_band, level_count):
    model_width = block_input.shape[-1]
    rows_dev = block_input.shape[1] * block_input.shape[2]
    n_space, per_peer = send_rows.shape[1], send_rows.shape[3]
    devices = lax.axis_size(("dp", "space"))
    group = WIN // math.gcd(per_peer, WIN)
    if n_space % group:
        group = n_space
    fused = group == 1
    dest = n_space // group
    per_dest = group * per_peer // WIN
    member_groups = [[first + k for k in range(group)] for first in range(0, n_space, group)]
    place = lax.axis_index("space")
    index = lax.axis_index(("dp", "space"))
    me = index.astype(jnp.int32).reshape(1)
    bits = devices.bit_length() - 1
    order = [0] + list(range(bits - 1, 0, -1))

    def swap(value, *across):
        flip = sum(1 << bit for bit in across)
        return lax.ppermute(value, ("dp", "space"), [(k, k ^ flip) for k in range(devices)])

    def exchange(value):
        return lax.all_to_all(
            value, "space", split_axis=0, concat_axis=0, tiled=True, axis_index_groups=member_groups
        )

    def to_windows(rows):
        moved = exchange(rows[route_flat]).reshape(group, dest, per_peer, model_width)
        windows = moved.transpose(1, 0, 2, 3).reshape(-1, WIN, model_width)
        windows = jnp.pad(windows, ((0, 0), (0, LANES - WIN), (0, 0)))
        return windows.reshape(-1, model_width).T

    def from_windows(rows_t):
        rows = rows_t.T.reshape(-1, LANES, model_width)[:, :WIN]
        moved = rows.reshape(dest, group, per_peer, model_width).transpose(1, 0, 2, 3)
        rows = exchange(moved.reshape(rows_dev, model_width))
        return jnp.zeros((rows_dev, model_width), rows.dtype).at[route_flat].set(rows)

    flat_in = block_input[0].reshape(rows_dev, model_width)
    routes = send_rows[0, :, 0, :]
    route_flat = routes.reshape(-1)
    slots = jnp.pad(
        routes.reshape(-1, WIN), ((0, 0), (0, LANES - WIN)), constant_values=-1
    ).reshape(1, -1)
    if fused:
        bands = jnp.zeros((1, LANES), jnp.int32)
    else:
        all_bands = lax.all_gather(window_band[0], "space", axis=0)
        bands = lax.dynamic_slice(
            all_bands, ((place % group) * dest, (place // group) * per_dest), (dest, per_dest)
        ).reshape(1, -1)
        shifted = to_windows(flat_in)

    shard_rows = params.shape[0] // LANES
    padded = padded_rows(shard_rows)
    band_row = jnp.pad(window_band[0].astype(BF16), (0, LANES - window_band.shape[1]))
    held = jnp.concatenate(
        [
            params.astype(BF16).reshape(shard_rows, LANES),
            band_row.reshape(1, LANES),
            jnp.zeros((padded - shard_rows - 1, LANES), BF16),
        ],
        axis=0,
    ).reshape(1, padded, LANES)
    near, far = order[-1], order[-2]
    direct = [swap(held, near), swap(held, far), swap(held, near, far)]
    held = jnp.concatenate([held] + direct, axis=0)
    for bit in reversed(order[3:-2]):
        held = jnp.concatenate([held, swap(held, bit)], axis=0)
    top, next_top = order[1], order[2]
    cut = padded // 16 * 8
    upper, lower = held[:, :cut], held[:, cut:]
    upper = jnp.concatenate([upper, swap(upper, next_top)], axis=0)
    lower = jnp.concatenate([lower, swap(lower, top)], axis=0)
    if fused:
        upper, lower, slots = lax.optimization_barrier((upper, lower, slots))
        shifted = shift_call(flat_in, slots)
    parts = [upper, swap(upper, top), lower, swap(lower, next_top)]
    if fused:
        parts, shifted = lax.optimization_barrier((parts, shifted))
    parts = parts + [swap(part, order[0]) for part in parts]
    few = devices // 8
    plan = []
    for core in range(2):
        base = core * 4 * few
        plan += [(4 * core, 0, base, 2 * few, 0), (4 * core + 1, 0, base + 2 * few, 2 * few, 0)]
        for part, spot in ((2, 0), (3, few)):
            plan += [
                (4 * core + part, 0, base + spot, few, cut),
                (4 * core + part, few, base + spot + 2 * few, few, cut),
            ]
    space = n_space if fused else 0
    first, qkv, mixed, prob, weights, column_rows, vec, table = window_forward_call(
        me, bands, parts, plan, order, devices, shard_rows, shifted, flat_in, slots, space
    )
    if fused:
        bands = table
    if fused:
        after_t = first
    else:
        after_t = (flat_in.astype(F32) + from_windows(first).astype(F32)).T
    counts = jnp.repeat(level_count[0], LEVELS).reshape(1, -1)
    output, grad_after, grad_branch, column_grad = column_call(
        column_rows, after_t, cotangent[0].reshape(rows_dev, model_width), counts
    )
    if not fused:
        grad_branch = to_windows(grad_branch.T)
    grad_shifted, keep, send = window_backward_call(
        me, bands, order, devices, shard_rows, slots, grad_branch, weights, vec, column_grad,
        shifted, qkv, mixed, prob, space
    )
    total = keep.astype(F32) + swap(send, order[0]).astype(F32)
    total, grad_shifted = lax.optimization_barrier((total, grad_shifted))
    if fused:
        input_grad = finish_call(grad_shifted, slots, grad_after)
    else:
        input_grad = grad_after.T + from_windows(grad_shifted).astype(F32)

    def fold(kept, sent, *across):
        return kept + swap(sent.astype(BF16), *across).astype(F32)

    upper = total[:, :cut]
    lower = total[:, cut:].reshape(2, 2, few, padded - cut, LANES)
    upper = fold(upper[: 2 * few], upper[2 * few :], top)
    lower = fold(lower[:, 0], lower[:, 1], next_top)
    upper, lower, input_grad = lax.optimization_barrier((upper, lower, input_grad))
    upper = fold(upper[:few], upper[few:], next_top)
    lower = fold(lower[0], lower[1], top)
    total = jnp.concatenate([upper, lower], axis=1)
    for bit in order[3:-2]:
        half = total.shape[0] // 2
        total = fold(total[:half], total[half:], bit)
    own = total[0]
    for k, across in ((1, (near,)), (2, (far,)), (3, (near, far))):
        own = fold(own, total[k], *across)
    total = own[:shard_rows]
    return (
        output.reshape(block_input.shape),
        input_grad.reshape(block_input.shape),
        total.reshape(-1),
    )


def solution(mesh):
    return jax.shard_map(
        body,
        mesh=mesh,
        in_specs=(
            P("dp", "space", None, None),
            P("dp", "space", None, None),
            P(("dp", "space")),
            P("dp", None, "space", None),
            P("dp", "space"),
            P("dp", "space"),
        ),
        out_specs=(P("dp", "space", None, None), P("dp", "space", None, None), P(("dp", "space"))),
        check_vma=False,
    )
```

```python
import functools
import math

import jax
import jax.numpy as jnp
from jax import lax
from jax.experimental import pallas as pl
from jax.experimental.pallas import tpu as pltpu
from jax.sharding import PartitionSpec as P

D = 192
HEADS = 6
HEAD_DIM = 32
FF = 768
LEVELS = 8
WIN = 72
LAT_BANDS = 20
LANES = 128
HALF = LANES // 2
KEYS = 80
SCALE = HEAD_DIM ** (-0.5)
LOG2E = math.log2(math.e)
F32 = jnp.float32
BF16 = jnp.bfloat16

norm_eps = 1e-05


def param_layout():
    return [
        ("norm1_gain", (D,)),
        ("norm1_shift", (D,)),
        ("qkv1", (D, 3 * D)),
        ("proj1", (D, D)),
        ("proj1_bias", (D,)),
        ("norm2_gain", (D,)),
        ("norm2_shift", (D,)),
        ("qkv2", (D, 3 * D)),
        ("proj2", (D, D)),
        ("proj2_bias", (D,)),
        ("norm3_gain", (D,)),
        ("norm3_shift", (D,)),
        ("mlp_in", (D, FF)),
        ("mlp_in_bias", (FF,)),
        ("mlp_out", (FF, D)),
        ("mlp_out_bias", (D,)),
        ("earth_bias", (LAT_BANDS, HEADS, WIN, WIN)),
    ]


def param_offsets():
    offsets = {}
    filled = 0
    for entry_name, entry_shape in param_layout():
        offsets[entry_name] = filled
        filled += math.prod(entry_shape)
    return offsets


OFFSET = param_offsets()
BIAS_ROW, BIAS_LANE = divmod(OFFSET["earth_bias"], LANES)
BIAS_ROWS = LAT_BANDS * HEADS * WIN
WIDE = LANES // math.gcd(WIN, LANES)
DENSE = WIN // math.gcd(WIN, LANES)
PERIODS = -(-(BIAS_ROWS // WIDE + 1) // 8) * 8
COL_LO = (OFFSET["norm2_gain"] // LANES) // 8 * 8
COL_HI = -(-BIAS_ROW // 8) * 8 + 8
BIAS_LO = BIAS_ROW // 8 * 8


def mm(left, right):
    return lax.dot_general(left, right, (((1,), (0,)), ((), ())), preferred_element_type=F32)


def mt(left, right):
    return lax.dot_general(left, right, (((1,), (1,)), ((), ())), preferred_element_type=F32)


def lane_ids(rows):
    return lax.broadcasted_iota(jnp.int32, (rows, LANES), 1)


def rows_at(start, count, stride):
    return pl.ds(start, count) if stride == 1 else pl.ds(start, count, stride=stride)


def read_matrix(dense, first_row, name, matrix):
    rows, width = dict(param_layout())[name]
    halves = width // HALF
    step = 1 + halves % 2
    count, stride = rows // step, halves * step // 2
    low = lane_ids(count) < HALF
    for part in range(step):
        for chunk in range(-(-halves // 2)):
            unit = OFFSET[name] // HALF + part * halves + 2 * chunk
            row = unit // 2 - first_row
            value = dense[rows_at(row, count, stride), :]
            if unit % 2:
                after = dense[rows_at(row + 1, count, stride), :]
                value = pltpu.roll(jnp.where(low, after, value), HALF, 1)
            matrix[chunk, rows_at(part, count, step), :] = value


def write_matrix(dense, first_row, name, matrix):
    rows, width = dict(param_layout())[name]
    halves = width // HALF
    step = 1 + halves % 2
    count, stride = rows // step, halves * step // 2
    lane = lane_ids(count)
    for part in range(step):
        piece = 0
        while piece < halves:
            unit = OFFSET[name] // HALF + part * halves + piece
            where_to = rows_at(unit // 2 - first_row, count, stride)
            chunk = piece // 2
            value = matrix[chunk, rows_at(part, count, step), :]
            if unit % 2 == piece % 2 == 0 and piece + 1 < halves:
                dense[where_to, :] = value
                piece += 2
                continue
            if unit % 2 != piece % 2:
                value = pltpu.roll(value, HALF, 1)
            mine = lane < HALF if unit % 2 == 0 else lane >= HALF
            dense[where_to, :] = jnp.where(mine, value, dense[where_to, :])
            piece += 1


def joined(matrix, width):
    chunks = [matrix[k] for k in range(-(-width // LANES))]
    return jnp.concatenate(chunks, axis=1)[:, :width]


def split_into(matrix, value):
    width = value.shape[1]
    for k in range(-(-width // LANES)):
        end = min(width, (k + 1) * LANES)
        matrix[k, :, : end - k * LANES] = value[:, k * LANES : end]


def read_vector(dense, first_row, name):
    size = dict(param_layout())[name][0]
    unit = OFFSET[name] // HALF
    row = unit // 2 - first_row
    turned = dense[row : row + 8, :].T
    pieces = []
    for k in range(size // HALF):
        spot = unit % 2 + k
        pieces.append(turned[spot % 2 * HALF : (spot % 2 + 1) * HALF, spot // 2 : spot // 2 + 1])
    return jnp.concatenate(pieces, axis=0)


def write_vector(dense, first_row, name, sums):
    size = dict(param_layout())[name][0]
    line = jnp.sum(sums.T, axis=0, keepdims=True)
    lane = lane_ids(1)
    for k in range(size // HALF):
        unit = OFFSET[name] // HALF + k
        row = unit // 2 - first_row
        if size % LANES and k == size // HALF - 1:
            tail = line[:, k * HALF :]
            piece = jnp.concatenate([tail, tail], axis=1)
        else:
            piece = line[:, k // 2 * LANES : (k // 2 + 1) * LANES]
            if unit % 2 != k % 2:
                piece = pltpu.roll(piece, HALF, 1)
        mine = lane < HALF if unit % 2 == 0 else lane >= HALF
        dense[row : row + 1, :] = jnp.where(mine, piece, dense[row : row + 1, :])


def read_bias(dense, wide):
    lane = lane_ids(PERIODS)
    for j in range(WIDE):
        row, first = divmod(BIAS_LANE + j * WIN, LANES)
        value = dense[pl.ds(BIAS_ROW + row, PERIODS, stride=DENSE), :]
        if first + WIN > LANES:
            after = dense[pl.ds(BIAS_ROW + row + 1, PERIODS, stride=DENSE), :]
            value = jnp.where(lane < first, after, value)
        if first:
            value = pltpu.roll(value, LANES - first, 1)
        wide[pl.ds(j, PERIODS, stride=WIDE), :] = value


def write_bias(wide, dense, first_row):
    lane = lane_ids(PERIODS)
    for i in range(DENSE):
        begin = i * LANES - BIAS_LANE
        line = begin // WIN
        value = None
        while line * WIN < begin + LANES:
            shift = line * WIN - begin
            piece = wide[pl.ds(WIDE + line, PERIODS, stride=WIDE), :]
            if shift % LANES:
                piece = pltpu.roll(piece, shift % LANES, 1)
            value = piece if value is None else jnp.where(lane >= shift, piece, value)
            line += 1
        dense[pl.ds(BIAS_ROW - first_row + i, PERIODS, stride=DENSE), :] = value


def norm_parts(rows_in):
    mean = jnp.mean(rows_in, axis=0, keepdims=True)
    centered = rows_in - mean
    var = jnp.mean(centered * centered, axis=0, keepdims=True)
    scale = lax.rsqrt(var + norm_eps)
    return centered * scale, scale


def norm_back(grad, unit, scale, gain):
    scaled = grad * gain
    first = jnp.mean(scaled, axis=0, keepdims=True)
    second = jnp.mean(scaled * unit, axis=0, keepdims=True)
    return scale * (scaled - first - unit * second)


def lane_fold(value):
    total = value[:, :LANES]
    for k in range(1, value.shape[1] // LANES):
        total = total + value[:, k * LANES : (k + 1) * LANES]
    return total


def head_rows(h):
    return slice(h * HEAD_DIM, (h + 1) * HEAD_DIM)


def head_lanes(h):
    return slice(h * LANES, (h + 1) * LANES)


def interleave(parts):
    parts = list(parts)
    live, started = [], 0
    while live or started < len(parts):
        if started < len(parts):
            live.append(parts[started])
            started += 1
        live = [part for part in live if next(part, live) is None]


def own_column(full, bits):
    heads = []
    for h in range(HEADS):
        tiles = [full[k * LEVELS : (k + 1) * LEVELS, head_lanes(h)] for k in range(LANES // LEVELS)]
        for bit in bits:
            tiles = [jnp.where(bit, b, a) for a, b in zip(tiles[::2], tiles[1::2])]
        heads.append(tiles[0])
    return jnp.concatenate(heads, axis=1)


def all_columns(own, same):
    pair = jnp.concatenate([own, own], axis=0).astype(BF16)
    tall = jnp.concatenate([pair] * (LANES // (2 * LEVELS)), axis=0)
    return jnp.concatenate([tall[:, head_lanes(h)] * same for h in range(HEADS)], axis=1)


def blend(rows_in, weights):
    pieces = []
    for h in range(0, HEADS, 2):
        pair = slice(h * HEAD_DIM, (h + 2) * HEAD_DIM)
        both = mm(rows_in[pair], weights[:, h * LANES : (h + 2) * LANES])
        pieces += [both[:HEAD_DIM, :LANES], both[HEAD_DIM:, LANES:]]
    return jnp.concatenate(pieces, axis=0)


def gather_pairs(block, weights):
    pieces = []
    for h in range(0, HEADS, 2):
        lanes = slice(h * LANES, (h + 2) * LANES)
        pieces.append(mt(block[h * HEAD_DIM : (h + 2) * HEAD_DIM, lanes], weights[:, lanes]))
    return jnp.concatenate(pieces, axis=0)


def scatter_heads(block, rows_in):
    for h in range(HEADS):
        block[head_rows(h), head_lanes(h)] = rows_in[head_rows(h), :]


def chooser(first, slots):
    ids = lax.broadcasted_iota(jnp.int32, (PICK, slots.shape[1]), 0).astype(F32).astype(BF16)
    near = jnp.clip(slots - first, -1, PICK).astype(F32).astype(BF16)
    return jnp.where(ids == near, jnp.ones((), BF16), jnp.zeros((), BF16))


def spread_windows(rows_t):
    blank = jnp.zeros((rows_t.shape[0], LANES - WIN), rows_t.dtype)
    pieces = []
    for k in range(0, rows_t.shape[1], WIN):
        pieces += [rows_t[:, k : k + WIN], blank]
    return jnp.concatenate(pieces, axis=1)


def join_windows(rows_t):
    return jnp.concatenate(
        [rows_t[:, k : k + WIN] for k in range(0, rows_t.shape[1], LANES)], axis=1
    )


def to_slots(rows_t, slots):
    tokens = rows_t.shape[1]
    pick = jnp.concatenate([chooser(k, slots) for k in range(0, tokens, PICK)], axis=0)
    return spread_windows(mm(rows_t, pick)).astype(BF16)


def from_slots(slot_rows, slots, first, rows):
    return jnp.concatenate(
        [mt(slot_rows, chooser(first + k, slots)) for k in range(0, rows, PICK)], axis=1
    )


def call(kernel, grid, ins, outs, scratch, name, macs, limit, scalars=0):
    in_specs = [s for _, s in ins]
    spec = pltpu.PrefetchScalarGridSpec(
        num_scalar_prefetch=scalars,
        grid=grid,
        in_specs=in_specs[scalars:],
        out_specs=[s for _, _, s in outs],
        scratch_shapes=scratch,
    )
    return pl.pallas_call(
        kernel,
        grid_spec=spec,
        out_shape=[jax.ShapeDtypeStruct(shape, kind) for shape, kind, _ in outs],
        compiler_params=pltpu.CompilerParams(
            dimension_semantics=("arbitrary",) * len(grid), vmem_limit_bytes=limit << 20
        ),
        cost_estimate=pl.CostEstimate(
            flops=2 * macs,
            transcendentals=0,
            bytes_accessed=sum(a.size * a.dtype.itemsize for a, _ in ins)
            + sum(math.prod(shape) * jnp.dtype(kind).itemsize for shape, kind, _ in outs),
        ),
        name=name,
    )(*[a for a, _ in ins])


def padded_rows(rows):
    return -(-(rows + 1) // 8) * 8


def whole_block(shape):
    return pl.BlockSpec(shape, lambda *_: (0,) * len(shape))


SLOT_BLOCK = 2048
TIGHT_BLOCK = SLOT_BLOCK // LANES * WIN
TURNS = 12
RING = 4
PICK = 256
TOKEN_BLOCK = 768


def shift_kernel(x_ref, slots_ref, out_ref, x_t):
    @pl.when(pl.program_id(0) == 0)
    def _():
        x_t[...] = x_ref[...].astype(F32).T.astype(BF16)

    out_ref[...] = to_slots(x_t[...], slots_ref[...])


def shift_call(tokens, slots):
    count, n = tokens.shape[0], slots.shape[1] // WIN * LANES
    return call(
        shift_kernel,
        (n // SLOT_BLOCK,),
        [
            (tokens, whole_block(tokens.shape)),
            (slots, pl.BlockSpec((1, TIGHT_BLOCK), lambda i: (0, i))),
        ],
        [((D, n), BF16, pl.BlockSpec((D, SLOT_BLOCK), lambda i: (0, i)))],
        [pltpu.VMEM((D, count), BF16)],
        "shift",
        D * count * n,
        24,
    )[0]


def load_dense(me_ref, parts, plan, blocks, dense, sem, order, rows):
    copies = []
    for part, first, spot, count, row in plan:
        copies.append(
            pltpu.make_async_copy(
                parts[part].at[pl.ds(first, count)],
                blocks.at[pl.ds(spot, count), pl.ds(row, parts[part].shape[1])],
                sem,
            )
        )
    for copy in copies:
        copy.start()
    for copy in copies:
        copy.wait()
    shards = blocks.shape[0]
    for shard in range(shards):
        spot = position(me_ref[0] ^ shard, order)
        dense[shard * rows : (shard + 1) * rows, :] = blocks[spot, :rows, :].astype(F32)
    if dense.shape[0] > shards * rows:
        dense[shards * rows :, :] = jnp.zeros((dense.shape[0] - shards * rows, LANES), F32)


def position(relative, order):
    spot = 0
    for place, bit in enumerate(reversed(order)):
        spot = spot + ((relative >> bit) & 1) * (1 << place)
    return spot


def band_of(table, window, me_ref, space, steps):
    if not space:
        return table[0, window]
    each = steps * (SLOT_BLOCK // LANES) // space
    return table[window // each, me_ref[0] % space * each + window % each]


def window_forward_kernel(me_ref, band_ref, *refs, parts, plan, order, rows, steps, space):
    fused = space > 0
    ins = refs[:parts]
    refs = refs[parts:]
    if fused:
        shifted_ref, slots_ref, x_ref = refs[:3]
        refs = refs[3:]
    else:
        shifted_ref, refs = refs[0], refs[1:]
    (
        out_ref,
        qkv_ref,
        mixed_ref,
        prob_ref,
        weights_ref,
        column_ref,
        vec,
        table_ref,
        blocks,
        dense,
        wide,
        bias,
        mat,
        qkv_t,
        proj_t,
        spread,
        y_all,
        band_s,
        sem,
    ) = refs
    step = pl.program_id(0)

    @pl.when(step == 0)
    def _():
        load_dense(me_ref, ins, plan, blocks, dense, sem, order, rows)
        if fused:
            lines = []
            for source in range(space):
                shard = me_ref[0] // space * space + source
                tile = blocks[position(me_ref[0] ^ shard, order), rows // 8 * 8 : rows // 8 * 8 + 8, :]
                lines.append(tile.astype(F32)[rows % 8 : rows % 8 + 1])
            table_ref[...] = jnp.concatenate(lines, axis=0).astype(jnp.int32)
            copy = pltpu.make_async_copy(table_ref, band_s, sem)
            copy.start()
            copy.wait()
        column_ref[...] = dense[COL_LO:COL_HI, :]
        read_matrix(dense, 0, "qkv1", mat)
        weights_ref[:, : 3 * D] = joined(mat, 3 * D).astype(BF16)
        qkv_t[...] = joined(mat, 3 * D).T.astype(BF16)
        read_matrix(dense, 0, "proj1", mat)
        weights_ref[:, 3 * D :] = joined(mat, D).astype(BF16)
        proj_t[...] = joined(mat, D).T.astype(BF16)
        vec[:, 0:1] = read_vector(dense, 0, "norm1_gain")
        vec[:, 1:2] = read_vector(dense, 0, "norm1_shift")
        vec[:, 2:3] = read_vector(dense, 0, "proj1_bias")
        read_bias(dense, wide)
        wide[BIAS_ROWS:, :] = jnp.zeros((wide.shape[0] - BIAS_ROWS, LANES), F32)

        def turn(k, _):
            for j in range(TURNS):
                spot = pl.multiple_of((k * TURNS + j) * WIN, 8)
                bias[k * TURNS + j, :WIN, :] = wide[pl.ds(spot, LANES), :].T[:WIN].astype(BF16)
            return 0

        lax.fori_loop(0, LAT_BANDS * HEADS // TURNS, turn, 0)
        bias[:, WIN:, :] = jnp.full((LAT_BANDS * HEADS, KEYS - WIN, LANES), -jnp.inf, BF16)
        spread[...] = jnp.zeros_like(spread)

    @pl.when(step < steps)
    def _():
        per_step = SLOT_BLOCK // LANES
        unit, _ = norm_parts(shifted_ref[...].astype(F32))
        normed = (unit * vec[:, 0:1] + vec[:, 1:2]).astype(BF16)
        qkv = mm(qkv_t[...], normed).astype(BF16)
        qkv_ref[...] = qkv
        blank = jnp.zeros((LANES - KEYS, HEADS * LANES), BF16)
        scores, probs, mixed = {}, {}, []
        for turn in range(per_step + 2):
            if turn < per_step:
                lanes = slice(turn * LANES, (turn + 1) * LANES)
                scatter_heads(spread.at[turn % RING], qkv[:D, lanes])
                scores[turn] = mm(qkv[D : 2 * D, lanes].T[:KEYS], spread[turn % RING])
            if 1 <= turn <= per_step:
                w = turn - 1
                table = band_s if fused else band_ref
                band = band_of(table, step * per_step + w, me_ref, space, steps)
                heads = []
                for h in range(HEADS):
                    score = scores[w][:, head_lanes(h)] * SCALE + bias[band * HEADS + h].astype(F32)
                    grown = jnp.exp(score - jnp.max(score, axis=0, keepdims=True))
                    heads.append(
                        (grown * (1.0 / jnp.sum(grown, axis=0, keepdims=True))).astype(BF16)
                    )
                probs[w] = jnp.concatenate(heads, axis=1)
                prob_ref[w] = probs[w]
            if turn >= 2:
                w = turn - 2
                tall = jnp.concatenate([probs[w], blank], axis=0)
                mixed.append(blend(qkv[2 * D :, w * LANES : (w + 1) * LANES], tall))
        mixed = jnp.concatenate(mixed, axis=1).astype(BF16)
        mixed_ref[...] = mixed
        result = mm(proj_t[...], mixed) + vec[:, 2:3]
        if fused:
            spot = pl.ds(pl.multiple_of(step * TIGHT_BLOCK, TIGHT_BLOCK), TIGHT_BLOCK)
            y_all[:, spot] = join_windows(result).astype(BF16)
        else:
            out_ref[...] = result.astype(BF16)

    if fused:

        @pl.when(step >= steps)
        def _():
            branch = from_slots(
                y_all[...], slots_ref[...], (step - steps) * TOKEN_BLOCK, TOKEN_BLOCK
            )
            out_ref[...] = x_ref[...].astype(F32).T + branch


def window_forward_call(me, bands, parts, plan, order, shards, rows, shifted, tokens, slots, space):
    fused = space > 0
    n = shifted.shape[1]
    steps = n // SLOT_BLOCK
    per_step = SLOT_BLOCK // LANES
    padded = padded_rows(rows)
    flat_rows = max(shards * rows, BIAS_ROW + DENSE * PERIODS + 8)
    slot_block = lambda r: pl.BlockSpec((r, SLOT_BLOCK), lambda i, *_: (0, jnp.minimum(i, steps - 1)))
    ins = [(me, None), (bands, None)]
    ins += [(p, pl.BlockSpec(memory_space=pl.ANY)) for p in parts]
    ins += [(shifted, slot_block(D))]
    if fused:
        count = tokens.shape[0]
        late = lambda i: jnp.maximum(i - steps, 0)
        ins += [
            (slots, whole_block(slots.shape)),
            (tokens, pl.BlockSpec((TOKEN_BLOCK, D), lambda i, *_: (late(i), 0))),
        ]
        first = ((D, count), F32, pl.BlockSpec((D, TOKEN_BLOCK), lambda i, *_: (0, late(i))))
        grid = steps + count // TOKEN_BLOCK
    else:
        first = ((D, n), BF16, slot_block(D))
        grid = steps
    outs = [
        first,
        ((3 * D, n), BF16, slot_block(3 * D)),
        ((D, n), BF16, slot_block(D)),
        (
            (n // LANES, KEYS, HEADS * LANES),
            BF16,
            pl.BlockSpec(
                (per_step, KEYS, HEADS * LANES), lambda i, *_: (jnp.minimum(i, steps - 1), 0, 0)
            ),
        ),
        ((D, 4 * D), BF16, whole_block((D, 4 * D))),
        ((COL_HI - COL_LO, LANES), F32, whole_block((COL_HI - COL_LO, LANES))),
        ((D, LANES), F32, whole_block((D, LANES))),
        ((max(space, 1), LANES), jnp.int32, whole_block((max(space, 1), LANES))),
    ]
    scratch = [
        pltpu.VMEM((shards, padded, LANES), BF16),
        pltpu.VMEM((flat_rows, LANES), F32),
        pltpu.VMEM((WIDE * PERIODS + LANES, LANES), F32),
        pltpu.VMEM((LAT_BANDS * HEADS, KEYS, LANES), BF16),
        pltpu.VMEM((5, D, LANES), F32),
        pltpu.VMEM((3 * D, D), BF16),
        pltpu.VMEM((D, D), BF16),
        pltpu.VMEM((RING, D, HEADS * LANES), BF16),
        pltpu.VMEM((D, n // LANES * WIN), BF16),
        pltpu.SMEM((max(space, 1), LANES), jnp.int32),
        pltpu.SemaphoreType.DMA,
    ]
    kernel = functools.partial(
        window_forward_kernel,
        parts=len(parts),
        plan=plan,
        order=order,
        rows=rows,
        steps=steps,
        space=space,
    )
    return call(kernel, (grid,), ins, outs, scratch, "window_forward", 12 * D * D * n, 40, scalars=2)


COLUMN_BLOCK = 768
COLUMN_PART = 768
COLUMN_VECTORS = (
    "norm2_gain",
    "norm2_shift",
    "proj2_bias",
    "norm3_gain",
    "norm3_shift",
    "mlp_out_bias",
)
COLUMN_MATRICES = ("qkv2", "proj2", "mlp_in", "mlp_out")


def column_kernel(
    dense,
    x_ref,
    cot_ref,
    count_ref,
    out_ref,
    after_ref,
    branch_ref,
    grad_ref,
    mat,
    tall,
    w_qkv,
    w_proj,
    w_in,
    w_out,
    t_qkv,
    t_proj,
    t_in,
    t_out,
    vec,
    fvec,
    grad_qkv,
    grad_proj,
    grad_in,
    grad_out,
    sums,
    fsums,
    spread,
):
    step = pl.program_id(0)

    @pl.when(step == 0)
    def _():
        for name, plain, turned in (
            ("qkv2", w_qkv, t_qkv),
            ("proj2", w_proj, t_proj),
            ("mlp_in", w_in, t_in),
            ("mlp_out", w_out, t_out),
        ):
            rows, width = plain.shape
            source = tall if rows == FF else mat
            read_matrix(dense, COL_LO, name, source)
            plain[...] = joined(source, width).astype(BF16)
            turned[...] = joined(source, width).T.astype(BF16)
        for k, name in enumerate(COLUMN_VECTORS):
            vec[:, k : k + 1] = read_vector(dense, COL_LO, name)
        fvec[:, 0:1] = read_vector(dense, COL_LO, "mlp_in_bias")
        sums[...] = jnp.zeros_like(sums)
        fsums[...] = jnp.zeros_like(fsums)
        for grad in (grad_qkv, grad_proj, grad_in, grad_out):
            grad[...] = jnp.zeros_like(grad)
        spread[...] = jnp.zeros_like(spread)

    gain2, shift2, bias2, gain3, shift3, bias_out = [vec[:, k : k + 1] for k in range(6)]
    key_id = lax.broadcasted_iota(jnp.int32, (LANES, LANES), 0)
    query_id = lax.broadcasted_iota(jnp.int32, (LANES, LANES), 1)
    same = jnp.where(key_id // LEVELS == query_id // LEVELS, 1.0, 0.0).astype(BF16)
    column = lax.broadcasted_iota(jnp.int32, (LEVELS, LANES), 1) // LEVELS
    bits = [(column >> k) & 1 == 1 for k in range(4)]
    level = lax.broadcasted_iota(jnp.int32, (LEVELS, LANES), 0)
    groups = COLUMN_PART // LANES

    def part_steps(part):
        here = slice(part * COLUMN_PART, (part + 1) * COLUMN_PART)
        x = x_ref[:, here]
        unit2, scale2 = norm_parts(x)
        n2 = (unit2 * gain2 + shift2).astype(BF16)
        yield
        qkv = mm(t_qkv[...], n2).astype(BF16)
        yield
        scores = []
        for g in range(groups):
            lanes = slice(g * LANES, (g + 1) * LANES)
            scatter_heads(spread.at[0, part * groups + g], qkv[:D, lanes])
            scores.append(own_column(mm(qkv[D : 2 * D, lanes].T, spread[0, part * groups + g]), bits))
        yield
        probs, tall_probs = [], []
        for g in range(groups):
            begin = part * COLUMN_PART + g * LANES
            valid = level < count_ref[:, begin : begin + LANES]
            score = jnp.where(jnp.concatenate([valid] * HEADS, axis=1), scores[g] * SCALE, -jnp.inf)
            grown = jnp.exp(score - jnp.max(score, axis=0, keepdims=True))
            prob = grown * (1.0 / jnp.sum(grown, axis=0, keepdims=True))
            probs.append(prob)
            tall_probs.append(all_columns(prob, same))
        yield
        mixed = [
            blend(qkv[2 * D :, g * LANES : (g + 1) * LANES], tall_probs[g]) for g in range(groups)
        ]
        mixed = jnp.concatenate(mixed, axis=1).astype(BF16)
        projected = mm(t_proj[...], mixed)
        yield
        middle = x + (projected + bias2)
        unit3, scale3 = norm_parts(middle)
        n3 = (unit3 * gain3 + shift3).astype(BF16)
        yield
        pre = mm(t_in[...], n3)
        cot = cot_ref[here, :].astype(F32).T
        cot_bf = cot.astype(BF16)
        dact = mm(w_out[...], cot_bf)
        yield
        pre = pre + fvec[:, 0:1]
        root = math.sqrt(2.0 / math.pi)
        square = pre * pre
        share = 0.5 + 0.5 * jnp.tanh(pre * (root + (root * 0.044715) * square))
        act = pre * share
        slope = share + act * (1.0 - share) * (2.0 * root + (6.0 * root * 0.044715) * square)
        act = act.astype(BF16)
        dpre = (dact * slope).astype(BF16)
        yield
        output = middle + (mm(t_out[...], act) + bias_out)
        out_ref[here, :] = output.T.astype(BF16)
        dn3 = mm(w_in[...], dpre)
        grad_out[...] += mt(act, cot_bf)
        grad_in[...] += mt(n3, dpre)
        yield
        dmiddle = cot + norm_back(dn3, unit3, scale3, gain3)
        dattn = dmiddle.astype(BF16)
        sums[2] += lane_fold(dattn.astype(F32))
        sums[3] += lane_fold(dn3 * unit3)
        sums[4] += lane_fold(dn3)
        sums[5] += lane_fold(cot_bf.astype(F32))
        fsums[...] += lane_fold(dpre.astype(F32))
        yield
        dmixed = mm(w_proj[...], dattn).astype(BF16)
        grad_proj[...] += mt(mixed, dattn)
        dprobs = []
        for g in range(groups):
            lanes = slice(g * LANES, (g + 1) * LANES)
            scatter_heads(spread.at[1, part * groups + g], dmixed[:, lanes])
            dprobs.append(own_column(mm(qkv[2 * D :, lanes].T, spread[1, part * groups + g]), bits))
        yield
        dscores = []
        for prob, dprob in zip(probs, dprobs):
            dscore = prob * (dprob - jnp.sum(prob * dprob, axis=0, keepdims=True))
            dscores.append(all_columns(dscore, same))
        yield
        dq, dk, dv = [], [], []
        for g in range(groups):
            dq.append(blend(qkv[D : 2 * D, g * LANES : (g + 1) * LANES], dscores[g]) * SCALE)
            dk.append(gather_pairs(spread.at[0, part * groups + g], dscores[g]) * SCALE)
            dv.append(gather_pairs(spread.at[1, part * groups + g], tall_probs[g]))
        dqkv = [jnp.concatenate(d, axis=1) for d in (dq, dk, dv)]
        dqkv = jnp.concatenate(dqkv, axis=0).astype(BF16)
        dn2 = mm(w_qkv[...], dqkv)
        grad_qkv[...] += mt(n2, dqkv)
        yield
        dafter = dmiddle + norm_back(dn2, unit2, scale2, gain2)
        after_ref[:, here] = dafter
        branch_ref[:, here] = dafter.astype(BF16)
        sums[0] += lane_fold(dn2 * unit2)
        sums[1] += lane_fold(dn2)

    interleave([part_steps(part) for part in range(COLUMN_BLOCK // COLUMN_PART)])

    @pl.when(step == pl.num_programs(0) - 1)
    def _():
        grad_ref[...] = jnp.zeros_like(grad_ref)
        split_into(mat, grad_qkv[...])
        write_matrix(grad_ref, COL_LO, "qkv2", mat)
        split_into(mat, grad_proj[...])
        write_matrix(grad_ref, COL_LO, "proj2", mat)
        split_into(mat, grad_in[...])
        write_matrix(grad_ref, COL_LO, "mlp_in", mat)
        split_into(tall, grad_out[...])
        write_matrix(grad_ref, COL_LO, "mlp_out", tall)
        for k, name in enumerate(COLUMN_VECTORS):
            write_vector(grad_ref, COL_LO, name, sums[k])
        write_vector(grad_ref, COL_LO, "mlp_in_bias", fsums[...])


def column_call(dense, after_t, cotangent, counts):
    n = after_t.shape[1]
    feature = lambda r: pl.BlockSpec((r, COLUMN_BLOCK), lambda i: (0, i))
    token = pl.BlockSpec((COLUMN_BLOCK, D), lambda i: (i, 0))
    return call(
        column_kernel,
        (n // COLUMN_BLOCK,),
        [
            (dense, whole_block(dense.shape)),
            (after_t, feature(D)),
            (cotangent, token),
            (counts, feature(1)),
        ],
        [
            ((n, D), BF16, token),
            ((D, n), F32, feature(D)),
            ((D, n), BF16, feature(D)),
            (dense.shape, F32, whole_block(dense.shape)),
        ],
        [
            pltpu.VMEM((FF // LANES, D, LANES), F32),
            pltpu.VMEM((2, FF, LANES), F32),
            pltpu.VMEM((D, 3 * D), BF16),
            pltpu.VMEM((D, D), BF16),
            pltpu.VMEM((D, FF), BF16),
            pltpu.VMEM((FF, D), BF16),
            pltpu.VMEM((3 * D, D), BF16),
            pltpu.VMEM((D, D), BF16),
            pltpu.VMEM((FF, D), BF16),
            pltpu.VMEM((D, FF), BF16),
            pltpu.VMEM((D, LANES), F32),
            pltpu.VMEM((FF, LANES), F32),
            pltpu.VMEM((D, 3 * D), F32),
            pltpu.VMEM((D, D), F32),
            pltpu.VMEM((D, FF), F32),
            pltpu.VMEM((FF, D), F32),
            pltpu.VMEM((6, D, LANES), F32),
            pltpu.VMEM((FF, LANES), F32),
            pltpu.VMEM((2, COLUMN_BLOCK // LANES, D, HEADS * LANES), BF16),
        ],
        "column",
        40 * D * D * n,
        44,
    )


def window_backward_kernel(me_ref, band_ref, *refs, order, shard_rows, space):
    fused = space > 0
    if fused:
        slots_ref, refs = refs[0], refs[1:]
    (
        grad_ref,
        weights_ref,
        vec,
        column_ref,
        shifted_ref,
        qkv_ref,
        mixed_ref,
        prob_ref,
        out_ref,
        keep_ref,
        send_ref,
        total,
        kept,
        wide,
        dense,
        mat,
        blocks,
        spread,
        grad_qkv,
        grad_proj,
        sums,
        sem,
    ) = refs
    step = pl.program_id(0)
    per_step = SLOT_BLOCK // LANES

    @pl.when(step == 0)
    def _():
        total[...] = jnp.zeros_like(total)
        sums[...] = jnp.zeros_like(sums)
        grad_qkv[...] = jnp.zeros_like(grad_qkv)
        grad_proj[...] = jnp.zeros_like(grad_proj)
        spread[...] = jnp.zeros_like(spread)

    if fused:
        grad = to_slots(grad_ref[...], slots_ref[...])
    else:
        grad = grad_ref[...]
    grad_proj[...] += mt(mixed_ref[...], grad)
    dmixed = mm(weights_ref[:, 3 * D :], grad).astype(BF16)
    qkv = qkv_ref[...]
    blank = jnp.zeros((LANES - KEYS, HEADS * LANES), BF16)
    dq, dk, dv, dprobs, dscores = [], [], [], {}, {}
    for turn in range(per_step + 2):
        if turn < per_step:
            lanes = slice(turn * LANES, (turn + 1) * LANES)
            scatter_heads(spread.at[0, turn % RING], qkv[:D, lanes])
            scatter_heads(spread.at[1, turn % RING], dmixed[:, lanes])
            dprobs[turn] = mm(qkv[2 * D :, lanes].T[:KEYS], spread[1, turn % RING])
        if 1 <= turn <= per_step:
            w = turn - 1
            heads = []
            for h in range(HEADS):
                prob = prob_ref[w, :, head_lanes(h)].astype(F32)
                dprob = dprobs[w][:, head_lanes(h)]
                heads.append(
                    (prob * (dprob - jnp.sum(prob * dprob, axis=0, keepdims=True))).astype(BF16)
                )
            dscores[w] = jnp.concatenate(heads, axis=1)
            kept[w] = dscores[w]
        if turn >= 2:
            w = turn - 2
            tall = jnp.concatenate([dscores[w], blank], axis=0)
            dq.append(blend(qkv[D : 2 * D, w * LANES : (w + 1) * LANES], tall) * SCALE)
            dk.append(gather_pairs(spread.at[0, w % RING], tall) * SCALE)
            tall = jnp.concatenate([prob_ref[w], blank], axis=0)
            dv.append(gather_pairs(spread.at[1, w % RING], tall))
    dqkv = jnp.concatenate([jnp.concatenate(d, axis=1) for d in (dq, dk, dv)], axis=0).astype(BF16)

    def add(w, _):
        band = band_of(band_ref, step * per_step + w, me_ref, space, pl.num_programs(0))
        for h in range(HEADS):
            total[band, h] += kept[w, :, head_lanes(h)].astype(F32)
        return 0

    lax.fori_loop(0, per_step, add, 0)
    unit, scale = norm_parts(shifted_ref[...].astype(F32))
    grad_qkv[...] += mt((unit * vec[:, 0:1] + vec[:, 1:2]).astype(BF16), dqkv)
    dnormed = mm(weights_ref[:, : 3 * D], dqkv)
    dshifted = norm_back(dnormed, unit, scale, vec[:, 0:1])
    out_ref[...] = (join_windows(dshifted) if fused else dshifted).astype(BF16)
    for k, value in enumerate((dnormed * unit, dnormed, grad.astype(F32))):
        sums[k] += lane_fold(value)

    @pl.when(step == pl.num_programs(0) - 1)
    def _():
        wide[:WIDE, :] = jnp.zeros((WIDE, LANES), F32)
        wide[WIDE + BIAS_ROWS :, :] = jnp.zeros((wide.shape[0] - WIDE - BIAS_ROWS, LANES), F32)

        def turn(k, _):
            for j in range(2):
                for h in range(HEADS):
                    spot = pl.multiple_of(WIDE + ((2 * k + j) * HEADS + h) * WIN, 8)
                    wide[pl.ds(spot, WIN), :KEYS] = total[2 * k + j, h].T[:WIN]
            return 0

        lax.fori_loop(0, LAT_BANDS // 2, turn, 0)
        dense[:COL_LO, :] = jnp.zeros((COL_LO, LANES), F32)
        write_bias(wide, dense, 0)
        covered = BIAS_ROW + DENSE * PERIODS
        dense[covered:, :] = jnp.zeros((dense.shape[0] - covered, LANES), F32)
        both = column_ref[COL_HI - COL_LO - 16 :, :]
        rows = lax.broadcasted_iota(jnp.int32, both.shape, 0) + (COL_HI - 16)
        lane = lane_ids(16)
        start = rows * LANES + lane < OFFSET["earth_bias"]
        dense[COL_LO : COL_HI - 16, :] = column_ref[: COL_HI - COL_LO - 16, :]
        dense[COL_HI - 16 : COL_HI, :] = jnp.where(start, both, dense[COL_HI - 16 : COL_HI, :])
        split_into(mat, grad_qkv[...])
        write_matrix(dense, 0, "qkv1", mat)
        split_into(mat, grad_proj[...])
        write_matrix(dense, 0, "proj1", mat)
        for k, name in enumerate(("norm1_gain", "norm1_shift", "proj1_bias")):
            write_vector(dense, 0, name, sums[k])
        shards, rows = blocks.shape[0], shard_rows
        for shard in range(shards):
            spot = position(me_ref[0] ^ shard, order)
            blocks[spot, :rows, :] = dense[shard * rows : (shard + 1) * rows, :].astype(BF16)
        first = pltpu.make_async_copy(blocks.at[pl.ds(0, shards // 2)], keep_ref, sem.at[0])
        second = pltpu.make_async_copy(
            blocks.at[pl.ds(shards // 2, shards // 2)], send_ref, sem.at[1]
        )
        first.start()
        second.start()
        first.wait()
        second.wait()


def window_backward_call(
    me, bands, order, shards, rows, slots, grad, weights, vec, column_grad, shifted, qkv, mixed, prob, space
):
    fused = space > 0
    padded = padded_rows(rows)
    n = shifted.shape[1]
    per_step = SLOT_BLOCK // LANES
    slot_block = lambda r: pl.BlockSpec((r, SLOT_BLOCK), lambda i, *_: (0, i))
    ins = [(me, None), (bands, None)]
    if fused:
        tight = pl.BlockSpec((1, TIGHT_BLOCK), lambda i, *_: (0, i))
        ins += [(slots, tight), (grad, whole_block(grad.shape))]
    else:
        ins += [(grad, slot_block(D))]
    ins += [
        (weights, whole_block(weights.shape)),
        (vec, whole_block(vec.shape)),
        (column_grad, whole_block(column_grad.shape)),
        (shifted, slot_block(D)),
        (qkv, slot_block(3 * D)),
        (mixed, slot_block(D)),
        (
            prob,
            pl.BlockSpec((per_step, KEYS, HEADS * LANES), lambda i, *_: (i, 0, 0)),
        ),
    ]
    flat_rows = max(shards * rows, BIAS_ROW + DENSE * PERIODS + 8)
    if fused:
        tight = pl.BlockSpec((D, TIGHT_BLOCK), lambda i, *_: (0, i))
        first = ((D, n // LANES * WIN), BF16, tight)
    else:
        first = ((D, n), BF16, slot_block(D))
    outs = [
        first,
        ((shards // 2, padded, LANES), BF16, pl.BlockSpec(memory_space=pl.ANY)),
        ((shards // 2, padded, LANES), BF16, pl.BlockSpec(memory_space=pl.ANY)),
    ]
    scratch = [
        pltpu.VMEM((LAT_BANDS, HEADS, KEYS, LANES), F32),
        pltpu.VMEM((per_step, KEYS, HEADS * LANES), BF16),
        pltpu.VMEM((WIDE * (PERIODS + 2), LANES), F32),
        pltpu.VMEM((flat_rows, LANES), F32),
        pltpu.VMEM((5, D, LANES), F32),
        pltpu.VMEM((shards, padded, LANES), BF16),
        pltpu.VMEM((2, RING, D, HEADS * LANES), BF16),
        pltpu.VMEM((D, 3 * D), F32),
        pltpu.VMEM((D, D), F32),
        pltpu.VMEM((3, D, LANES), F32),
        pltpu.SemaphoreType.DMA((2,)),
    ]
    kernel = functools.partial(
        window_backward_kernel, order=order, shard_rows=rows, space=space
    )
    return call(kernel, (n // SLOT_BLOCK,), ins, outs, scratch, "window_backward", 24 * D * D * n, 48, scalars=2)


def finish_kernel(shift_ref, slots_ref, after_ref, out_ref):
    first = pl.program_id(0) * TOKEN_BLOCK
    back = from_slots(shift_ref[...], slots_ref[...], first, TOKEN_BLOCK)
    out_ref[...] = (after_ref[...] + back).T


def finish_call(grad_shifted, slots, after_t):
    n = after_t.shape[1]
    return call(
        finish_kernel,
        (n // TOKEN_BLOCK,),
        [
            (grad_shifted, whole_block(grad_shifted.shape)),
            (slots, whole_block(slots.shape)),
            (after_t, pl.BlockSpec((D, TOKEN_BLOCK), lambda i: (0, i))),
        ],
        [((n, D), F32, pl.BlockSpec((TOKEN_BLOCK, D), lambda i: (i, 0)))],
        [],
        "finish",
        D * n * slots.shape[1],
        24,
    )[0]


def body(block_input, cotangent, params, send_rows, window_band, level_count):
    model_width = block_input.shape[-1]
    rows_dev = block_input.shape[1] * block_input.shape[2]
    n_space, per_peer = send_rows.shape[1], send_rows.shape[3]
    devices = lax.axis_size(("dp", "space"))
    group = WIN // math.gcd(per_peer, WIN)
    if n_space % group:
        group = n_space
    fused = group == 1
    dest = n_space // group
    per_dest = group * per_peer // WIN
    member_groups = [[first + k for k in range(group)] for first in range(0, n_space, group)]
    place = lax.axis_index("space")
    index = lax.axis_index(("dp", "space"))
    me = index.astype(jnp.int32).reshape(1)
    bits = devices.bit_length() - 1
    order = [0] + list(range(bits - 1, 0, -1))

    def swap(value, *across):
        flip = sum(1 << bit for bit in across)
        return lax.ppermute(value, ("dp", "space"), [(k, k ^ flip) for k in range(devices)])

    def exchange(value):
        return lax.all_to_all(
            value, "space", split_axis=0, concat_axis=0, tiled=True, axis_index_groups=member_groups
        )

    def to_windows(rows):
        moved = exchange(rows[route_flat]).reshape(group, dest, per_peer, model_width)
        windows = moved.transpose(1, 0, 2, 3).reshape(-1, WIN, model_width)
        windows = jnp.pad(windows, ((0, 0), (0, LANES - WIN), (0, 0)))
        return windows.reshape(-1, model_width).T

    def from_windows(rows_t):
        rows = rows_t.T.reshape(-1, LANES, model_width)[:, :WIN]
        moved = rows.reshape(dest, group, per_peer, model_width).transpose(1, 0, 2, 3)
        rows = exchange(moved.reshape(rows_dev, model_width))
        return jnp.zeros((rows_dev, model_width), rows.dtype).at[route_flat].set(rows)

    flat_in = block_input[0].reshape(rows_dev, model_width)
    routes = send_rows[0, :, 0, :]
    route_flat = routes.reshape(-1)
    slots = routes.reshape(1, -1)
    if fused:
        bands = jnp.zeros((1, LANES), jnp.int32)
    else:
        all_bands = lax.all_gather(window_band[0], "space", axis=0)
        bands = lax.dynamic_slice(
            all_bands, ((place % group) * dest, (place // group) * per_dest), (dest, per_dest)
        ).reshape(1, -1)
        shifted = to_windows(flat_in)

    shard_rows = params.shape[0] // LANES
    padded = padded_rows(shard_rows)
    band_row = jnp.pad(window_band[0].astype(BF16), (0, LANES - window_band.shape[1]))
    held = jnp.concatenate(
        [
            params.astype(BF16).reshape(shard_rows, LANES),
            band_row.reshape(1, LANES),
            jnp.zeros((padded - shard_rows - 1, LANES), BF16),
        ],
        axis=0,
    ).reshape(1, padded, LANES)
    near, far = order[-1], order[-2]
    direct = [swap(held, near), swap(held, far), swap(held, near, far)]
    held = jnp.concatenate([held] + direct, axis=0)
    for bit in reversed(order[3:-2]):
        held = jnp.concatenate([held, swap(held, bit)], axis=0)
    top, next_top = order[1], order[2]
    cut = padded // 16 * 8
    upper, lower = held[:, :cut], held[:, cut:]
    upper = jnp.concatenate([upper, swap(upper, next_top)], axis=0)
    lower = jnp.concatenate([lower, swap(lower, top)], axis=0)
    if fused:
        upper, lower, slots = lax.optimization_barrier((upper, lower, slots))
        shifted = shift_call(flat_in, slots)
    parts = [upper, swap(upper, top), lower, swap(lower, next_top)]
    if fused:
        parts, shifted = lax.optimization_barrier((parts, shifted))
    parts = parts + [swap(part, order[0]) for part in parts]
    few = devices // 8
    plan = []
    for core in range(2):
        base = core * 4 * few
        plan += [(4 * core, 0, base, 2 * few, 0), (4 * core + 1, 0, base + 2 * few, 2 * few, 0)]
        for part, spot in ((2, 0), (3, few)):
            plan += [
                (4 * core + part, 0, base + spot, few, cut),
                (4 * core + part, few, base + spot + 2 * few, few, cut),
            ]
    space = n_space if fused else 0
    first, qkv, mixed, prob, weights, column_rows, vec, table = window_forward_call(
        me, bands, parts, plan, order, devices, shard_rows, shifted, flat_in, slots, space
    )
    if fused:
        bands = table
    if fused:
        after_t = first
    else:
        after_t = (flat_in.astype(F32) + from_windows(first).astype(F32)).T
    counts = jnp.repeat(level_count[0], LEVELS).reshape(1, -1)
    output, grad_after, grad_branch, column_grad = column_call(
        column_rows, after_t, cotangent[0].reshape(rows_dev, model_width), counts
    )
    if not fused:
        grad_branch = to_windows(grad_branch.T)
    grad_shifted, keep, send = window_backward_call(
        me, bands, order, devices, shard_rows, slots, grad_branch, weights, vec, column_grad,
        shifted, qkv, mixed, prob, space
    )
    total = keep.astype(F32) + swap(send, order[0]).astype(F32)
    total, grad_shifted = lax.optimization_barrier((total, grad_shifted))
    if fused:
        input_grad = finish_call(grad_shifted, slots, grad_after)
    else:
        input_grad = grad_after.T + from_windows(grad_shifted).astype(F32)

    def fold(kept, sent, *across):
        return kept + swap(sent.astype(BF16), *across).astype(F32)

    upper = total[:, :cut]
    lower = total[:, cut:].reshape(2, 2, few, padded - cut, LANES)
    upper = fold(upper[: 2 * few], upper[2 * few :], top)
    lower = fold(lower[:, 0], lower[:, 1], next_top)
    upper, lower, input_grad = lax.optimization_barrier((upper, lower, input_grad))
    upper = fold(upper[:few], upper[few:], next_top)
    lower = fold(lower[0], lower[1], top)
    total = jnp.concatenate([upper, lower], axis=1)
    for bit in order[3:-2]:
        half = total.shape[0] // 2
        total = fold(total[:half], total[half:], bit)
    own = total[0]
    for k, across in ((1, (near,)), (2, (far,)), (3, (near, far))):
        own = fold(own, total[k], *across)
    total = own[:shard_rows]
    return (
        output.reshape(block_input.shape),
        input_grad.reshape(block_input.shape),
        total.reshape(-1),
    )


def solution(mesh):
    return jax.shard_map(
        body,
        mesh=mesh,
        in_specs=(
            P("dp", "space", None, None),
            P("dp", "space", None, None),
            P(("dp", "space")),
            P("dp", None, "space", None),
            P("dp", "space"),
            P("dp", "space"),
        ),
        out_specs=(P("dp", "space", None, None), P("dp", "space", None, None), P(("dp", "space"))),
        check_vma=False,
    )
```

```python
import functools
import math

import jax
import jax.numpy as jnp
from jax import lax
from jax.experimental import pallas as pl
from jax.experimental.pallas import tpu as pltpu
from jax.sharding import PartitionSpec as P

D = 192
HEADS = 6
HEAD_DIM = 32
FF = 768
LEVELS = 8
WIN = 72
LAT_BANDS = 20
LANES = 128
HALF = LANES // 2
KEYS = 80
SCALE = HEAD_DIM ** (-0.5)
LOG2E = math.log2(math.e)
F32 = jnp.float32
BF16 = jnp.bfloat16

norm_eps = 1e-05


def param_layout():
    return [
        ("norm1_gain", (D,)),
        ("norm1_shift", (D,)),
        ("qkv1", (D, 3 * D)),
        ("proj1", (D, D)),
        ("proj1_bias", (D,)),
        ("norm2_gain", (D,)),
        ("norm2_shift", (D,)),
        ("qkv2", (D, 3 * D)),
        ("proj2", (D, D)),
        ("proj2_bias", (D,)),
        ("norm3_gain", (D,)),
        ("norm3_shift", (D,)),
        ("mlp_in", (D, FF)),
        ("mlp_in_bias", (FF,)),
        ("mlp_out", (FF, D)),
        ("mlp_out_bias", (D,)),
        ("earth_bias", (LAT_BANDS, HEADS, WIN, WIN)),
    ]


def param_offsets():
    offsets = {}
    filled = 0
    for entry_name, entry_shape in param_layout():
        offsets[entry_name] = filled
        filled += math.prod(entry_shape)
    return offsets


OFFSET = param_offsets()
BIAS_ROW, BIAS_LANE = divmod(OFFSET["earth_bias"], LANES)
BIAS_ROWS = LAT_BANDS * HEADS * WIN
WIDE = LANES // math.gcd(WIN, LANES)
DENSE = WIN // math.gcd(WIN, LANES)
PERIODS = -(-(BIAS_ROWS // WIDE + 1) // 8) * 8
PITCH = PERIODS + 1
USED = BIAS_ROWS // WIDE
COL_LO = (OFFSET["norm2_gain"] // LANES) // 8 * 8
COL_HI = -(-BIAS_ROW // 8) * 8 + 8
BIAS_LO = BIAS_ROW // 8 * 8


def mm(left, right):
    return lax.dot_general(left, right, (((1,), (0,)), ((), ())), preferred_element_type=F32)


def mt(left, right):
    return lax.dot_general(left, right, (((1,), (1,)), ((), ())), preferred_element_type=F32)


def lane_ids(rows):
    return lax.broadcasted_iota(jnp.int32, (rows, LANES), 1)


def rows_at(start, count, stride):
    return pl.ds(start, count) if stride == 1 else pl.ds(start, count, stride=stride)


def read_matrix(dense, first_row, name, matrix):
    rows, width = dict(param_layout())[name]
    halves = width // HALF
    step = 1 + halves % 2
    count, stride = rows // step, halves * step // 2
    low = lane_ids(count) < HALF
    for part in range(step):
        for chunk in range(-(-halves // 2)):
            unit = OFFSET[name] // HALF + part * halves + 2 * chunk
            row = unit // 2 - first_row
            value = dense[rows_at(row, count, stride), :]
            if unit % 2:
                after = dense[rows_at(row + 1, count, stride), :]
                value = pltpu.roll(jnp.where(low, after, value), HALF, 1)
            matrix[chunk, rows_at(part, count, step), :] = value


def write_matrix(dense, first_row, name, matrix):
    rows, width = dict(param_layout())[name]
    halves = width // HALF
    step = 1 + halves % 2
    count, stride = rows // step, halves * step // 2
    lane = lane_ids(count)
    for part in range(step):
        piece = 0
        while piece < halves:
            unit = OFFSET[name] // HALF + part * halves + piece
            where_to = rows_at(unit // 2 - first_row, count, stride)
            chunk = piece // 2
            value = matrix[chunk, rows_at(part, count, step), :]
            if unit % 2 == piece % 2 == 0 and piece + 1 < halves:
                dense[where_to, :] = value
                piece += 2
                continue
            if unit % 2 != piece % 2:
                value = pltpu.roll(value, HALF, 1)
            mine = lane < HALF if unit % 2 == 0 else lane >= HALF
            dense[where_to, :] = jnp.where(mine, value, dense[where_to, :])
            piece += 1


def joined(matrix, width):
    chunks = [matrix[k] for k in range(-(-width // LANES))]
    return jnp.concatenate(chunks, axis=1)[:, :width]


def split_into(matrix, value):
    width = value.shape[1]
    for k in range(-(-width // LANES)):
        end = min(width, (k + 1) * LANES)
        matrix[k, :, : end - k * LANES] = value[:, k * LANES : end]


def read_vector(dense, first_row, name):
    size = dict(param_layout())[name][0]
    unit = OFFSET[name] // HALF
    row = unit // 2 - first_row
    turned = dense[row : row + 8, :].T
    pieces = []
    for k in range(size // HALF):
        spot = unit % 2 + k
        pieces.append(turned[spot % 2 * HALF : (spot % 2 + 1) * HALF, spot // 2 : spot // 2 + 1])
    return jnp.concatenate(pieces, axis=0)


def write_vector(dense, first_row, name, sums):
    size = dict(param_layout())[name][0]
    line = jnp.sum(sums.T, axis=0, keepdims=True)
    lane = lane_ids(1)
    for k in range(size // HALF):
        unit = OFFSET[name] // HALF + k
        row = unit // 2 - first_row
        if size % LANES and k == size // HALF - 1:
            tail = line[:, k * HALF :]
            piece = jnp.concatenate([tail, tail], axis=1)
        else:
            piece = line[:, k // 2 * LANES : (k // 2 + 1) * LANES]
            if unit % 2 != k % 2:
                piece = pltpu.roll(piece, HALF, 1)
        mine = lane < HALF if unit % 2 == 0 else lane >= HALF
        dense[row : row + 1, :] = jnp.where(mine, piece, dense[row : row + 1, :])


def read_bias(dense, wide):
    lane = lane_ids(PERIODS)
    for j in range(WIDE):
        row, first = divmod(BIAS_LANE + j * WIN, LANES)
        value = dense[pl.ds(BIAS_ROW + row, PERIODS, stride=DENSE), :]
        if first + WIN > LANES:
            after = dense[pl.ds(BIAS_ROW + row + 1, PERIODS, stride=DENSE), :]
            value = jnp.where(lane < first, after, value)
        if first:
            value = pltpu.roll(value, LANES - first, 1)
        wide[pl.ds(j * PITCH, PERIODS), :] = value


def wide_rows(pair, part, tile):
    line = part * WIN + tile * 8
    return pl.ds(line % WIDE * PITCH + WIN * 2 // WIDE * pair + line // WIDE, 8, stride=PITCH)


def write_bias(wide, dense, first_row):
    lane = lane_ids(PERIODS)
    for i in range(DENSE):
        begin = i * LANES - BIAS_LANE
        line = begin // WIN
        value = None
        while line * WIN < begin + LANES:
            shift = line * WIN - begin
            piece = wide[pl.ds(line % WIDE * PITCH + line // WIDE, PERIODS), :]
            if shift % LANES:
                piece = pltpu.roll(piece, shift % LANES, 1)
            value = piece if value is None else jnp.where(lane >= shift, piece, value)
            line += 1
        dense[pl.ds(BIAS_ROW - first_row + i, PERIODS, stride=DENSE), :] = value


def norm_parts(rows_in):
    mean = jnp.mean(rows_in, axis=0, keepdims=True)
    centered = rows_in - mean
    var = jnp.mean(centered * centered, axis=0, keepdims=True)
    scale = lax.rsqrt(var + norm_eps)
    return centered * scale, scale


def norm_back(grad, unit, scale, gain):
    scaled = grad * gain
    first = jnp.mean(scaled, axis=0, keepdims=True)
    second = jnp.mean(scaled * unit, axis=0, keepdims=True)
    return scale * (scaled - first - unit * second)


def lane_fold(value):
    total = value[:, :LANES]
    for k in range(1, value.shape[1] // LANES):
        total = total + value[:, k * LANES : (k + 1) * LANES]
    return total


def head_rows(h):
    return slice(h * HEAD_DIM, (h + 1) * HEAD_DIM)


def head_lanes(h):
    return slice(h * LANES, (h + 1) * LANES)


def interleave(parts):
    parts = list(parts)
    live, started = [], 0
    while live or started < len(parts):
        if started < len(parts):
            live.append(parts[started])
            started += 1
        live = [part for part in live if next(part, live) is None]


def own_column(full, bits):
    heads = []
    for h in range(HEADS):
        tiles = [full[k * LEVELS : (k + 1) * LEVELS, head_lanes(h)] for k in range(LANES // LEVELS)]
        for bit in bits:
            tiles = [jnp.where(bit, b, a) for a, b in zip(tiles[::2], tiles[1::2])]
        heads.append(tiles[0])
    return jnp.concatenate(heads, axis=1)


def all_columns(own, same):
    pair = jnp.concatenate([own, own], axis=0).astype(BF16)
    tall = jnp.concatenate([pair] * (LANES // (2 * LEVELS)), axis=0)
    return jnp.concatenate([tall[:, head_lanes(h)] * same for h in range(HEADS)], axis=1)


def blend(rows_in, weights):
    pieces = []
    for h in range(0, HEADS, 2):
        pair = slice(h * HEAD_DIM, (h + 2) * HEAD_DIM)
        both = mm(rows_in[pair], weights[:, h * LANES : (h + 2) * LANES])
        pieces += [both[:HEAD_DIM, :LANES], both[HEAD_DIM:, LANES:]]
    return jnp.concatenate(pieces, axis=0)


def gather_pairs(block, weights):
    pieces = []
    for h in range(0, HEADS, 2):
        lanes = slice(h * LANES, (h + 2) * LANES)
        pieces.append(mt(block[h * HEAD_DIM : (h + 2) * HEAD_DIM, lanes], weights[:, lanes]))
    return jnp.concatenate(pieces, axis=0)


def scatter_heads(block, rows_in):
    for h in range(HEADS):
        block[head_rows(h), head_lanes(h)] = rows_in[head_rows(h), :]


def chooser(first, slots):
    ids = lax.broadcasted_iota(jnp.int32, (PICK, slots.shape[1]), 0).astype(F32).astype(BF16)
    near = jnp.clip(slots - first, -1, PICK).astype(F32).astype(BF16)
    return jnp.where(ids == near, jnp.ones((), BF16), jnp.zeros((), BF16))


def spread_windows(rows_t):
    blank = jnp.zeros((rows_t.shape[0], LANES - WIN), rows_t.dtype)
    pieces = []
    for k in range(0, rows_t.shape[1], WIN):
        pieces += [rows_t[:, k : k + WIN], blank]
    return jnp.concatenate(pieces, axis=1)


def join_windows(rows_t):
    return jnp.concatenate(
        [rows_t[:, k : k + WIN] for k in range(0, rows_t.shape[1], LANES)], axis=1
    )


def to_slots(rows_t, slots):
    tokens = rows_t.shape[1]
    pick = jnp.concatenate([chooser(k, slots) for k in range(0, tokens, PICK)], axis=0)
    return spread_windows(mm(rows_t, pick)).astype(BF16)


def from_slots(slot_rows, slots, first, rows):
    return jnp.concatenate(
        [mt(slot_rows, chooser(first + k, slots)) for k in range(0, rows, PICK)], axis=1
    )


def call(kernel, grid, ins, outs, scratch, name, macs, limit, scalars=0):
    in_specs = [s for _, s in ins]
    spec = pltpu.PrefetchScalarGridSpec(
        num_scalar_prefetch=scalars,
        grid=grid,
        in_specs=in_specs[scalars:],
        out_specs=[s for _, _, s in outs],
        scratch_shapes=scratch,
    )
    return pl.pallas_call(
        kernel,
        grid_spec=spec,
        out_shape=[jax.ShapeDtypeStruct(shape, kind) for shape, kind, _ in outs],
        compiler_params=pltpu.CompilerParams(
            dimension_semantics=("arbitrary",) * len(grid), vmem_limit_bytes=limit << 20
        ),
        cost_estimate=pl.CostEstimate(
            flops=2 * macs,
            transcendentals=0,
            bytes_accessed=sum(a.size * a.dtype.itemsize for a, _ in ins)
            + sum(math.prod(shape) * jnp.dtype(kind).itemsize for shape, kind, _ in outs),
        ),
        name=name,
    )(*[a for a, _ in ins])


def padded_rows(rows):
    return -(-(rows + 1) // 8) * 8


def whole_block(shape):
    return pl.BlockSpec(shape, lambda *_: (0,) * len(shape))


def fixed_block(array):
    return pl.BlockSpec(
        array.shape, lambda *_: (0,) * array.ndim, pipeline_mode=pl.Buffered(buffer_count=1)
    )


SLOT_BLOCK = 2048
TIGHT_BLOCK = SLOT_BLOCK // LANES * WIN
TURNS = 12
RING = 4
PICK = 256
TOKEN_BLOCK = 768


def shift_kernel(x_ref, slots_ref, out_ref, again_ref, x_t):
    @pl.when(pl.program_id(0) == 0)
    def _():
        x_t[...] = x_ref[...].astype(F32).T.astype(BF16)

    result = to_slots(x_t[...], slots_ref[...])
    out_ref[...] = result
    again_ref[...] = result


def shift_call(tokens, slots):
    count, n = tokens.shape[0], slots.shape[1] // WIN * LANES
    return call(
        shift_kernel,
        (n // SLOT_BLOCK,),
        [
            (tokens, fixed_block(tokens)),
            (slots, pl.BlockSpec((1, TIGHT_BLOCK), lambda i: (0, i))),
        ],
        [((D, n), BF16, pl.BlockSpec((D, SLOT_BLOCK), lambda i: (0, i)))] * 2,
        [pltpu.VMEM((D, count), BF16)],
        "shift",
        D * count * n,
        24,
    )


def load_dense(me_ref, parts, plan, blocks, dense, sem, order, rows):
    copies = []
    for part, first, spot, count, row in plan:
        copies.append(
            pltpu.make_async_copy(
                parts[part].at[pl.ds(first, count)],
                blocks.at[pl.ds(spot, count), pl.ds(row, parts[part].shape[1])],
                sem,
            )
        )
    for copy in copies:
        copy.start()
    for copy in copies:
        copy.wait()
    shards = blocks.shape[0]
    for shard in range(shards):
        spot = position(me_ref[0] ^ shard, order)
        dense[shard * rows : (shard + 1) * rows, :] = blocks[spot, :rows, :].astype(F32)
    if dense.shape[0] > shards * rows:
        dense[shards * rows :, :] = jnp.zeros((dense.shape[0] - shards * rows, LANES), F32)


def position(relative, order):
    spot = 0
    for place, bit in enumerate(reversed(order)):
        spot = spot + ((relative >> bit) & 1) * (1 << place)
    return spot


def band_of(table, window, me_ref, space, steps):
    if not space:
        return table[0, window]
    each = steps * (SLOT_BLOCK // LANES) // space
    return table[window // each, me_ref[0] % space * each + window % each]


def window_forward_kernel(me_ref, band_ref, *refs, parts, plan, order, rows, steps, space):
    fused = space > 0
    ins = refs[:parts]
    refs = refs[parts:]
    if fused:
        shifted_ref, slots_ref, x_ref = refs[:3]
        refs = refs[3:]
    else:
        shifted_ref, refs = refs[0], refs[1:]
    (
        out_ref,
        qkv_ref,
        mixed_ref,
        prob_ref,
        weights_ref,
        column_ref,
        vec,
        table_ref,
        blocks,
        dense,
        wide,
        bias,
        mat,
        qkv_t,
        proj_t,
        spread,
        y_all,
        band_s,
        sem,
    ) = refs
    step = pl.program_id(0)

    @pl.when(step == 0)
    def _():
        load_dense(me_ref, ins, plan, blocks, dense, sem, order, rows)
        if fused:
            lines = []
            for source in range(space):
                shard = me_ref[0] // space * space + source
                tile = blocks[position(me_ref[0] ^ shard, order), rows // 8 * 8 : rows // 8 * 8 + 8, :]
                lines.append(tile.astype(F32)[rows % 8 : rows % 8 + 1])
            table_ref[...] = jnp.concatenate(lines, axis=0).astype(jnp.int32)
            copy = pltpu.make_async_copy(table_ref, band_s, sem)
            copy.start()
            copy.wait()
        column_ref[...] = dense[COL_LO:COL_HI, :]
        read_matrix(dense, 0, "qkv1", mat)
        weights_ref[:, : 3 * D] = joined(mat, 3 * D).astype(BF16)
        qkv_t[...] = joined(mat, 3 * D).T.astype(BF16)
        read_matrix(dense, 0, "proj1", mat)
        weights_ref[:, 3 * D :] = joined(mat, D).astype(BF16)
        proj_t[...] = joined(mat, D).T.astype(BF16)
        vec[:, 0:1] = read_vector(dense, 0, "norm1_gain")
        vec[:, 1:2] = read_vector(dense, 0, "norm1_shift")
        vec[:, 2:3] = read_vector(dense, 0, "proj1_bias")
        read_bias(dense, wide)
        blank = jnp.zeros((LANES - WIN, LANES), F32)

        def turn(k, _):
            for j in range(TURNS):
                pair, part = k * (TURNS // 2) + j // 2, j % 2
                tiles = [wide[wide_rows(pair, part, tile), :] for tile in range(WIN // 8)]
                block = jnp.concatenate(tiles + [blank], axis=0).T
                bias[k * TURNS + j, :WIN, :] = block[:WIN].astype(BF16)
            return 0

        lax.fori_loop(0, LAT_BANDS * HEADS // TURNS, turn, 0)
        bias[:, WIN:, :] = jnp.full((LAT_BANDS * HEADS, KEYS - WIN, LANES), -jnp.inf, BF16)
        spread[...] = jnp.zeros_like(spread)

    @pl.when(step < steps)
    def _():
        per_step = SLOT_BLOCK // LANES
        unit, _ = norm_parts(shifted_ref[...].astype(F32))
        normed = (unit * vec[:, 0:1] + vec[:, 1:2]).astype(BF16)
        qkv = mm(qkv_t[...], normed).astype(BF16)
        qkv_ref[...] = qkv
        blank = jnp.zeros((LANES - KEYS, HEADS * LANES), BF16)
        scores, probs, mixed = {}, {}, []
        for turn in range(per_step + 2):
            if turn < per_step:
                lanes = slice(turn * LANES, (turn + 1) * LANES)
                scatter_heads(spread.at[turn % RING], qkv[:D, lanes])
                scores[turn] = mm(qkv[D : 2 * D, lanes].T[:KEYS], spread[turn % RING])
            if 1 <= turn <= per_step:
                w = turn - 1
                table = band_s if fused else band_ref
                band = band_of(table, step * per_step + w, me_ref, space, steps)
                heads = []
                for h in range(HEADS):
                    score = scores[w][:, head_lanes(h)] * SCALE + bias[band * HEADS + h].astype(F32)
                    grown = jnp.exp(score - jnp.max(score, axis=0, keepdims=True))
                    heads.append(
                        (grown * (1.0 / jnp.sum(grown, axis=0, keepdims=True))).astype(BF16)
                    )
                probs[w] = jnp.concatenate(heads, axis=1)
                prob_ref[w] = probs[w]
            if turn >= 2:
                w = turn - 2
                tall = jnp.concatenate([probs[w], blank], axis=0)
                mixed.append(blend(qkv[2 * D :, w * LANES : (w + 1) * LANES], tall))
        mixed = jnp.concatenate(mixed, axis=1).astype(BF16)
        mixed_ref[...] = mixed
        result = mm(proj_t[...], mixed) + vec[:, 2:3]
        if fused:
            spot = pl.ds(pl.multiple_of(step * TIGHT_BLOCK, TIGHT_BLOCK), TIGHT_BLOCK)
            y_all[:, spot] = join_windows(result).astype(BF16)
        else:
            out_ref[...] = result.astype(BF16)

    if fused:

        @pl.when(step >= steps)
        def _():
            branch = from_slots(
                y_all[...], slots_ref[...], (step - steps) * TOKEN_BLOCK, TOKEN_BLOCK
            )
            out_ref[...] = x_ref[...].astype(F32).T + branch


def window_forward_call(me, bands, parts, plan, order, shards, rows, shifted, tokens, slots, space):
    fused = space > 0
    n = shifted.shape[1]
    steps = n // SLOT_BLOCK
    per_step = SLOT_BLOCK // LANES
    padded = padded_rows(rows)
    flat_rows = max(shards * rows, BIAS_ROW + DENSE * PERIODS + 8)
    slot_block = lambda r: pl.BlockSpec((r, SLOT_BLOCK), lambda i, *_: (0, jnp.minimum(i, steps - 1)))
    ins = [(me, None), (bands, None)]
    ins += [(p, pl.BlockSpec(memory_space=pl.ANY)) for p in parts]
    ins += [(shifted, slot_block(D))]
    if fused:
        count = tokens.shape[0]
        late = lambda i: jnp.maximum(i - steps, 0)
        ins += [
            (slots, fixed_block(slots)),
            (tokens, pl.BlockSpec((TOKEN_BLOCK, D), lambda i, *_: (late(i), 0))),
        ]
        first = ((D, count), F32, pl.BlockSpec((D, TOKEN_BLOCK), lambda i, *_: (0, late(i))))
        grid = steps + count // TOKEN_BLOCK
    else:
        first = ((D, n), BF16, slot_block(D))
        grid = steps
    outs = [
        first,
        ((3 * D, n), BF16, slot_block(3 * D)),
        ((D, n), BF16, slot_block(D)),
        (
            (n // LANES, KEYS, HEADS * LANES),
            BF16,
            pl.BlockSpec(
                (per_step, KEYS, HEADS * LANES), lambda i, *_: (jnp.minimum(i, steps - 1), 0, 0)
            ),
        ),
        ((D, 4 * D), BF16, whole_block((D, 4 * D))),
        ((COL_HI - COL_LO, LANES), F32, whole_block((COL_HI - COL_LO, LANES))),
        ((D, LANES), F32, whole_block((D, LANES))),
        ((max(space, 1), LANES), jnp.int32, whole_block((max(space, 1), LANES))),
    ]
    scratch = [
        pltpu.VMEM((shards, padded, LANES), BF16),
        pltpu.VMEM((flat_rows, LANES), F32),
        pltpu.VMEM((WIDE * PITCH, LANES), F32),
        pltpu.VMEM((LAT_BANDS * HEADS, KEYS, LANES), BF16),
        pltpu.VMEM((5, D, LANES), F32),
        pltpu.VMEM((3 * D, D), BF16),
        pltpu.VMEM((D, D), BF16),
        pltpu.VMEM((RING, D, HEADS * LANES), BF16),
        pltpu.VMEM((D, n // LANES * WIN), BF16),
        pltpu.SMEM((max(space, 1), LANES), jnp.int32),
        pltpu.SemaphoreType.DMA,
    ]
    kernel = functools.partial(
        window_forward_kernel,
        parts=len(parts),
        plan=plan,
        order=order,
        rows=rows,
        steps=steps,
        space=space,
    )
    return call(kernel, (grid,), ins, outs, scratch, "window_forward", 12 * D * D * n, 36, scalars=2)


COLUMN_BLOCK = 768
COLUMN_PART = 768
COLUMN_VECTORS = (
    "norm2_gain",
    "norm2_shift",
    "proj2_bias",
    "norm3_gain",
    "norm3_shift",
    "mlp_out_bias",
)
COLUMN_MATRICES = ("qkv2", "proj2", "mlp_in", "mlp_out")


def column_kernel(
    dense,
    x_ref,
    cot_ref,
    count_ref,
    out_ref,
    after_ref,
    branch_ref,
    grad_ref,
    mat,
    tall,
    w_qkv,
    w_proj,
    w_in,
    w_out,
    t_qkv,
    t_proj,
    t_in,
    t_out,
    vec,
    fvec,
    grad_qkv,
    grad_proj,
    grad_in,
    grad_out,
    sums,
    fsums,
    spread,
):
    step = pl.program_id(0)

    @pl.when(step == 0)
    def _():
        for name, plain, turned in (
            ("qkv2", w_qkv, t_qkv),
            ("proj2", w_proj, t_proj),
            ("mlp_in", w_in, t_in),
            ("mlp_out", w_out, t_out),
        ):
            rows, width = plain.shape
            source = tall if rows == FF else mat
            read_matrix(dense, COL_LO, name, source)
            plain[...] = joined(source, width).astype(BF16)
            turned[...] = joined(source, width).T.astype(BF16)
        for k, name in enumerate(COLUMN_VECTORS):
            vec[:, k : k + 1] = read_vector(dense, COL_LO, name)
        fvec[:, 0:1] = read_vector(dense, COL_LO, "mlp_in_bias")
        sums[...] = jnp.zeros_like(sums)
        fsums[...] = jnp.zeros_like(fsums)
        for grad in (grad_qkv, grad_proj, grad_in, grad_out):
            grad[...] = jnp.zeros_like(grad)
        spread[...] = jnp.zeros_like(spread)

    gain2, shift2, bias2, gain3, shift3, bias_out = [vec[:, k : k + 1] for k in range(6)]
    key_id = lax.broadcasted_iota(jnp.int32, (LANES, LANES), 0)
    query_id = lax.broadcasted_iota(jnp.int32, (LANES, LANES), 1)
    same = jnp.where(key_id // LEVELS == query_id // LEVELS, 1.0, 0.0).astype(BF16)
    column = lax.broadcasted_iota(jnp.int32, (LEVELS, LANES), 1) // LEVELS
    bits = [(column >> k) & 1 == 1 for k in range(4)]
    level = lax.broadcasted_iota(jnp.int32, (LEVELS, LANES), 0)
    groups = COLUMN_PART // LANES

    def part_steps(part):
        here = slice(part * COLUMN_PART, (part + 1) * COLUMN_PART)
        x = x_ref[:, here]
        unit2, scale2 = norm_parts(x)
        n2 = (unit2 * gain2 + shift2).astype(BF16)
        yield
        qkv = mm(t_qkv[...], n2).astype(BF16)
        yield
        scores = []
        for g in range(groups):
            lanes = slice(g * LANES, (g + 1) * LANES)
            scatter_heads(spread.at[0, part * groups + g], qkv[:D, lanes])
            scores.append(own_column(mm(qkv[D : 2 * D, lanes].T, spread[0, part * groups + g]), bits))
        yield
        probs, tall_probs = [], []
        for g in range(groups):
            begin = part * COLUMN_PART + g * LANES
            valid = level < count_ref[:, begin : begin + LANES]
            score = jnp.where(jnp.concatenate([valid] * HEADS, axis=1), scores[g] * SCALE, -jnp.inf)
            grown = jnp.exp(score - jnp.max(score, axis=0, keepdims=True))
            prob = grown * (1.0 / jnp.sum(grown, axis=0, keepdims=True))
            probs.append(prob)
            tall_probs.append(all_columns(prob, same))
        yield
        mixed = [
            blend(qkv[2 * D :, g * LANES : (g + 1) * LANES], tall_probs[g]) for g in range(groups)
        ]
        mixed = jnp.concatenate(mixed, axis=1).astype(BF16)
        projected = mm(t_proj[...], mixed)
        yield
        middle = x + (projected + bias2)
        unit3, scale3 = norm_parts(middle)
        n3 = (unit3 * gain3 + shift3).astype(BF16)
        yield
        pre = mm(t_in[...], n3)
        cot = cot_ref[here, :].astype(F32).T
        cot_bf = cot.astype(BF16)
        dact = mm(w_out[...], cot_bf)
        yield
        pre = pre + fvec[:, 0:1]
        root = math.sqrt(2.0 / math.pi)
        square = pre * pre
        share = 0.5 + 0.5 * jnp.tanh(pre * (root + (root * 0.044715) * square))
        act = pre * share
        slope = share + act * (1.0 - share) * (2.0 * root + (6.0 * root * 0.044715) * square)
        act = act.astype(BF16)
        dpre = (dact * slope).astype(BF16)
        yield
        output = middle + (mm(t_out[...], act) + bias_out)
        out_ref[here, :] = output.T.astype(BF16)
        dn3 = mm(w_in[...], dpre)
        grad_out[...] += mt(act, cot_bf)
        grad_in[...] += mt(n3, dpre)
        yield
        dmiddle = cot + norm_back(dn3, unit3, scale3, gain3)
        dattn = dmiddle.astype(BF16)
        sums[2] += lane_fold(dattn.astype(F32))
        sums[3] += lane_fold(dn3 * unit3)
        sums[4] += lane_fold(dn3)
        sums[5] += lane_fold(cot_bf.astype(F32))
        fsums[...] += lane_fold(dpre.astype(F32))
        yield
        dmixed = mm(w_proj[...], dattn).astype(BF16)
        grad_proj[...] += mt(mixed, dattn)
        dprobs = []
        for g in range(groups):
            lanes = slice(g * LANES, (g + 1) * LANES)
            scatter_heads(spread.at[1, part * groups + g], dmixed[:, lanes])
            dprobs.append(own_column(mm(qkv[2 * D :, lanes].T, spread[1, part * groups + g]), bits))
        yield
        dscores = []
        for prob, dprob in zip(probs, dprobs):
            dscore = prob * (dprob - jnp.sum(prob * dprob, axis=0, keepdims=True))
            dscores.append(all_columns(dscore, same))
        yield
        dq, dk, dv = [], [], []
        for g in range(groups):
            dq.append(blend(qkv[D : 2 * D, g * LANES : (g + 1) * LANES], dscores[g]) * SCALE)
            dk.append(gather_pairs(spread.at[0, part * groups + g], dscores[g]) * SCALE)
            dv.append(gather_pairs(spread.at[1, part * groups + g], tall_probs[g]))
        dqkv = [jnp.concatenate(d, axis=1) for d in (dq, dk, dv)]
        dqkv = jnp.concatenate(dqkv, axis=0).astype(BF16)
        dn2 = mm(w_qkv[...], dqkv)
        grad_qkv[...] += mt(n2, dqkv)
        yield
        dafter = dmiddle + norm_back(dn2, unit2, scale2, gain2)
        after_ref[:, here] = dafter
        branch_ref[:, here] = dafter.astype(BF16)
        sums[0] += lane_fold(dn2 * unit2)
        sums[1] += lane_fold(dn2)

    interleave([part_steps(part) for part in range(COLUMN_BLOCK // COLUMN_PART)])

    @pl.when(step == pl.num_programs(0) - 1)
    def _():
        grad_ref[...] = jnp.zeros_like(grad_ref)
        split_into(mat, grad_qkv[...])
        write_matrix(grad_ref, COL_LO, "qkv2", mat)
        split_into(mat, grad_proj[...])
        write_matrix(grad_ref, COL_LO, "proj2", mat)
        split_into(mat, grad_in[...])
        write_matrix(grad_ref, COL_LO, "mlp_in", mat)
        split_into(tall, grad_out[...])
        write_matrix(grad_ref, COL_LO, "mlp_out", tall)
        for k, name in enumerate(COLUMN_VECTORS):
            write_vector(grad_ref, COL_LO, name, sums[k])
        write_vector(grad_ref, COL_LO, "mlp_in_bias", fsums[...])


def column_call(dense, after_t, cotangent, counts):
    n = after_t.shape[1]
    feature = lambda r: pl.BlockSpec((r, COLUMN_BLOCK), lambda i: (0, i))
    token = pl.BlockSpec((COLUMN_BLOCK, D), lambda i: (i, 0))
    return call(
        column_kernel,
        (n // COLUMN_BLOCK,),
        [
            (dense, fixed_block(dense)),
            (after_t, feature(D)),
            (cotangent, token),
            (counts, feature(1)),
        ],
        [
            ((n, D), BF16, token),
            ((D, n), F32, feature(D)),
            ((D, n), BF16, feature(D)),
            (dense.shape, F32, whole_block(dense.shape)),
        ],
        [
            pltpu.VMEM((FF // LANES, D, LANES), F32),
            pltpu.VMEM((2, FF, LANES), F32),
            pltpu.VMEM((D, 3 * D), BF16),
            pltpu.VMEM((D, D), BF16),
            pltpu.VMEM((D, FF), BF16),
            pltpu.VMEM((FF, D), BF16),
            pltpu.VMEM((3 * D, D), BF16),
            pltpu.VMEM((D, D), BF16),
            pltpu.VMEM((FF, D), BF16),
            pltpu.VMEM((D, FF), BF16),
            pltpu.VMEM((D, LANES), F32),
            pltpu.VMEM((FF, LANES), F32),
            pltpu.VMEM((D, 3 * D), F32),
            pltpu.VMEM((D, D), F32),
            pltpu.VMEM((D, FF), F32),
            pltpu.VMEM((FF, D), F32),
            pltpu.VMEM((6, D, LANES), F32),
            pltpu.VMEM((FF, LANES), F32),
            pltpu.VMEM((2, COLUMN_BLOCK // LANES, D, HEADS * LANES), BF16),
        ],
        "column",
        40 * D * D * n,
        40,
    )


def window_backward_kernel(me_ref, band_ref, *refs, order, shard_rows, space):
    fused = space > 0
    if fused:
        slots_ref, refs = refs[0], refs[1:]
    (
        grad_ref,
        weights_ref,
        vec,
        column_ref,
        shifted_ref,
        qkv_ref,
        mixed_ref,
        prob_ref,
        out_ref,
        keep_ref,
        send_ref,
        total,
        wide,
        dense,
        mat,
        blocks,
        spread,
        grad_qkv,
        grad_proj,
        sums,
        sem,
    ) = refs
    step = pl.program_id(0)
    per_step = SLOT_BLOCK // LANES

    @pl.when(step == 0)
    def _():
        total[...] = jnp.zeros_like(total)
        sums[...] = jnp.zeros_like(sums)
        grad_qkv[...] = jnp.zeros_like(grad_qkv)
        grad_proj[...] = jnp.zeros_like(grad_proj)
        spread[...] = jnp.zeros_like(spread)

    if fused:
        grad = to_slots(grad_ref[...], slots_ref[...])
    else:
        grad = grad_ref[...]
    grad_proj[...] += mt(mixed_ref[...], grad)
    dmixed = mm(weights_ref[:, 3 * D :], grad).astype(BF16)
    qkv = qkv_ref[...]
    blank = jnp.zeros((LANES - KEYS, HEADS * LANES), BF16)
    dq, dk, dv, dprobs, dscores = [], [], [], {}, {}
    for turn in range(per_step + 2):
        if turn < per_step:
            lanes = slice(turn * LANES, (turn + 1) * LANES)
            scatter_heads(spread.at[0, turn % RING], qkv[:D, lanes])
            scatter_heads(spread.at[1, turn % RING], dmixed[:, lanes])
            dprobs[turn] = mm(qkv[2 * D :, lanes].T[:KEYS], spread[1, turn % RING])
        if 1 <= turn <= per_step:
            w = turn - 1
            heads = []
            for h in range(HEADS):
                prob = prob_ref[w, :, head_lanes(h)].astype(F32)
                dprob = dprobs[w][:, head_lanes(h)]
                heads.append(
                    (prob * (dprob - jnp.sum(prob * dprob, axis=0, keepdims=True))).astype(BF16)
                )
            dscores[w] = jnp.concatenate(heads, axis=1)
            band = band_of(band_ref, step * per_step + w, me_ref, space, pl.num_programs(0))
            for h in range(HEADS):
                spot = pl.ds(pl.multiple_of((band * HEADS + h) * KEYS, 8), KEYS)
                total[spot, :] += heads[h].astype(F32)
        if turn >= 2:
            w = turn - 2
            tall = jnp.concatenate([dscores[w], blank], axis=0)
            dq.append(blend(qkv[D : 2 * D, w * LANES : (w + 1) * LANES], tall) * SCALE)
            dk.append(gather_pairs(spread.at[0, w % RING], tall) * SCALE)
            tall = jnp.concatenate([prob_ref[w], blank], axis=0)
            dv.append(gather_pairs(spread.at[1, w % RING], tall))
    dqkv = jnp.concatenate([jnp.concatenate(d, axis=1) for d in (dq, dk, dv)], axis=0).astype(BF16)
    unit, scale = norm_parts(shifted_ref[...].astype(F32))
    grad_qkv[...] += mt((unit * vec[:, 0:1] + vec[:, 1:2]).astype(BF16), dqkv)
    dnormed = mm(weights_ref[:, : 3 * D], dqkv)
    dshifted = norm_back(dnormed, unit, scale, vec[:, 0:1])
    out_ref[...] = (join_windows(dshifted) if fused else dshifted).astype(BF16)
    for k, value in enumerate((dnormed * unit, dnormed, grad.astype(F32))):
        sums[k] += lane_fold(value)

    @pl.when(step == pl.num_programs(0) - 1)
    def _():
        for j in range(WIDE):
            wide[j * PITCH + USED : (j + 1) * PITCH, :] = jnp.zeros((PITCH - USED, LANES), F32)
        blank = jnp.zeros((WIN, LANES - KEYS), F32)

        def turn(k, _):
            for j in range(TURNS):
                pair, part = k * (TURNS // 2) + j // 2, j % 2
                spot = pl.ds(pl.multiple_of((k * TURNS + j) * KEYS, 8), KEYS)
                block = jnp.concatenate([total[spot, :].T[:WIN], blank], axis=1)
                for tile in range(WIN // 8):
                    wide[wide_rows(pair, part, tile), :] = block[tile * 8 : tile * 8 + 8]
            return 0

        lax.fori_loop(0, LAT_BANDS * HEADS // TURNS, turn, 0)
        dense[:COL_LO, :] = jnp.zeros((COL_LO, LANES), F32)
        write_bias(wide, dense, 0)
        covered = BIAS_ROW + DENSE * PERIODS
        dense[covered:, :] = jnp.zeros((dense.shape[0] - covered, LANES), F32)
        both = column_ref[COL_HI - COL_LO - 16 :, :]
        rows = lax.broadcasted_iota(jnp.int32, both.shape, 0) + (COL_HI - 16)
        lane = lane_ids(16)
        start = rows * LANES + lane < OFFSET["earth_bias"]
        dense[COL_LO : COL_HI - 16, :] = column_ref[: COL_HI - COL_LO - 16, :]
        dense[COL_HI - 16 : COL_HI, :] = jnp.where(start, both, dense[COL_HI - 16 : COL_HI, :])
        split_into(mat, grad_qkv[...])
        write_matrix(dense, 0, "qkv1", mat)
        split_into(mat, grad_proj[...])
        write_matrix(dense, 0, "proj1", mat)
        for k, name in enumerate(("norm1_gain", "norm1_shift", "proj1_bias")):
            write_vector(dense, 0, name, sums[k])
        shards, rows = blocks.shape[0], shard_rows
        for shard in range(shards):
            spot = position(me_ref[0] ^ shard, order)
            blocks[spot, :rows, :] = dense[shard * rows : (shard + 1) * rows, :].astype(BF16)
        first = pltpu.make_async_copy(blocks.at[pl.ds(0, shards // 2)], keep_ref, sem.at[0])
        second = pltpu.make_async_copy(
            blocks.at[pl.ds(shards // 2, shards // 2)], send_ref, sem.at[1]
        )
        first.start()
        second.start()
        first.wait()
        second.wait()


def window_backward_call(
    me, bands, order, shards, rows, slots, grad, weights, vec, column_grad, shifted, qkv, mixed, prob, space
):
    fused = space > 0
    padded = padded_rows(rows)
    n = shifted.shape[1]
    per_step = SLOT_BLOCK // LANES
    slot_block = lambda r: pl.BlockSpec((r, SLOT_BLOCK), lambda i, *_: (0, i))
    ins = [(me, None), (bands, None)]
    if fused:
        tight = pl.BlockSpec((1, TIGHT_BLOCK), lambda i, *_: (0, i))
        ins += [(slots, tight), (grad, fixed_block(grad))]
    else:
        ins += [(grad, slot_block(D))]
    ins += [
        (weights, fixed_block(weights)),
        (vec, fixed_block(vec)),
        (column_grad, fixed_block(column_grad)),
        (shifted, slot_block(D)),
        (qkv, slot_block(3 * D)),
        (mixed, slot_block(D)),
        (
            prob,
            pl.BlockSpec((per_step, KEYS, HEADS * LANES), lambda i, *_: (i, 0, 0)),
        ),
    ]
    flat_rows = max(shards * rows, BIAS_ROW + DENSE * PERIODS + 8)
    if fused:
        tight = pl.BlockSpec((D, TIGHT_BLOCK), lambda i, *_: (0, i))
        first = ((D, n // LANES * WIN), BF16, tight)
    else:
        first = ((D, n), BF16, slot_block(D))
    outs = [
        first,
        ((shards // 2, padded, LANES), BF16, pl.BlockSpec(memory_space=pl.ANY)),
        ((shards // 2, padded, LANES), BF16, pl.BlockSpec(memory_space=pl.ANY)),
    ]
    scratch = [
        pltpu.VMEM((LAT_BANDS * HEADS * KEYS, LANES), F32),
        pltpu.VMEM((WIDE * PITCH, LANES), F32),
        pltpu.VMEM((flat_rows, LANES), F32),
        pltpu.VMEM((5, D, LANES), F32),
        pltpu.VMEM((shards, padded, LANES), BF16),
        pltpu.VMEM((2, RING, D, HEADS * LANES), BF16),
        pltpu.VMEM((D, 3 * D), F32),
        pltpu.VMEM((D, D), F32),
        pltpu.VMEM((3, D, LANES), F32),
        pltpu.SemaphoreType.DMA((2,)),
    ]
    kernel = functools.partial(
        window_backward_kernel, order=order, shard_rows=rows, space=space
    )
    return call(kernel, (n // SLOT_BLOCK,), ins, outs, scratch, "window_backward", 24 * D * D * n, 44, scalars=2)


def finish_kernel(shift_ref, slots_ref, after_ref, out_ref):
    first = pl.program_id(0) * TOKEN_BLOCK
    back = from_slots(shift_ref[...], slots_ref[...], first, TOKEN_BLOCK)
    out_ref[...] = (after_ref[...] + back).T


def finish_call(grad_shifted, slots, after_t):
    n = after_t.shape[1]
    return call(
        finish_kernel,
        (n // TOKEN_BLOCK,),
        [
            (grad_shifted, fixed_block(grad_shifted)),
            (slots, fixed_block(slots)),
            (after_t, pl.BlockSpec((D, TOKEN_BLOCK), lambda i: (0, i))),
        ],
        [((n, D), F32, pl.BlockSpec((TOKEN_BLOCK, D), lambda i: (i, 0)))],
        [],
        "finish",
        D * n * slots.shape[1],
        24,
    )[0]


def body(block_input, cotangent, params, send_rows, window_band, level_count):
    model_width = block_input.shape[-1]
    rows_dev = block_input.shape[1] * block_input.shape[2]
    n_space, per_peer = send_rows.shape[1], send_rows.shape[3]
    devices = lax.axis_size(("dp", "space"))
    group = WIN // math.gcd(per_peer, WIN)
    if n_space % group:
        group = n_space
    fused = group == 1
    dest = n_space // group
    per_dest = group * per_peer // WIN
    member_groups = [[first + k for k in range(group)] for first in range(0, n_space, group)]
    place = lax.axis_index("space")
    index = lax.axis_index(("dp", "space"))
    me = index.astype(jnp.int32).reshape(1)
    bits = devices.bit_length() - 1
    order = [0] + list(range(bits - 1, 0, -1))

    def swap(value, *across):
        flip = sum(1 << bit for bit in across)
        return lax.ppermute(value, ("dp", "space"), [(k, k ^ flip) for k in range(devices)])

    def exchange(value):
        return lax.all_to_all(
            value, "space", split_axis=0, concat_axis=0, tiled=True, axis_index_groups=member_groups
        )

    def to_windows(rows):
        moved = exchange(rows[route_flat]).reshape(group, dest, per_peer, model_width)
        windows = moved.transpose(1, 0, 2, 3).reshape(-1, WIN, model_width)
        windows = jnp.pad(windows, ((0, 0), (0, LANES - WIN), (0, 0)))
        return windows.reshape(-1, model_width).T

    def from_windows(rows_t):
        rows = rows_t.T.reshape(-1, LANES, model_width)[:, :WIN]
        moved = rows.reshape(dest, group, per_peer, model_width).transpose(1, 0, 2, 3)
        rows = exchange(moved.reshape(rows_dev, model_width))
        return jnp.zeros((rows_dev, model_width), rows.dtype).at[route_flat].set(rows)

    flat_in = block_input[0].reshape(rows_dev, model_width)
    routes = send_rows[0, :, 0, :]
    route_flat = routes.reshape(-1)
    slots = routes.reshape(1, -1)
    if fused:
        bands = jnp.zeros((1, LANES), jnp.int32)
    else:
        all_bands = lax.all_gather(window_band[0], "space", axis=0)
        bands = lax.dynamic_slice(
            all_bands, ((place % group) * dest, (place // group) * per_dest), (dest, per_dest)
        ).reshape(1, -1)
        shifted = shifted_again = to_windows(flat_in)

    shard_rows = params.shape[0] // LANES
    padded = padded_rows(shard_rows)
    band_row = jnp.pad(window_band[0], (0, LANES - window_band.shape[1])).astype(BF16)
    own_rows = jnp.pad(params.reshape(shard_rows, LANES), ((0, padded - shard_rows), (0, 0)))
    row_id = lax.broadcasted_iota(jnp.int32, (padded, 1), 0)
    held = jnp.where(row_id == shard_rows, band_row[None, :], own_rows.astype(BF16))[None]
    near, far = order[-1], order[-2]
    direct = [swap(held, near), swap(held, far), swap(held, near, far)]
    held = jnp.concatenate([held] + direct, axis=0)
    for bit in reversed(order[3:-2]):
        held = jnp.concatenate([held, swap(held, bit)], axis=0)
    top, next_top = order[1], order[2]
    cut = padded // 16 * 8
    upper, lower = held[:, :cut], held[:, cut:]
    upper = jnp.concatenate([upper, swap(upper, next_top)], axis=0)
    lower = jnp.concatenate([lower, swap(lower, top)], axis=0)
    if fused:
        upper, lower, slots = lax.optimization_barrier((upper, lower, slots))
        shifted, shifted_again = shift_call(flat_in, slots)
    parts = [upper, swap(upper, top), lower, swap(lower, next_top)]
    if fused:
        parts, shifted, shifted_again = lax.optimization_barrier((parts, shifted, shifted_again))
    parts = parts + [swap(part, order[0]) for part in parts]
    few = devices // 8
    plan = []
    for core in range(2):
        base = core * 4 * few
        plan += [(4 * core, 0, base, 2 * few, 0), (4 * core + 1, 0, base + 2 * few, 2 * few, 0)]
        for part, spot in ((2, 0), (3, few)):
            plan += [
                (4 * core + part, 0, base + spot, few, cut),
                (4 * core + part, few, base + spot + 2 * few, few, cut),
            ]
    space = n_space if fused else 0
    first, qkv, mixed, prob, weights, column_rows, vec, table = window_forward_call(
        me, bands, parts, plan, order, devices, shard_rows, shifted, flat_in, slots, space
    )
    if fused:
        bands = table
    if fused:
        after_t = first
    else:
        after_t = (flat_in.astype(F32) + from_windows(first).astype(F32)).T
    counts = jnp.repeat(level_count[0], LEVELS).reshape(1, -1)
    output, grad_after, grad_branch, column_grad = column_call(
        column_rows, after_t, cotangent[0].reshape(rows_dev, model_width), counts
    )
    if not fused:
        grad_branch = to_windows(grad_branch.T)
    grad_shifted, keep, send = window_backward_call(
        me, bands, order, devices, shard_rows, slots, grad_branch, weights, vec, column_grad,
        shifted_again, qkv, mixed, prob, space
    )
    total = keep.astype(F32) + swap(send, order[0]).astype(F32)
    total, grad_shifted = lax.optimization_barrier((total, grad_shifted))
    if fused:
        input_grad = finish_call(grad_shifted, slots, grad_after)
    else:
        input_grad = grad_after.T + from_windows(grad_shifted).astype(F32)

    def fold(kept, sent, *across):
        return kept + swap(sent.astype(BF16), *across).astype(F32)

    upper = total[:, :cut]
    lower = total[:, cut:].reshape(2, 2, few, padded - cut, LANES)
    upper = fold(upper[: 2 * few], upper[2 * few :], top)
    lower = fold(lower[:, 0], lower[:, 1], next_top)
    upper, lower, input_grad = lax.optimization_barrier((upper, lower, input_grad))
    upper = fold(upper[:few], upper[few:], next_top)
    lower = fold(lower[0], lower[1], top)
    total = jnp.concatenate([upper, lower], axis=1)
    for bit in order[3:-2]:
        half = total.shape[0] // 2
        total = fold(total[:half], total[half:], bit)
    own = total[0]
    for k, across in ((1, (near,)), (2, (far,)), (3, (near, far))):
        own = fold(own, total[k], *across)
    total = own[:shard_rows]
    return (
        output.reshape(block_input.shape),
        input_grad.reshape(block_input.shape),
        total.reshape(-1),
    )


def solution(mesh):
    return jax.shard_map(
        body,
        mesh=mesh,
        in_specs=(
            P("dp", "space", None, None),
            P("dp", "space", None, None),
            P(("dp", "space")),
            P("dp", None, "space", None),
            P("dp", "space"),
            P("dp", "space"),
        ),
        out_specs=(P("dp", "space", None, None), P("dp", "space", None, None), P(("dp", "space"))),
        check_vma=False,
    )
```

```python
import functools
import math

import jax
import jax.numpy as jnp
from jax import lax
from jax.experimental import pallas as pl
from jax.experimental.pallas import tpu as pltpu
from jax.sharding import PartitionSpec as P

D = 192
HEADS = 6
HEAD_DIM = 32
FF = 768
LEVELS = 8
WIN = 72
LAT_BANDS = 20
LANES = 128
HALF = LANES // 2
KEYS = 80
SCALE = HEAD_DIM ** (-0.5)
LOG2E = math.log2(math.e)
F32 = jnp.float32
BF16 = jnp.bfloat16

norm_eps = 1e-05


def param_layout():
    return [
        ("norm1_gain", (D,)),
        ("norm1_shift", (D,)),
        ("qkv1", (D, 3 * D)),
        ("proj1", (D, D)),
        ("proj1_bias", (D,)),
        ("norm2_gain", (D,)),
        ("norm2_shift", (D,)),
        ("qkv2", (D, 3 * D)),
        ("proj2", (D, D)),
        ("proj2_bias", (D,)),
        ("norm3_gain", (D,)),
        ("norm3_shift", (D,)),
        ("mlp_in", (D, FF)),
        ("mlp_in_bias", (FF,)),
        ("mlp_out", (FF, D)),
        ("mlp_out_bias", (D,)),
        ("earth_bias", (LAT_BANDS, HEADS, WIN, WIN)),
    ]


def param_offsets():
    offsets = {}
    filled = 0
    for entry_name, entry_shape in param_layout():
        offsets[entry_name] = filled
        filled += math.prod(entry_shape)
    return offsets


OFFSET = param_offsets()
BIAS_ROW, BIAS_LANE = divmod(OFFSET["earth_bias"], LANES)
BIAS_ROWS = LAT_BANDS * HEADS * WIN
WIDE = LANES // math.gcd(WIN, LANES)
DENSE = WIN // math.gcd(WIN, LANES)
PERIODS = -(-(BIAS_ROWS // WIDE + 1) // 8) * 8
PITCH = PERIODS + 1
USED = BIAS_ROWS // WIDE
COL_LO = (OFFSET["norm2_gain"] // LANES) // 8 * 8
COL_HI = -(-BIAS_ROW // 8) * 8 + 8
BIAS_LO = BIAS_ROW // 8 * 8


def mm(left, right):
    return lax.dot_general(left, right, (((1,), (0,)), ((), ())), preferred_element_type=F32)


def mt(left, right):
    return lax.dot_general(left, right, (((1,), (1,)), ((), ())), preferred_element_type=F32)


def lane_ids(rows):
    return lax.broadcasted_iota(jnp.int32, (rows, LANES), 1)


def rows_at(start, count, stride):
    return pl.ds(start, count) if stride == 1 else pl.ds(start, count, stride=stride)


def read_matrix(dense, first_row, name, matrix):
    rows, width = dict(param_layout())[name]
    halves = width // HALF
    step = 1 + halves % 2
    count, stride = rows // step, halves * step // 2
    low = lane_ids(count) < HALF
    for part in range(step):
        for chunk in range(-(-halves // 2)):
            unit = OFFSET[name] // HALF + part * halves + 2 * chunk
            row = unit // 2 - first_row
            value = dense[rows_at(row, count, stride), :]
            if unit % 2:
                after = dense[rows_at(row + 1, count, stride), :]
                value = pltpu.roll(jnp.where(low, after, value), HALF, 1)
            matrix[chunk, rows_at(part, count, step), :] = value


def write_matrix(dense, first_row, name, matrix):
    rows, width = dict(param_layout())[name]
    halves = width // HALF
    step = 1 + halves % 2
    count, stride = rows // step, halves * step // 2
    lane = lane_ids(count)
    for part in range(step):
        piece = 0
        while piece < halves:
            unit = OFFSET[name] // HALF + part * halves + piece
            where_to = rows_at(unit // 2 - first_row, count, stride)
            chunk = piece // 2
            value = matrix[chunk, rows_at(part, count, step), :]
            if unit % 2 == piece % 2 == 0 and piece + 1 < halves:
                dense[where_to, :] = value
                piece += 2
                continue
            if unit % 2 != piece % 2:
                value = pltpu.roll(value, HALF, 1)
            mine = lane < HALF if unit % 2 == 0 else lane >= HALF
            dense[where_to, :] = jnp.where(mine, value, dense[where_to, :])
            piece += 1


def joined(matrix, width):
    chunks = [matrix[k] for k in range(-(-width // LANES))]
    return jnp.concatenate(chunks, axis=1)[:, :width]


def split_into(matrix, value):
    width = value.shape[1]
    for k in range(-(-width // LANES)):
        end = min(width, (k + 1) * LANES)
        matrix[k, :, : end - k * LANES] = value[:, k * LANES : end]


def read_vector(dense, first_row, name):
    size = dict(param_layout())[name][0]
    unit = OFFSET[name] // HALF
    row = unit // 2 - first_row
    turned = dense[row : row + 8, :].T
    pieces = []
    for k in range(size // HALF):
        spot = unit % 2 + k
        pieces.append(turned[spot % 2 * HALF : (spot % 2 + 1) * HALF, spot // 2 : spot // 2 + 1])
    return jnp.concatenate(pieces, axis=0)


def write_vector(dense, first_row, name, sums):
    size = dict(param_layout())[name][0]
    line = jnp.sum(sums.T, axis=0, keepdims=True)
    lane = lane_ids(1)
    for k in range(size // HALF):
        unit = OFFSET[name] // HALF + k
        row = unit // 2 - first_row
        if size % LANES and k == size // HALF - 1:
            tail = line[:, k * HALF :]
            piece = jnp.concatenate([tail, tail], axis=1)
        else:
            piece = line[:, k // 2 * LANES : (k // 2 + 1) * LANES]
            if unit % 2 != k % 2:
                piece = pltpu.roll(piece, HALF, 1)
        mine = lane < HALF if unit % 2 == 0 else lane >= HALF
        dense[row : row + 1, :] = jnp.where(mine, piece, dense[row : row + 1, :])


def read_bias(dense, wide):
    lane = lane_ids(PERIODS)
    for j in range(WIDE):
        row, first = divmod(BIAS_LANE + j * WIN, LANES)
        value = dense[pl.ds(BIAS_ROW + row, PERIODS, stride=DENSE), :]
        if first + WIN > LANES:
            after = dense[pl.ds(BIAS_ROW + row + 1, PERIODS, stride=DENSE), :]
            value = jnp.where(lane < first, after, value)
        if first:
            value = pltpu.roll(value, LANES - first, 1)
        wide[pl.ds(j * PITCH, PERIODS), :] = value


def wide_rows(pair, part, tile):
    line = part * WIN + tile * 8
    return pl.ds(line % WIDE * PITCH + WIN * 2 // WIDE * pair + line // WIDE, 8, stride=PITCH)


def write_bias(wide, dense, first_row):
    lane = lane_ids(PERIODS)
    for i in range(DENSE):
        begin = i * LANES - BIAS_LANE
        line = begin // WIN
        value = None
        while line * WIN < begin + LANES:
            shift = line * WIN - begin
            piece = wide[pl.ds(line % WIDE * PITCH + line // WIDE, PERIODS), :]
            if shift % LANES:
                piece = pltpu.roll(piece, shift % LANES, 1)
            value = piece if value is None else jnp.where(lane >= shift, piece, value)
            line += 1
        dense[pl.ds(BIAS_ROW - first_row + i, PERIODS, stride=DENSE), :] = value


def norm_parts(rows_in):
    mean = jnp.mean(rows_in, axis=0, keepdims=True)
    centered = rows_in - mean
    var = jnp.mean(centered * centered, axis=0, keepdims=True)
    scale = lax.rsqrt(var + norm_eps)
    return centered * scale, scale


def norm_back(grad, unit, scale, gain):
    scaled = grad * gain
    first = jnp.mean(scaled, axis=0, keepdims=True)
    second = jnp.mean(scaled * unit, axis=0, keepdims=True)
    return scale * (scaled - first - unit * second)


def lane_fold(value):
    total = value[:, :LANES]
    for k in range(1, value.shape[1] // LANES):
        total = total + value[:, k * LANES : (k + 1) * LANES]
    return total


def head_rows(h):
    return slice(h * HEAD_DIM, (h + 1) * HEAD_DIM)


def head_lanes(h):
    return slice(h * LANES, (h + 1) * LANES)


def interleave(parts):
    parts = list(parts)
    live, started = [], 0
    while live or started < len(parts):
        if started < len(parts):
            live.append(parts[started])
            started += 1
        live = [part for part in live if next(part, live) is None]


def own_column(full, bits):
    heads = []
    for h in range(HEADS):
        tiles = [full[k * LEVELS : (k + 1) * LEVELS, head_lanes(h)] for k in range(LANES // LEVELS)]
        for bit in bits:
            tiles = [jnp.where(bit, b, a) for a, b in zip(tiles[::2], tiles[1::2])]
        heads.append(tiles[0])
    return jnp.concatenate(heads, axis=1)


def all_columns(own, same):
    pair = jnp.concatenate([own, own], axis=0).astype(BF16)
    tall = jnp.concatenate([pair] * (LANES // (2 * LEVELS)), axis=0)
    return jnp.concatenate([tall[:, head_lanes(h)] * same for h in range(HEADS)], axis=1)


def blend(rows_in, weights):
    pieces = []
    for h in range(0, HEADS, 2):
        pair = slice(h * HEAD_DIM, (h + 2) * HEAD_DIM)
        both = mm(rows_in[pair], weights[:, h * LANES : (h + 2) * LANES])
        pieces += [both[:HEAD_DIM, :LANES], both[HEAD_DIM:, LANES:]]
    return jnp.concatenate(pieces, axis=0)


def gather_pairs(block, weights):
    pieces = []
    for h in range(0, HEADS, 2):
        lanes = slice(h * LANES, (h + 2) * LANES)
        pieces.append(mt(block[h * HEAD_DIM : (h + 2) * HEAD_DIM, lanes], weights[:, lanes]))
    return jnp.concatenate(pieces, axis=0)


def scatter_heads(block, rows_in):
    for h in range(HEADS):
        block[head_rows(h), head_lanes(h)] = rows_in[head_rows(h), :]


def chooser(first, slots):
    ids = lax.broadcasted_iota(jnp.int32, (PICK, slots.shape[1]), 0).astype(F32).astype(BF16)
    near = jnp.clip(slots - first, -1, PICK).astype(F32).astype(BF16)
    return jnp.where(ids == near, jnp.ones((), BF16), jnp.zeros((), BF16))


def spread_windows(rows_t):
    blank = jnp.zeros((rows_t.shape[0], LANES - WIN), rows_t.dtype)
    pieces = []
    for k in range(0, rows_t.shape[1], WIN):
        pieces += [rows_t[:, k : k + WIN], blank]
    return jnp.concatenate(pieces, axis=1)


def join_windows(rows_t):
    return jnp.concatenate(
        [rows_t[:, k : k + WIN] for k in range(0, rows_t.shape[1], LANES)], axis=1
    )


def to_slots(rows_t, slots):
    tokens = rows_t.shape[1]
    pick = jnp.concatenate([chooser(k, slots) for k in range(0, tokens, PICK)], axis=0)
    return spread_windows(mm(rows_t, pick)).astype(BF16)


def from_slots(slot_rows, slots, first, rows):
    return jnp.concatenate(
        [mt(slot_rows, chooser(first + k, slots)) for k in range(0, rows, PICK)], axis=1
    )


def call(kernel, grid, ins, outs, scratch, name, macs, limit, scalars=0):
    in_specs = [s for _, s in ins]
    spec = pltpu.PrefetchScalarGridSpec(
        num_scalar_prefetch=scalars,
        grid=grid,
        in_specs=in_specs[scalars:],
        out_specs=[s for _, _, s in outs],
        scratch_shapes=scratch,
    )
    return pl.pallas_call(
        kernel,
        grid_spec=spec,
        out_shape=[jax.ShapeDtypeStruct(shape, kind) for shape, kind, _ in outs],
        compiler_params=pltpu.CompilerParams(
            dimension_semantics=("arbitrary",) * len(grid), vmem_limit_bytes=limit << 20
        ),
        cost_estimate=pl.CostEstimate(
            flops=2 * macs,
            transcendentals=0,
            bytes_accessed=sum(a.size * a.dtype.itemsize for a, _ in ins)
            + sum(math.prod(shape) * jnp.dtype(kind).itemsize for shape, kind, _ in outs),
        ),
        name=name,
    )(*[a for a, _ in ins])


def padded_rows(rows):
    return -(-(rows + 1) // 8) * 8


def whole_block(shape):
    return pl.BlockSpec(shape, lambda *_: (0,) * len(shape))


def fixed_block(array):
    return pl.BlockSpec(
        array.shape, lambda *_: (0,) * array.ndim, pipeline_mode=pl.Buffered(buffer_count=1)
    )


SLOT_BLOCK = 2048
TIGHT_BLOCK = SLOT_BLOCK // LANES * WIN
TURNS = 12
RING = 4
PICK = 256
TOKEN_BLOCK = 768


def shift_kernel(x_ref, slots_ref, out_ref, again_ref, x_t):
    @pl.when(pl.program_id(0) == 0)
    def _():
        x_t[...] = x_ref[...].astype(F32).T.astype(BF16)

    result = to_slots(x_t[...], slots_ref[...])
    out_ref[...] = result
    again_ref[...] = result


def shift_call(tokens, slots):
    count, n = tokens.shape[0], slots.shape[1] // WIN * LANES
    return call(
        shift_kernel,
        (n // SLOT_BLOCK,),
        [
            (tokens, fixed_block(tokens)),
            (slots, pl.BlockSpec((1, TIGHT_BLOCK), lambda i: (0, i))),
        ],
        [((D, n), BF16, pl.BlockSpec((D, SLOT_BLOCK), lambda i: (0, i)))] * 2,
        [pltpu.VMEM((D, count), BF16)],
        "shift",
        D * count * n,
        24,
    )


def load_dense(me_ref, parts, plan, blocks, dense, sem, order, rows):
    copies = []
    for part, first, spot, count, row in plan:
        copies.append(
            pltpu.make_async_copy(
                parts[part].at[pl.ds(first, count)],
                blocks.at[pl.ds(spot, count), pl.ds(row, parts[part].shape[1])],
                sem,
            )
        )
    for copy in copies:
        copy.start()
    for copy in copies:
        copy.wait()
    shards = blocks.shape[0]
    for shard in range(shards):
        spot = position(me_ref[0] ^ shard, order)
        dense[shard * rows : (shard + 1) * rows, :] = blocks[spot, :rows, :].astype(F32)
    if dense.shape[0] > shards * rows:
        dense[shards * rows :, :] = jnp.zeros((dense.shape[0] - shards * rows, LANES), F32)


def position(relative, order):
    spot = 0
    for place, bit in enumerate(reversed(order)):
        spot = spot + ((relative >> bit) & 1) * (1 << place)
    return spot


def band_of(table, window, me_ref, space, steps):
    if not space:
        return table[0, window]
    each = steps * (SLOT_BLOCK // LANES) // space
    return table[window // each, me_ref[0] % space * each + window % each]


def window_forward_kernel(me_ref, band_ref, *refs, parts, plan, order, rows, steps, space):
    fused = space > 0
    ins = refs[:parts]
    refs = refs[parts:]
    if fused:
        shifted_ref, slots_ref, x_ref = refs[:3]
        refs = refs[3:]
    else:
        shifted_ref, refs = refs[0], refs[1:]
    (
        out_ref,
        qkv_ref,
        mixed_ref,
        prob_ref,
        weights_ref,
        column_ref,
        vec,
        table_ref,
        blocks,
        dense,
        wide,
        bias,
        mat,
        qkv_t,
        proj_t,
        spread,
        y_all,
        band_s,
        sem,
    ) = refs
    step = pl.program_id(0)

    @pl.when(step == 0)
    def _():
        load_dense(me_ref, ins, plan, blocks, dense, sem, order, rows)
        if fused:
            lines = []
            for source in range(space):
                shard = me_ref[0] // space * space + source
                tile = blocks[position(me_ref[0] ^ shard, order), rows // 8 * 8 : rows // 8 * 8 + 8, :]
                lines.append(tile.astype(F32)[rows % 8 : rows % 8 + 1])
            table_ref[...] = jnp.concatenate(lines, axis=0).astype(jnp.int32)
            copy = pltpu.make_async_copy(table_ref, band_s, sem)
            copy.start()
            copy.wait()
        column_ref[...] = dense[COL_LO:COL_HI, :]
        read_matrix(dense, 0, "qkv1", mat)
        weights_ref[:, : 3 * D] = joined(mat, 3 * D).astype(BF16)
        qkv_t[...] = joined(mat, 3 * D).T.astype(BF16)
        read_matrix(dense, 0, "proj1", mat)
        weights_ref[:, 3 * D :] = joined(mat, D).astype(BF16)
        proj_t[...] = joined(mat, D).T.astype(BF16)
        vec[:, 0:1] = read_vector(dense, 0, "norm1_gain")
        vec[:, 1:2] = read_vector(dense, 0, "norm1_shift")
        vec[:, 2:3] = read_vector(dense, 0, "proj1_bias")
        read_bias(dense, wide)
        blank = jnp.zeros((LANES - WIN, LANES), F32)

        def turn(k, _):
            for j in range(TURNS):
                pair, part = k * (TURNS // 2) + j // 2, j % 2
                tiles = [wide[wide_rows(pair, part, tile), :] for tile in range(WIN // 8)]
                block = jnp.concatenate(tiles + [blank], axis=0).T
                bias[k * TURNS + j, :WIN, :] = block[:WIN].astype(BF16)
            return 0

        lax.fori_loop(0, LAT_BANDS * HEADS // TURNS, turn, 0)
        bias[:, WIN:, :] = jnp.full((LAT_BANDS * HEADS, KEYS - WIN, LANES), -jnp.inf, BF16)
        spread[...] = jnp.zeros_like(spread)

    @pl.when(step < steps)
    def _():
        per_step = SLOT_BLOCK // LANES
        unit, _ = norm_parts(shifted_ref[...].astype(F32))
        normed = (unit * vec[:, 0:1] + vec[:, 1:2]).astype(BF16)
        qkv = mm(qkv_t[...], normed).astype(BF16)
        qkv_ref[...] = qkv
        blank = jnp.zeros((LANES - KEYS, HEADS * LANES), BF16)
        scores, probs, mixed = {}, {}, []
        for turn in range(per_step + 2):
            if turn < per_step:
                lanes = slice(turn * LANES, (turn + 1) * LANES)
                scatter_heads(spread.at[turn % RING], qkv[:D, lanes])
                scores[turn] = mm(qkv[D : 2 * D, lanes].T[:KEYS], spread[turn % RING])
            if 1 <= turn <= per_step:
                w = turn - 1
                table = band_s if fused else band_ref
                band = band_of(table, step * per_step + w, me_ref, space, steps)
                heads = []
                for h in range(HEADS):
                    score = scores[w][:, head_lanes(h)] * SCALE + bias[band * HEADS + h].astype(F32)
                    grown = jnp.exp(score - jnp.max(score, axis=0, keepdims=True))
                    heads.append(
                        (grown * (1.0 / jnp.sum(grown, axis=0, keepdims=True))).astype(BF16)
                    )
                probs[w] = jnp.concatenate(heads, axis=1)
                prob_ref[w] = probs[w]
            if turn >= 2:
                w = turn - 2
                tall = jnp.concatenate([probs[w], blank], axis=0)
                mixed.append(blend(qkv[2 * D :, w * LANES : (w + 1) * LANES], tall))
        mixed = jnp.concatenate(mixed, axis=1).astype(BF16)
        mixed_ref[...] = mixed
        result = mm(proj_t[...], mixed) + vec[:, 2:3]
        if fused:
            spot = pl.ds(pl.multiple_of(step * TIGHT_BLOCK, TIGHT_BLOCK), TIGHT_BLOCK)
            y_all[:, spot] = join_windows(result).astype(BF16)
        else:
            out_ref[...] = result.astype(BF16)

    if fused:

        @pl.when(step >= steps)
        def _():
            branch = from_slots(
                y_all[...], slots_ref[...], (step - steps) * TOKEN_BLOCK, TOKEN_BLOCK
            )
            out_ref[...] = x_ref[...].astype(F32).T + branch


def window_forward_call(me, bands, parts, plan, order, shards, rows, shifted, tokens, slots, space):
    fused = space > 0
    n = shifted.shape[1]
    steps = n // SLOT_BLOCK
    per_step = SLOT_BLOCK // LANES
    padded = padded_rows(rows)
    flat_rows = max(shards * rows, BIAS_ROW + DENSE * PERIODS + 16)
    slot_block = lambda r: pl.BlockSpec((r, SLOT_BLOCK), lambda i, *_: (0, jnp.minimum(i, steps - 1)))
    ins = [(me, None), (bands, None)]
    ins += [(p, pl.BlockSpec(memory_space=pl.ANY)) for p in parts]
    ins += [(shifted, slot_block(D))]
    if fused:
        count = tokens.shape[0]
        late = lambda i: jnp.maximum(i - steps, 0)
        ins += [
            (slots, fixed_block(slots)),
            (tokens, pl.BlockSpec((TOKEN_BLOCK, D), lambda i, *_: (late(i), 0))),
        ]
        first = ((D, count), F32, pl.BlockSpec((D, TOKEN_BLOCK), lambda i, *_: (0, late(i))))
        grid = steps + count // TOKEN_BLOCK
    else:
        first = ((D, n), BF16, slot_block(D))
        grid = steps
    outs = [
        first,
        ((3 * D, n), BF16, slot_block(3 * D)),
        ((D, n), BF16, slot_block(D)),
        (
            (n // LANES, KEYS, HEADS * LANES),
            BF16,
            pl.BlockSpec(
                (per_step, KEYS, HEADS * LANES), lambda i, *_: (jnp.minimum(i, steps - 1), 0, 0)
            ),
        ),
        ((D, 4 * D), BF16, whole_block((D, 4 * D))),
        ((COL_HI - COL_LO, LANES), F32, whole_block((COL_HI - COL_LO, LANES))),
        ((D, LANES), F32, whole_block((D, LANES))),
        ((max(space, 1), LANES), jnp.int32, whole_block((max(space, 1), LANES))),
    ]
    scratch = [
        pltpu.VMEM((shards, padded, LANES), BF16),
        pltpu.VMEM((flat_rows, LANES), F32),
        pltpu.VMEM((WIDE * PITCH, LANES), F32),
        pltpu.VMEM((LAT_BANDS * HEADS, KEYS, LANES), BF16),
        pltpu.VMEM((5, D, LANES), F32),
        pltpu.VMEM((3 * D, D), BF16),
        pltpu.VMEM((D, D), BF16),
        pltpu.VMEM((RING, D, HEADS * LANES), BF16),
        pltpu.VMEM((D, n // LANES * WIN), BF16),
        pltpu.SMEM((max(space, 1), LANES), jnp.int32),
        pltpu.SemaphoreType.DMA,
    ]
    kernel = functools.partial(
        window_forward_kernel,
        parts=len(parts),
        plan=plan,
        order=order,
        rows=rows,
        steps=steps,
        space=space,
    )
    return call(kernel, (grid,), ins, outs, scratch, "window_forward", 12 * D * D * n, 36, scalars=2)


COLUMN_BLOCK = 768
COLUMN_PART = 768
COLUMN_VECTORS = (
    "norm2_gain",
    "norm2_shift",
    "proj2_bias",
    "norm3_gain",
    "norm3_shift",
    "mlp_out_bias",
)
COLUMN_MATRICES = ("qkv2", "proj2", "mlp_in", "mlp_out")


def column_kernel(
    dense,
    x_ref,
    cot_ref,
    count_ref,
    out_ref,
    after_ref,
    branch_ref,
    grad_ref,
    mat,
    tall,
    w_qkv,
    w_proj,
    w_in,
    w_out,
    t_qkv,
    t_proj,
    t_in,
    t_out,
    vec,
    fvec,
    grad_qkv,
    grad_proj,
    grad_in,
    grad_out,
    sums,
    fsums,
    spread,
):
    step = pl.program_id(0)

    @pl.when(step == 0)
    def _():
        for name, plain, turned in (
            ("qkv2", w_qkv, t_qkv),
            ("proj2", w_proj, t_proj),
            ("mlp_in", w_in, t_in),
            ("mlp_out", w_out, t_out),
        ):
            rows, width = plain.shape
            source = tall if rows == FF else mat
            read_matrix(dense, COL_LO, name, source)
            plain[...] = joined(source, width).astype(BF16)
            turned[...] = joined(source, width).T.astype(BF16)
        for k, name in enumerate(COLUMN_VECTORS):
            vec[:, k : k + 1] = read_vector(dense, COL_LO, name)
        fvec[:, 0:1] = read_vector(dense, COL_LO, "mlp_in_bias")
        sums[...] = jnp.zeros_like(sums)
        fsums[...] = jnp.zeros_like(fsums)
        for grad in (grad_qkv, grad_proj, grad_in, grad_out):
            grad[...] = jnp.zeros_like(grad)
        spread[...] = jnp.zeros_like(spread)

    gain2, shift2, bias2, gain3, shift3, bias_out = [vec[:, k : k + 1] for k in range(6)]
    key_id = lax.broadcasted_iota(jnp.int32, (LANES, LANES), 0)
    query_id = lax.broadcasted_iota(jnp.int32, (LANES, LANES), 1)
    same = jnp.where(key_id // LEVELS == query_id // LEVELS, 1.0, 0.0).astype(BF16)
    column = lax.broadcasted_iota(jnp.int32, (LEVELS, LANES), 1) // LEVELS
    bits = [(column >> k) & 1 == 1 for k in range(4)]
    level = lax.broadcasted_iota(jnp.int32, (LEVELS, LANES), 0)
    groups = COLUMN_PART // LANES

    def part_steps(part):
        here = slice(part * COLUMN_PART, (part + 1) * COLUMN_PART)
        x = x_ref[:, here]
        unit2, scale2 = norm_parts(x)
        n2 = (unit2 * gain2 + shift2).astype(BF16)
        yield
        qkv = mm(t_qkv[...], n2).astype(BF16)
        yield
        scores = []
        for g in range(groups):
            lanes = slice(g * LANES, (g + 1) * LANES)
            scatter_heads(spread.at[0, part * groups + g], qkv[:D, lanes])
            scores.append(own_column(mm(qkv[D : 2 * D, lanes].T, spread[0, part * groups + g]), bits))
        yield
        probs, tall_probs = [], []
        for g in range(groups):
            begin = part * COLUMN_PART + g * LANES
            valid = level < count_ref[:, begin : begin + LANES]
            score = jnp.where(jnp.concatenate([valid] * HEADS, axis=1), scores[g] * SCALE, -jnp.inf)
            grown = jnp.exp(score - jnp.max(score, axis=0, keepdims=True))
            prob = grown * (1.0 / jnp.sum(grown, axis=0, keepdims=True))
            probs.append(prob)
            tall_probs.append(all_columns(prob, same))
        yield
        mixed = [
            blend(qkv[2 * D :, g * LANES : (g + 1) * LANES], tall_probs[g]) for g in range(groups)
        ]
        mixed = jnp.concatenate(mixed, axis=1).astype(BF16)
        projected = mm(t_proj[...], mixed)
        yield
        middle = x + (projected + bias2)
        unit3, scale3 = norm_parts(middle)
        n3 = (unit3 * gain3 + shift3).astype(BF16)
        yield
        pre = mm(t_in[...], n3)
        cot = cot_ref[here, :].astype(F32).T
        cot_bf = cot.astype(BF16)
        dact = mm(w_out[...], cot_bf)
        yield
        pre = pre + fvec[:, 0:1]
        root = math.sqrt(2.0 / math.pi)
        square = pre * pre
        share = 0.5 + 0.5 * jnp.tanh(pre * (root + (root * 0.044715) * square))
        act = pre * share
        slope = share + act * (1.0 - share) * (2.0 * root + (6.0 * root * 0.044715) * square)
        act = act.astype(BF16)
        dpre = (dact * slope).astype(BF16)
        yield
        output = middle + (mm(t_out[...], act) + bias_out)
        out_ref[here, :] = output.T.astype(BF16)
        dn3 = mm(w_in[...], dpre)
        grad_out[...] += mt(act, cot_bf)
        grad_in[...] += mt(n3, dpre)
        yield
        dmiddle = cot + norm_back(dn3, unit3, scale3, gain3)
        dattn = dmiddle.astype(BF16)
        sums[2] += lane_fold(dattn.astype(F32))
        sums[3] += lane_fold(dn3 * unit3)
        sums[4] += lane_fold(dn3)
        sums[5] += lane_fold(cot_bf.astype(F32))
        fsums[...] += lane_fold(dpre.astype(F32))
        yield
        dmixed = mm(w_proj[...], dattn).astype(BF16)
        grad_proj[...] += mt(mixed, dattn)
        dprobs = []
        for g in range(groups):
            lanes = slice(g * LANES, (g + 1) * LANES)
            scatter_heads(spread.at[1, part * groups + g], dmixed[:, lanes])
            dprobs.append(own_column(mm(qkv[2 * D :, lanes].T, spread[1, part * groups + g]), bits))
        yield
        dscores = []
        for prob, dprob in zip(probs, dprobs):
            dscore = prob * (dprob - jnp.sum(prob * dprob, axis=0, keepdims=True))
            dscores.append(all_columns(dscore, same))
        yield
        dq, dk, dv = [], [], []
        for g in range(groups):
            dq.append(blend(qkv[D : 2 * D, g * LANES : (g + 1) * LANES], dscores[g]) * SCALE)
            dk.append(gather_pairs(spread.at[0, part * groups + g], dscores[g]) * SCALE)
            dv.append(gather_pairs(spread.at[1, part * groups + g], tall_probs[g]))
        dqkv = [jnp.concatenate(d, axis=1) for d in (dq, dk, dv)]
        dqkv = jnp.concatenate(dqkv, axis=0).astype(BF16)
        dn2 = mm(w_qkv[...], dqkv)
        grad_qkv[...] += mt(n2, dqkv)
        yield
        dafter = dmiddle + norm_back(dn2, unit2, scale2, gain2)
        after_ref[:, here] = dafter
        branch_ref[:, here] = dafter.astype(BF16)
        sums[0] += lane_fold(dn2 * unit2)
        sums[1] += lane_fold(dn2)

    interleave([part_steps(part) for part in range(COLUMN_BLOCK // COLUMN_PART)])

    @pl.when(step == pl.num_programs(0) - 1)
    def _():
        grad_ref[...] = jnp.zeros_like(grad_ref)
        split_into(mat, grad_qkv[...])
        write_matrix(grad_ref, COL_LO, "qkv2", mat)
        split_into(mat, grad_proj[...])
        write_matrix(grad_ref, COL_LO, "proj2", mat)
        split_into(mat, grad_in[...])
        write_matrix(grad_ref, COL_LO, "mlp_in", mat)
        split_into(tall, grad_out[...])
        write_matrix(grad_ref, COL_LO, "mlp_out", tall)
        for k, name in enumerate(COLUMN_VECTORS):
            write_vector(grad_ref, COL_LO, name, sums[k])
        write_vector(grad_ref, COL_LO, "mlp_in_bias", fsums[...])


def column_call(dense, after_t, cotangent, counts):
    n = after_t.shape[1]
    feature = lambda r: pl.BlockSpec((r, COLUMN_BLOCK), lambda i: (0, i))
    token = pl.BlockSpec((COLUMN_BLOCK, D), lambda i: (i, 0))
    return call(
        column_kernel,
        (n // COLUMN_BLOCK,),
        [
            (dense, fixed_block(dense)),
            (after_t, feature(D)),
            (cotangent, token),
            (counts, feature(1)),
        ],
        [
            ((n, D), BF16, token),
            ((D, n), F32, feature(D)),
            ((D, n), BF16, feature(D)),
            (dense.shape, F32, whole_block(dense.shape)),
        ],
        [
            pltpu.VMEM((FF // LANES, D, LANES), F32),
            pltpu.VMEM((2, FF, LANES), F32),
            pltpu.VMEM((D, 3 * D), BF16),
            pltpu.VMEM((D, D), BF16),
            pltpu.VMEM((D, FF), BF16),
            pltpu.VMEM((FF, D), BF16),
            pltpu.VMEM((3 * D, D), BF16),
            pltpu.VMEM((D, D), BF16),
            pltpu.VMEM((FF, D), BF16),
            pltpu.VMEM((D, FF), BF16),
            pltpu.VMEM((D, LANES), F32),
            pltpu.VMEM((FF, LANES), F32),
            pltpu.VMEM((D, 3 * D), F32),
            pltpu.VMEM((D, D), F32),
            pltpu.VMEM((D, FF), F32),
            pltpu.VMEM((FF, D), F32),
            pltpu.VMEM((6, D, LANES), F32),
            pltpu.VMEM((FF, LANES), F32),
            pltpu.VMEM((2, COLUMN_BLOCK // LANES, D, HEADS * LANES), BF16),
        ],
        "column",
        40 * D * D * n,
        40,
    )


def window_backward_kernel(me_ref, band_ref, *refs, order, shard_rows, space):
    fused = space > 0
    if fused:
        slots_ref, refs = refs[0], refs[1:]
    (
        grad_ref,
        weights_ref,
        vec,
        column_ref,
        shifted_ref,
        qkv_ref,
        mixed_ref,
        prob_ref,
        out_ref,
        keep_ref,
        send_ref,
        total,
        wide,
        dense,
        mat,
        blocks,
        spread,
        grad_qkv,
        grad_proj,
        sums,
        sem,
    ) = refs
    step = pl.program_id(0)
    per_step = SLOT_BLOCK // LANES

    @pl.when(step == 0)
    def _():
        total[...] = jnp.zeros_like(total)
        sums[...] = jnp.zeros_like(sums)
        grad_qkv[...] = jnp.zeros_like(grad_qkv)
        grad_proj[...] = jnp.zeros_like(grad_proj)
        spread[...] = jnp.zeros_like(spread)

    if fused:
        grad = to_slots(grad_ref[...], slots_ref[...])
    else:
        grad = grad_ref[...]
    grad_proj[...] += mt(mixed_ref[...], grad)
    dmixed = mm(weights_ref[:, 3 * D :], grad).astype(BF16)
    qkv = qkv_ref[...]
    blank = jnp.zeros((LANES - KEYS, HEADS * LANES), BF16)
    dq, dk, dv, dprobs, dscores = [], [], [], {}, {}
    for turn in range(per_step + 2):
        if turn < per_step:
            lanes = slice(turn * LANES, (turn + 1) * LANES)
            scatter_heads(spread.at[0, turn % RING], qkv[:D, lanes])
            scatter_heads(spread.at[1, turn % RING], dmixed[:, lanes])
            dprobs[turn] = mm(qkv[2 * D :, lanes].T[:KEYS], spread[1, turn % RING])
        if 1 <= turn <= per_step:
            w = turn - 1
            heads = []
            for h in range(HEADS):
                prob = prob_ref[w, :, head_lanes(h)].astype(F32)
                dprob = dprobs[w][:, head_lanes(h)]
                heads.append(
                    (prob * (dprob - jnp.sum(prob * dprob, axis=0, keepdims=True))).astype(BF16)
                )
            dscores[w] = jnp.concatenate(heads, axis=1)
            band = band_of(band_ref, step * per_step + w, me_ref, space, pl.num_programs(0))
            for h in range(HEADS):
                spot = pl.ds(pl.multiple_of((band * HEADS + h) * KEYS, 8), KEYS)
                total[spot, :] += heads[h].astype(F32)
        if turn >= 2:
            w = turn - 2
            tall = jnp.concatenate([dscores[w], blank], axis=0)
            dq.append(blend(qkv[D : 2 * D, w * LANES : (w + 1) * LANES], tall) * SCALE)
            dk.append(gather_pairs(spread.at[0, w % RING], tall) * SCALE)
            tall = jnp.concatenate([prob_ref[w], blank], axis=0)
            dv.append(gather_pairs(spread.at[1, w % RING], tall))
    dqkv = jnp.concatenate([jnp.concatenate(d, axis=1) for d in (dq, dk, dv)], axis=0).astype(BF16)
    unit, scale = norm_parts(shifted_ref[...].astype(F32))
    grad_qkv[...] += mt((unit * vec[:, 0:1] + vec[:, 1:2]).astype(BF16), dqkv)
    dnormed = mm(weights_ref[:, : 3 * D], dqkv)
    dshifted = norm_back(dnormed, unit, scale, vec[:, 0:1])
    out_ref[...] = (join_windows(dshifted) if fused else dshifted).astype(BF16)
    for k, value in enumerate((dnormed * unit, dnormed, grad.astype(F32))):
        sums[k] += lane_fold(value)

    @pl.when(step == pl.num_programs(0) - 1)
    def _():
        for j in range(WIDE):
            wide[j * PITCH + USED : (j + 1) * PITCH, :] = jnp.zeros((PITCH - USED, LANES), F32)
        blank = jnp.zeros((WIN, LANES - KEYS), F32)

        def turn(k, _):
            for j in range(TURNS):
                pair, part = k * (TURNS // 2) + j // 2, j % 2
                spot = pl.ds(pl.multiple_of((k * TURNS + j) * KEYS, 8), KEYS)
                block = jnp.concatenate([total[spot, :].T[:WIN], blank], axis=1)
                for tile in range(WIN // 8):
                    wide[wide_rows(pair, part, tile), :] = block[tile * 8 : tile * 8 + 8]
            return 0

        lax.fori_loop(0, LAT_BANDS * HEADS // TURNS, turn, 0)
        dense[:COL_LO, :] = jnp.zeros((COL_LO, LANES), F32)
        write_bias(wide, dense, 0)
        covered = BIAS_ROW + DENSE * PERIODS
        dense[covered:, :] = jnp.zeros((dense.shape[0] - covered, LANES), F32)
        both = column_ref[COL_HI - COL_LO - 16 :, :]
        rows = lax.broadcasted_iota(jnp.int32, both.shape, 0) + (COL_HI - 16)
        lane = lane_ids(16)
        start = rows * LANES + lane < OFFSET["earth_bias"]
        dense[COL_LO : COL_HI - 16, :] = column_ref[: COL_HI - COL_LO - 16, :]
        dense[COL_HI - 16 : COL_HI, :] = jnp.where(start, both, dense[COL_HI - 16 : COL_HI, :])
        split_into(mat, grad_qkv[...])
        write_matrix(dense, 0, "qkv1", mat)
        split_into(mat, grad_proj[...])
        write_matrix(dense, 0, "proj1", mat)
        for k, name in enumerate(("norm1_gain", "norm1_shift", "proj1_bias")):
            write_vector(dense, 0, name, sums[k])
        shards, rows = blocks.shape[0], shard_rows
        for shard in range(shards):
            spot = position(me_ref[0] ^ shard, order)
            blocks[spot, :rows, :] = dense[shard * rows : (shard + 1) * rows, :].astype(BF16)
        first = pltpu.make_async_copy(blocks.at[pl.ds(0, shards // 2)], keep_ref, sem.at[0])
        second = pltpu.make_async_copy(
            blocks.at[pl.ds(shards // 2, shards // 2)], send_ref, sem.at[1]
        )
        first.start()
        second.start()
        first.wait()
        second.wait()


def window_backward_call(
    me, bands, order, shards, rows, slots, grad, weights, vec, column_grad, shifted, qkv, mixed, prob, space
):
    fused = space > 0
    padded = padded_rows(rows)
    n = shifted.shape[1]
    per_step = SLOT_BLOCK // LANES
    slot_block = lambda r: pl.BlockSpec((r, SLOT_BLOCK), lambda i, *_: (0, i))
    ins = [(me, None), (bands, None)]
    if fused:
        tight = pl.BlockSpec((1, TIGHT_BLOCK), lambda i, *_: (0, i))
        ins += [(slots, tight), (grad, fixed_block(grad))]
    else:
        ins += [(grad, slot_block(D))]
    ins += [
        (weights, fixed_block(weights)),
        (vec, fixed_block(vec)),
        (column_grad, fixed_block(column_grad)),
        (shifted, slot_block(D)),
        (qkv, slot_block(3 * D)),
        (mixed, slot_block(D)),
        (
            prob,
            pl.BlockSpec((per_step, KEYS, HEADS * LANES), lambda i, *_: (i, 0, 0)),
        ),
    ]
    flat_rows = max(shards * rows, BIAS_ROW + DENSE * PERIODS + 16)
    if fused:
        tight = pl.BlockSpec((D, TIGHT_BLOCK), lambda i, *_: (0, i))
        first = ((D, n // LANES * WIN), BF16, tight)
    else:
        first = ((D, n), BF16, slot_block(D))
    outs = [
        first,
        ((shards // 2, padded, LANES), BF16, pl.BlockSpec(memory_space=pl.ANY)),
        ((shards // 2, padded, LANES), BF16, pl.BlockSpec(memory_space=pl.ANY)),
    ]
    scratch = [
        pltpu.VMEM((LAT_BANDS * HEADS * KEYS, LANES), F32),
        pltpu.VMEM((WIDE * PITCH, LANES), F32),
        pltpu.VMEM((flat_rows, LANES), F32),
        pltpu.VMEM((5, D, LANES), F32),
        pltpu.VMEM((shards, padded, LANES), BF16),
        pltpu.VMEM((2, RING, D, HEADS * LANES), BF16),
        pltpu.VMEM((D, 3 * D), F32),
        pltpu.VMEM((D, D), F32),
        pltpu.VMEM((3, D, LANES), F32),
        pltpu.SemaphoreType.DMA((2,)),
    ]
    kernel = functools.partial(
        window_backward_kernel, order=order, shard_rows=rows, space=space
    )
    return call(kernel, (n // SLOT_BLOCK,), ins, outs, scratch, "window_backward", 24 * D * D * n, 40, scalars=2)


def finish_kernel(shift_ref, slots_ref, after_ref, out_ref):
    first = pl.program_id(0) * TOKEN_BLOCK
    back = from_slots(shift_ref[...], slots_ref[...], first, TOKEN_BLOCK)
    out_ref[...] = (after_ref[...] + back).T


def finish_call(grad_shifted, slots, after_t):
    n = after_t.shape[1]
    return call(
        finish_kernel,
        (n // TOKEN_BLOCK,),
        [
            (grad_shifted, fixed_block(grad_shifted)),
            (slots, fixed_block(slots)),
            (after_t, pl.BlockSpec((D, TOKEN_BLOCK), lambda i: (0, i))),
        ],
        [((n, D), F32, pl.BlockSpec((TOKEN_BLOCK, D), lambda i: (i, 0)))],
        [],
        "finish",
        D * n * slots.shape[1],
        24,
    )[0]


def body(block_input, cotangent, params, send_rows, window_band, level_count):
    model_width = block_input.shape[-1]
    rows_dev = block_input.shape[1] * block_input.shape[2]
    n_space, per_peer = send_rows.shape[1], send_rows.shape[3]
    devices = lax.axis_size(("dp", "space"))
    group = WIN // math.gcd(per_peer, WIN)
    if n_space % group:
        group = n_space
    fused = group == 1
    dest = n_space // group
    per_dest = group * per_peer // WIN
    member_groups = [[first + k for k in range(group)] for first in range(0, n_space, group)]
    place = lax.axis_index("space")
    index = lax.axis_index(("dp", "space"))
    me = index.astype(jnp.int32).reshape(1)
    bits = devices.bit_length() - 1
    order = [0] + list(range(bits - 1, 0, -1))

    def swap(value, *across):
        flip = sum(1 << bit for bit in across)
        return lax.ppermute(value, ("dp", "space"), [(k, k ^ flip) for k in range(devices)])

    def exchange(value):
        return lax.all_to_all(
            value, "space", split_axis=0, concat_axis=0, tiled=True, axis_index_groups=member_groups
        )

    def to_windows(rows):
        moved = exchange(rows[route_flat]).reshape(group, dest, per_peer, model_width)
        windows = moved.transpose(1, 0, 2, 3).reshape(-1, WIN, model_width)
        windows = jnp.pad(windows, ((0, 0), (0, LANES - WIN), (0, 0)))
        return windows.reshape(-1, model_width).T

    def from_windows(rows_t):
        rows = rows_t.T.reshape(-1, LANES, model_width)[:, :WIN]
        moved = rows.reshape(dest, group, per_peer, model_width).transpose(1, 0, 2, 3)
        rows = exchange(moved.reshape(rows_dev, model_width))
        return jnp.zeros((rows_dev, model_width), rows.dtype).at[route_flat].set(rows)

    flat_in = block_input[0].reshape(rows_dev, model_width)
    routes = send_rows[0, :, 0, :]
    route_flat = routes.reshape(-1)
    slots = routes.reshape(1, -1)
    if fused:
        bands = jnp.zeros((1, LANES), jnp.int32)
    else:
        all_bands = lax.all_gather(window_band[0], "space", axis=0)
        bands = lax.dynamic_slice(
            all_bands, ((place % group) * dest, (place // group) * per_dest), (dest, per_dest)
        ).reshape(1, -1)
        shifted = shifted_again = to_windows(flat_in)

    shard_rows = params.shape[0] // LANES
    padded = padded_rows(shard_rows)
    band_row = jnp.pad(window_band[0], (0, LANES - window_band.shape[1])).astype(BF16)
    own_rows = jnp.pad(params.reshape(shard_rows, LANES), ((0, padded - shard_rows), (0, 0)))
    row_id = lax.broadcasted_iota(jnp.int32, (padded, 1), 0)
    held = jnp.where(row_id == shard_rows, band_row[None, :], own_rows.astype(BF16))[None]
    near, far = order[-1], order[-2]
    direct = [swap(held, near), swap(held, far), swap(held, near, far)]
    held = jnp.concatenate([held] + direct, axis=0)
    for bit in reversed(order[3:-2]):
        held = jnp.concatenate([held, swap(held, bit)], axis=0)
    top, next_top = order[1], order[2]
    cut = padded // 16 * 8
    upper, lower = held[:, :cut], held[:, cut:]
    upper = jnp.concatenate([upper, swap(upper, next_top)], axis=0)
    lower = jnp.concatenate([lower, swap(lower, top)], axis=0)
    if fused:
        upper, lower, slots = lax.optimization_barrier((upper, lower, slots))
        shifted, shifted_again = shift_call(flat_in, slots)
    parts = [upper, swap(upper, top), lower, swap(lower, next_top)]
    if fused:
        parts, shifted, shifted_again = lax.optimization_barrier((parts, shifted, shifted_again))
    parts = parts + [swap(part, order[0]) for part in parts]
    few = devices // 8
    plan = []
    for core in range(2):
        base = core * 4 * few
        plan += [(4 * core, 0, base, 2 * few, 0), (4 * core + 1, 0, base + 2 * few, 2 * few, 0)]
        for part, spot in ((2, 0), (3, few)):
            plan += [
                (4 * core + part, 0, base + spot, few, cut),
                (4 * core + part, few, base + spot + 2 * few, few, cut),
            ]
    space = n_space if fused else 0
    first, qkv, mixed, prob, weights, column_rows, vec, table = window_forward_call(
        me, bands, parts, plan, order, devices, shard_rows, shifted, flat_in, slots, space
    )
    if fused:
        bands = table
    if fused:
        after_t = first
    else:
        after_t = (flat_in.astype(F32) + from_windows(first).astype(F32)).T
    counts = jnp.repeat(level_count[0], LEVELS).reshape(1, -1)
    output, grad_after, grad_branch, column_grad = column_call(
        column_rows, after_t, cotangent[0].reshape(rows_dev, model_width), counts
    )
    if not fused:
        grad_branch = to_windows(grad_branch.T)
    grad_shifted, keep, send = window_backward_call(
        me, bands, order, devices, shard_rows, slots, grad_branch, weights, vec, column_grad,
        shifted_again, qkv, mixed, prob, space
    )
    total = keep.astype(F32) + swap(send, order[0]).astype(F32)
    total, grad_shifted = lax.optimization_barrier((total, grad_shifted))
    if fused:
        input_grad = finish_call(grad_shifted, slots, grad_after)
    else:
        input_grad = grad_after.T + from_windows(grad_shifted).astype(F32)

    def fold(kept, sent, *across):
        return kept + swap(sent.astype(BF16), *across).astype(F32)

    upper = total[:, :cut]
    lower = total[:, cut:].reshape(2, 2, few, padded - cut, LANES)
    upper = fold(upper[: 2 * few], upper[2 * few :], top)
    lower = fold(lower[:, 0], lower[:, 1], next_top)
    upper, lower, input_grad = lax.optimization_barrier((upper, lower, input_grad))
    upper = fold(upper[:few], upper[few:], next_top)
    lower = fold(lower[0], lower[1], top)
    total = jnp.concatenate([upper, lower], axis=1)
    for bit in order[3:-2]:
        half = total.shape[0] // 2
        total = fold(total[:half], total[half:], bit)
    own = total[0]
    for k, across in ((1, (near,)), (2, (far,)), (3, (near, far))):
        own = fold(own, total[k], *across)
    total = own[:shard_rows]
    return (
        output.reshape(block_input.shape),
        input_grad.reshape(block_input.shape),
        total.reshape(-1),
    )


def solution(mesh):
    return jax.shard_map(
        body,
        mesh=mesh,
        in_specs=(
            P("dp", "space", None, None),
            P("dp", "space", None, None),
            P(("dp", "space")),
            P("dp", None, "space", None),
            P("dp", "space"),
            P("dp", "space"),
        ),
        out_specs=(P("dp", "space", None, None), P("dp", "space", None, None), P(("dp", "space"))),
        check_vma=False,
    )
```

```python
import functools
import math

import jax
import jax.numpy as jnp
from jax import lax
from jax.experimental import pallas as pl
from jax.experimental.pallas import tpu as pltpu
from jax.sharding import PartitionSpec as P

D = 192
HEADS = 6
HEAD_DIM = 32
FF = 768
LEVELS = 8
WIN = 72
LAT_BANDS = 20
LANES = 128
HALF = LANES // 2
KEYS = 80
SCALE = HEAD_DIM ** (-0.5)
LOG2E = math.log2(math.e)
F32 = jnp.float32
BF16 = jnp.bfloat16

norm_eps = 1e-05


def param_layout():
    return [
        ("norm1_gain", (D,)),
        ("norm1_shift", (D,)),
        ("qkv1", (D, 3 * D)),
        ("proj1", (D, D)),
        ("proj1_bias", (D,)),
        ("norm2_gain", (D,)),
        ("norm2_shift", (D,)),
        ("qkv2", (D, 3 * D)),
        ("proj2", (D, D)),
        ("proj2_bias", (D,)),
        ("norm3_gain", (D,)),
        ("norm3_shift", (D,)),
        ("mlp_in", (D, FF)),
        ("mlp_in_bias", (FF,)),
        ("mlp_out", (FF, D)),
        ("mlp_out_bias", (D,)),
        ("earth_bias", (LAT_BANDS, HEADS, WIN, WIN)),
    ]


def param_offsets():
    offsets = {}
    filled = 0
    for entry_name, entry_shape in param_layout():
        offsets[entry_name] = filled
        filled += math.prod(entry_shape)
    return offsets


OFFSET = param_offsets()
BIAS_ROW, BIAS_LANE = divmod(OFFSET["earth_bias"], LANES)
BIAS_ROWS = LAT_BANDS * HEADS * WIN
WIDE = LANES // math.gcd(WIN, LANES)
DENSE = WIN // math.gcd(WIN, LANES)
PERIODS = -(-(BIAS_ROWS // WIDE + 1) // 8) * 8
PITCH = PERIODS + 1
USED = BIAS_ROWS // WIDE
COL_LO = (OFFSET["norm2_gain"] // LANES) // 8 * 8
COL_HI = -(-BIAS_ROW // 8) * 8 + 8
BIAS_LO = BIAS_ROW // 8 * 8


def mm(left, right):
    return lax.dot_general(left, right, (((1,), (0,)), ((), ())), preferred_element_type=F32)


def mt(left, right):
    return lax.dot_general(left, right, (((1,), (1,)), ((), ())), preferred_element_type=F32)


def lane_ids(rows):
    return lax.broadcasted_iota(jnp.int32, (rows, LANES), 1)


def rows_at(start, count, stride):
    return pl.ds(start, count) if stride == 1 else pl.ds(start, count, stride=stride)


def read_matrix(dense, first_row, name, matrix):
    rows, width = dict(param_layout())[name]
    halves = width // HALF
    step = 1 + halves % 2
    count, stride = rows // step, halves * step // 2
    low = lane_ids(count) < HALF
    for part in range(step):
        for chunk in range(-(-halves // 2)):
            unit = OFFSET[name] // HALF + part * halves + 2 * chunk
            row = unit // 2 - first_row
            value = dense[rows_at(row, count, stride), :]
            if unit % 2:
                after = dense[rows_at(row + 1, count, stride), :]
                value = pltpu.roll(jnp.where(low, after, value), HALF, 1)
            matrix[chunk, rows_at(part, count, step), :] = value


def write_matrix(dense, first_row, name, matrix):
    rows, width = dict(param_layout())[name]
    halves = width // HALF
    step = 1 + halves % 2
    count, stride = rows // step, halves * step // 2
    lane = lane_ids(count)
    for part in range(step):
        piece = 0
        while piece < halves:
            unit = OFFSET[name] // HALF + part * halves + piece
            where_to = rows_at(unit // 2 - first_row, count, stride)
            chunk = piece // 2
            value = matrix[chunk, rows_at(part, count, step), :]
            if unit % 2 == piece % 2 == 0 and piece + 1 < halves:
                dense[where_to, :] = value
                piece += 2
                continue
            if unit % 2 != piece % 2:
                value = pltpu.roll(value, HALF, 1)
            mine = lane < HALF if unit % 2 == 0 else lane >= HALF
            dense[where_to, :] = jnp.where(mine, value, dense[where_to, :])
            piece += 1


def joined(matrix, width):
    chunks = [matrix[k] for k in range(-(-width // LANES))]
    return jnp.concatenate(chunks, axis=1)[:, :width]


def split_into(matrix, value):
    width = value.shape[1]
    for k in range(-(-width // LANES)):
        end = min(width, (k + 1) * LANES)
        matrix[k, :, : end - k * LANES] = value[:, k * LANES : end]


def read_vector(dense, first_row, name):
    size = dict(param_layout())[name][0]
    unit = OFFSET[name] // HALF
    row = unit // 2 - first_row
    turned = dense[row : row + 8, :].T
    pieces = []
    for k in range(size // HALF):
        spot = unit % 2 + k
        pieces.append(turned[spot % 2 * HALF : (spot % 2 + 1) * HALF, spot // 2 : spot // 2 + 1])
    return jnp.concatenate(pieces, axis=0)


def write_vector(dense, first_row, name, sums):
    size = dict(param_layout())[name][0]
    line = jnp.sum(sums.T, axis=0, keepdims=True)
    lane = lane_ids(1)
    for k in range(size // HALF):
        unit = OFFSET[name] // HALF + k
        row = unit // 2 - first_row
        if size % LANES and k == size // HALF - 1:
            tail = line[:, k * HALF :]
            piece = jnp.concatenate([tail, tail], axis=1)
        else:
            piece = line[:, k // 2 * LANES : (k // 2 + 1) * LANES]
            if unit % 2 != k % 2:
                piece = pltpu.roll(piece, HALF, 1)
        mine = lane < HALF if unit % 2 == 0 else lane >= HALF
        dense[row : row + 1, :] = jnp.where(mine, piece, dense[row : row + 1, :])


def read_bias(dense, wide):
    lane = lane_ids(PERIODS)
    for j in range(WIDE):
        row, first = divmod(BIAS_LANE + j * WIN, LANES)
        value = dense[pl.ds(BIAS_ROW + row, PERIODS, stride=DENSE), :]
        if first + WIN > LANES:
            after = dense[pl.ds(BIAS_ROW + row + 1, PERIODS, stride=DENSE), :]
            value = jnp.where(lane < first, after, value)
        if first:
            value = pltpu.roll(value, LANES - first, 1)
        wide[pl.ds(j * PITCH, PERIODS), :] = value


def wide_rows(pair, part, tile):
    line = part * WIN + tile * 8
    return pl.ds(line % WIDE * PITCH + WIN * 2 // WIDE * pair + line // WIDE, 8, stride=PITCH)


def write_bias(wide, dense, first_row):
    lane = lane_ids(PERIODS)
    for i in range(DENSE):
        begin = i * LANES - BIAS_LANE
        line = begin // WIN
        value = None
        while line * WIN < begin + LANES:
            shift = line * WIN - begin
            piece = wide[pl.ds(line % WIDE * PITCH + line // WIDE, PERIODS), :]
            if shift % LANES:
                piece = pltpu.roll(piece, shift % LANES, 1)
            value = piece if value is None else jnp.where(lane >= shift, piece, value)
            line += 1
        dense[pl.ds(BIAS_ROW - first_row + i, PERIODS, stride=DENSE), :] = value


def norm_parts(rows_in):
    mean = jnp.mean(rows_in, axis=0, keepdims=True)
    centered = rows_in - mean
    var = jnp.mean(centered * centered, axis=0, keepdims=True)
    scale = lax.rsqrt(var + norm_eps)
    return centered * scale, scale


def norm_back(grad, unit, scale, gain):
    scaled = grad * gain
    first = jnp.mean(scaled, axis=0, keepdims=True)
    second = jnp.mean(scaled * unit, axis=0, keepdims=True)
    return scale * (scaled - first - unit * second)


def lane_fold(value):
    total = value[:, :LANES]
    for k in range(1, value.shape[1] // LANES):
        total = total + value[:, k * LANES : (k + 1) * LANES]
    return total


def head_rows(h):
    return slice(h * HEAD_DIM, (h + 1) * HEAD_DIM)


def head_lanes(h):
    return slice(h * LANES, (h + 1) * LANES)


def interleave(parts):
    parts = list(parts)
    live, started = [], 0
    while live or started < len(parts):
        if started < len(parts):
            live.append(parts[started])
            started += 1
        live = [part for part in live if next(part, live) is None]


def own_column(full, bits):
    heads = []
    for h in range(HEADS):
        tiles = [full[k * LEVELS : (k + 1) * LEVELS, head_lanes(h)] for k in range(LANES // LEVELS)]
        for bit in bits:
            tiles = [jnp.where(bit, b, a) for a, b in zip(tiles[::2], tiles[1::2])]
        heads.append(tiles[0])
    return jnp.concatenate(heads, axis=1)


def all_columns(own, same):
    pair = jnp.concatenate([own, own], axis=0).astype(BF16)
    tall = jnp.concatenate([pair] * (LANES // (2 * LEVELS)), axis=0)
    return jnp.concatenate([tall[:, head_lanes(h)] * same for h in range(HEADS)], axis=1)


def blend(rows_in, weights):
    pieces = []
    for h in range(0, HEADS, 2):
        pair = slice(h * HEAD_DIM, (h + 2) * HEAD_DIM)
        both = mm(rows_in[pair], weights[:, h * LANES : (h + 2) * LANES])
        pieces += [both[:HEAD_DIM, :LANES], both[HEAD_DIM:, LANES:]]
    return jnp.concatenate(pieces, axis=0)


def gather_pairs(block, weights):
    pieces = []
    for h in range(0, HEADS, 2):
        lanes = slice(h * LANES, (h + 2) * LANES)
        pieces.append(mt(block[h * HEAD_DIM : (h + 2) * HEAD_DIM, lanes], weights[:, lanes]))
    return jnp.concatenate(pieces, axis=0)


def scatter_heads(block, rows_in):
    for h in range(HEADS):
        block[head_rows(h), head_lanes(h)] = rows_in[head_rows(h), :]


def chooser(first, slots):
    ids = lax.broadcasted_iota(jnp.int32, (PICK, slots.shape[1]), 0).astype(F32).astype(BF16)
    near = jnp.clip(slots - first, -1, PICK).astype(F32).astype(BF16)
    return jnp.where(ids == near, jnp.ones((), BF16), jnp.zeros((), BF16))


def spread_windows(rows_t):
    blank = jnp.zeros((rows_t.shape[0], LANES - WIN), rows_t.dtype)
    pieces = []
    for k in range(0, rows_t.shape[1], WIN):
        pieces += [rows_t[:, k : k + WIN], blank]
    return jnp.concatenate(pieces, axis=1)


def join_windows(rows_t):
    return jnp.concatenate(
        [rows_t[:, k : k + WIN] for k in range(0, rows_t.shape[1], LANES)], axis=1
    )


def to_slots(rows_t, slots):
    tokens = rows_t.shape[1]
    pick = jnp.concatenate([chooser(k, slots) for k in range(0, tokens, PICK)], axis=0)
    return spread_windows(mm(rows_t, pick)).astype(BF16)


def from_slots(slot_rows, slots, first, rows):
    return jnp.concatenate(
        [mt(slot_rows, chooser(first + k, slots)) for k in range(0, rows, PICK)], axis=1
    )


def call(kernel, grid, ins, outs, scratch, name, macs, limit, scalars=0):
    in_specs = [s for _, s in ins]
    spec = pltpu.PrefetchScalarGridSpec(
        num_scalar_prefetch=scalars,
        grid=grid,
        in_specs=in_specs[scalars:],
        out_specs=[s for _, _, s in outs],
        scratch_shapes=scratch,
    )
    return pl.pallas_call(
        kernel,
        grid_spec=spec,
        out_shape=[jax.ShapeDtypeStruct(shape, kind) for shape, kind, _ in outs],
        compiler_params=pltpu.CompilerParams(
            dimension_semantics=("arbitrary",) * len(grid), vmem_limit_bytes=limit << 20
        ),
        cost_estimate=pl.CostEstimate(
            flops=2 * macs,
            transcendentals=0,
            bytes_accessed=sum(a.size * a.dtype.itemsize for a, _ in ins)
            + sum(math.prod(shape) * jnp.dtype(kind).itemsize for shape, kind, _ in outs),
        ),
        name=name,
    )(*[a for a, _ in ins])


def padded_rows(rows):
    return -(-(rows + 1) // 8) * 8


def whole_block(shape):
    return pl.BlockSpec(shape, lambda *_: (0,) * len(shape))


def fixed_block(array):
    return pl.BlockSpec(
        array.shape, lambda *_: (0,) * array.ndim, pipeline_mode=pl.Buffered(buffer_count=1)
    )


SLOT_BLOCK = 2048
TIGHT_BLOCK = SLOT_BLOCK // LANES * WIN
TURNS = 12
RING = 4
PICK = 256
TOKEN_BLOCK = 768


def shift_kernel(x_ref, slots_ref, out_ref, again_ref, x_t):
    @pl.when(pl.program_id(0) == 0)
    def _():
        x_t[...] = x_ref[...].astype(F32).T.astype(BF16)

    result = to_slots(x_t[...], slots_ref[...])
    out_ref[...] = result
    again_ref[...] = result


def shift_call(tokens, slots):
    count, n = tokens.shape[0], slots.shape[1] // WIN * LANES
    return call(
        shift_kernel,
        (n // SLOT_BLOCK,),
        [
            (tokens, fixed_block(tokens)),
            (slots, pl.BlockSpec((1, TIGHT_BLOCK), lambda i: (0, i))),
        ],
        [((D, n), BF16, pl.BlockSpec((D, SLOT_BLOCK), lambda i: (0, i)))] * 2,
        [pltpu.VMEM((D, count), BF16)],
        "shift",
        D * count * n,
        24,
    )


def load_dense(me_ref, parts, plan, blocks, dense, sem, order, rows):
    copies = []
    for part, first, spot, count, row in plan:
        copies.append(
            pltpu.make_async_copy(
                parts[part].at[pl.ds(first, count)],
                blocks.at[pl.ds(spot, count), pl.ds(row, parts[part].shape[1])],
                sem,
            )
        )
    for copy in copies:
        copy.start()
    for copy in copies:
        copy.wait()
    shards = blocks.shape[0]
    for shard in range(shards):
        spot = position(me_ref[0] ^ shard, order)
        dense[shard * rows : (shard + 1) * rows, :] = blocks[spot, :rows, :].astype(F32)
    if dense.shape[0] > shards * rows:
        dense[shards * rows :, :] = jnp.zeros((dense.shape[0] - shards * rows, LANES), F32)


def position(relative, order):
    spot = 0
    for place, bit in enumerate(reversed(order)):
        spot = spot + ((relative >> bit) & 1) * (1 << place)
    return spot


def band_of(table, window, me_ref, space, steps):
    if not space:
        return table[0, window]
    each = steps * (SLOT_BLOCK // LANES) // space
    return table[window // each, me_ref[0] % space * each + window % each]


def window_forward_kernel(me_ref, band_ref, *refs, parts, plan, order, rows, steps, space):
    fused = space > 0
    ins = refs[:parts]
    refs = refs[parts:]
    if fused:
        shifted_ref, slots_ref, x_ref = refs[:3]
        refs = refs[3:]
    else:
        shifted_ref, refs = refs[0], refs[1:]
    (
        out_ref,
        qkv_ref,
        mixed_ref,
        prob_ref,
        weights_ref,
        column_ref,
        vec,
        table_ref,
        blocks,
        dense,
        wide,
        bias,
        mat,
        qkv_t,
        proj_t,
        spread,
        y_all,
        band_s,
        sem,
    ) = refs
    step = pl.program_id(0)

    @pl.when(step == 0)
    def _():
        load_dense(me_ref, ins, plan, blocks, dense, sem, order, rows)
        if fused:
            lines = []
            for source in range(space):
                shard = me_ref[0] // space * space + source
                tile = blocks[position(me_ref[0] ^ shard, order), rows // 8 * 8 : rows // 8 * 8 + 8, :]
                lines.append(tile.astype(F32)[rows % 8 : rows % 8 + 1])
            table_ref[...] = jnp.concatenate(lines, axis=0).astype(jnp.int32)
            copy = pltpu.make_async_copy(table_ref, band_s, sem)
            copy.start()
            copy.wait()
        column_ref[...] = dense[COL_LO:COL_HI, :]
        read_matrix(dense, 0, "qkv1", mat)
        weights_ref[:, : 3 * D] = joined(mat, 3 * D).astype(BF16)
        qkv_t[...] = joined(mat, 3 * D).T.astype(BF16)
        read_matrix(dense, 0, "proj1", mat)
        weights_ref[:, 3 * D :] = joined(mat, D).astype(BF16)
        proj_t[...] = joined(mat, D).T.astype(BF16)
        vec[:, 0:1] = read_vector(dense, 0, "norm1_gain")
        vec[:, 1:2] = read_vector(dense, 0, "norm1_shift")
        vec[:, 2:3] = read_vector(dense, 0, "proj1_bias")
        read_bias(dense, wide)
        blank = jnp.zeros((LANES - WIN, LANES), F32)

        def turn(k, _):
            for j in range(TURNS):
                pair, part = k * (TURNS // 2) + j // 2, j % 2
                tiles = [wide[wide_rows(pair, part, tile), :] for tile in range(WIN // 8)]
                block = jnp.concatenate(tiles + [blank], axis=0).T
                bias[k * TURNS + j, :WIN, :] = block[:WIN].astype(BF16)
            return 0

        lax.fori_loop(0, LAT_BANDS * HEADS // TURNS, turn, 0)
        bias[:, WIN:, :] = jnp.full((LAT_BANDS * HEADS, KEYS - WIN, LANES), -jnp.inf, BF16)
        spread[...] = jnp.zeros_like(spread)

    @pl.when(step < steps)
    def _():
        per_step = SLOT_BLOCK // LANES
        unit, _ = norm_parts(shifted_ref[...].astype(F32))
        normed = (unit * vec[:, 0:1] + vec[:, 1:2]).astype(BF16)
        qkv = mm(qkv_t[...], normed).astype(BF16)
        qkv_ref[...] = qkv
        blank = jnp.zeros((LANES - KEYS, HEADS * LANES), BF16)
        scores, probs, mixed = {}, {}, []
        for turn in range(per_step + 2):
            if turn < per_step:
                lanes = slice(turn * LANES, (turn + 1) * LANES)
                scatter_heads(spread.at[turn % RING], qkv[:D, lanes])
                scores[turn] = mm(qkv[D : 2 * D, lanes].T[:KEYS], spread[turn % RING])
            if 1 <= turn <= per_step:
                w = turn - 1
                table = band_s if fused else band_ref
                band = band_of(table, step * per_step + w, me_ref, space, steps)
                heads = []
                for h in range(HEADS):
                    score = scores[w][:, head_lanes(h)] * SCALE + bias[band * HEADS + h].astype(F32)
                    grown = jnp.exp(score - jnp.max(score, axis=0, keepdims=True))
                    heads.append(
                        (grown * (1.0 / jnp.sum(grown, axis=0, keepdims=True))).astype(BF16)
                    )
                probs[w] = jnp.concatenate(heads, axis=1)
                prob_ref[w] = probs[w]
            if turn >= 2:
                w = turn - 2
                tall = jnp.concatenate([probs[w], blank], axis=0)
                mixed.append(blend(qkv[2 * D :, w * LANES : (w + 1) * LANES], tall))
        mixed = jnp.concatenate(mixed, axis=1).astype(BF16)
        mixed_ref[...] = mixed
        result = mm(proj_t[...], mixed) + vec[:, 2:3]
        if fused:
            spot = pl.ds(pl.multiple_of(step * TIGHT_BLOCK, TIGHT_BLOCK), TIGHT_BLOCK)
            y_all[:, spot] = join_windows(result).astype(BF16)
        else:
            out_ref[...] = result.astype(BF16)

    if fused:

        @pl.when(step >= steps)
        def _():
            branch = from_slots(
                y_all[...], slots_ref[...], (step - steps) * TOKEN_BLOCK, TOKEN_BLOCK
            )
            out_ref[...] = x_ref[...].astype(F32).T + branch


def window_forward_call(me, bands, parts, plan, order, shards, rows, shifted, tokens, slots, space):
    fused = space > 0
    n = shifted.shape[1]
    steps = n // SLOT_BLOCK
    per_step = SLOT_BLOCK // LANES
    padded = padded_rows(rows)
    flat_rows = max(shards * rows, BIAS_ROW + DENSE * PERIODS + 16)
    slot_block = lambda r: pl.BlockSpec((r, SLOT_BLOCK), lambda i, *_: (0, jnp.minimum(i, steps - 1)))
    ins = [(me, None), (bands, None)]
    ins += [(p, pl.BlockSpec(memory_space=pl.ANY)) for p in parts]
    ins += [(shifted, slot_block(D))]
    if fused:
        count = tokens.shape[0]
        late = lambda i: jnp.maximum(i - steps, 0)
        ins += [
            (slots, fixed_block(slots)),
            (tokens, pl.BlockSpec((TOKEN_BLOCK, D), lambda i, *_: (late(i), 0))),
        ]
        first = ((D, count), F32, pl.BlockSpec((D, TOKEN_BLOCK), lambda i, *_: (0, late(i))))
        grid = steps + count // TOKEN_BLOCK
    else:
        first = ((D, n), BF16, slot_block(D))
        grid = steps
    outs = [
        first,
        ((3 * D, n), BF16, slot_block(3 * D)),
        ((D, n), BF16, slot_block(D)),
        (
            (n // LANES, KEYS, HEADS * LANES),
            BF16,
            pl.BlockSpec(
                (per_step, KEYS, HEADS * LANES), lambda i, *_: (jnp.minimum(i, steps - 1), 0, 0)
            ),
        ),
        ((D, 4 * D), BF16, whole_block((D, 4 * D))),
        ((COL_HI - COL_LO, LANES), F32, whole_block((COL_HI - COL_LO, LANES))),
        ((D, LANES), F32, whole_block((D, LANES))),
        ((max(space, 1), LANES), jnp.int32, whole_block((max(space, 1), LANES))),
    ]
    scratch = [
        pltpu.VMEM((shards, padded, LANES), BF16),
        pltpu.VMEM((flat_rows, LANES), F32),
        pltpu.VMEM((WIDE * PITCH, LANES), F32),
        pltpu.VMEM((LAT_BANDS * HEADS, KEYS, LANES), BF16),
        pltpu.VMEM((5, D, LANES), F32),
        pltpu.VMEM((3 * D, D), BF16),
        pltpu.VMEM((D, D), BF16),
        pltpu.VMEM((RING, D, HEADS * LANES), BF16),
        pltpu.VMEM((D, n // LANES * WIN), BF16),
        pltpu.SMEM((max(space, 1), LANES), jnp.int32),
        pltpu.SemaphoreType.DMA,
    ]
    kernel = functools.partial(
        window_forward_kernel,
        parts=len(parts),
        plan=plan,
        order=order,
        rows=rows,
        steps=steps,
        space=space,
    )
    return call(kernel, (grid,), ins, outs, scratch, "window_forward", 12 * D * D * n, 36, scalars=2)


COLUMN_BLOCK = 768
COLUMN_PART = 768
COLUMN_VECTORS = (
    "norm2_gain",
    "norm2_shift",
    "proj2_bias",
    "norm3_gain",
    "norm3_shift",
    "mlp_out_bias",
)
COLUMN_MATRICES = ("qkv2", "proj2", "mlp_in", "mlp_out")


def column_kernel(
    dense,
    x_ref,
    cot_ref,
    count_ref,
    out_ref,
    after_ref,
    branch_ref,
    grad_ref,
    mat,
    tall,
    w_qkv,
    w_proj,
    w_in,
    w_out,
    t_qkv,
    t_proj,
    t_in,
    t_out,
    vec,
    fvec,
    grad_qkv,
    grad_proj,
    grad_in,
    grad_out,
    sums,
    fsums,
    spread,
):
    step = pl.program_id(0)

    @pl.when(step == 0)
    def _():
        for name, plain, turned in (
            ("qkv2", w_qkv, t_qkv),
            ("proj2", w_proj, t_proj),
            ("mlp_in", w_in, t_in),
            ("mlp_out", w_out, t_out),
        ):
            rows, width = plain.shape
            source = tall if rows == FF else mat
            read_matrix(dense, COL_LO, name, source)
            plain[...] = joined(source, width).astype(BF16)
            turned[...] = joined(source, width).T.astype(BF16)
        for k, name in enumerate(COLUMN_VECTORS):
            vec[:, k : k + 1] = read_vector(dense, COL_LO, name)
        fvec[:, 0:1] = read_vector(dense, COL_LO, "mlp_in_bias")
        sums[...] = jnp.zeros_like(sums)
        fsums[...] = jnp.zeros_like(fsums)
        for grad in (grad_qkv, grad_proj, grad_in, grad_out):
            grad[...] = jnp.zeros_like(grad)
        spread[...] = jnp.zeros_like(spread)

    gain2, shift2, bias2, gain3, shift3, bias_out = [vec[:, k : k + 1] for k in range(6)]
    key_id = lax.broadcasted_iota(jnp.int32, (LANES, LANES), 0)
    query_id = lax.broadcasted_iota(jnp.int32, (LANES, LANES), 1)
    same = jnp.where(key_id // LEVELS == query_id // LEVELS, 1.0, 0.0).astype(BF16)
    column = lax.broadcasted_iota(jnp.int32, (LEVELS, LANES), 1) // LEVELS
    bits = [(column >> k) & 1 == 1 for k in range(4)]
    level = lax.broadcasted_iota(jnp.int32, (LEVELS, LANES), 0)
    groups = COLUMN_PART // LANES

    def part_steps(part):
        here = slice(part * COLUMN_PART, (part + 1) * COLUMN_PART)
        x = x_ref[:, here]
        unit2, scale2 = norm_parts(x)
        n2 = (unit2 * gain2 + shift2).astype(BF16)
        yield
        qkv = mm(t_qkv[...], n2).astype(BF16)
        yield
        scores = []
        for g in range(groups):
            lanes = slice(g * LANES, (g + 1) * LANES)
            scatter_heads(spread.at[0, part * groups + g], qkv[:D, lanes])
            scores.append(own_column(mm(qkv[D : 2 * D, lanes].T, spread[0, part * groups + g]), bits))
        yield
        probs, tall_probs = [], []
        for g in range(groups):
            begin = part * COLUMN_PART + g * LANES
            valid = level < count_ref[:, begin : begin + LANES]
            score = jnp.where(jnp.concatenate([valid] * HEADS, axis=1), scores[g] * SCALE, -jnp.inf)
            grown = jnp.exp(score - jnp.max(score, axis=0, keepdims=True))
            prob = grown * (1.0 / jnp.sum(grown, axis=0, keepdims=True))
            probs.append(prob)
            tall_probs.append(all_columns(prob, same))
        yield
        mixed = [
            blend(qkv[2 * D :, g * LANES : (g + 1) * LANES], tall_probs[g]) for g in range(groups)
        ]
        mixed = jnp.concatenate(mixed, axis=1).astype(BF16)
        projected = mm(t_proj[...], mixed)
        yield
        middle = x + (projected + bias2)
        unit3, scale3 = norm_parts(middle)
        n3 = (unit3 * gain3 + shift3).astype(BF16)
        yield
        pre = mm(t_in[...], n3)
        cot = cot_ref[here, :].astype(F32).T
        cot_bf = cot.astype(BF16)
        dact = mm(w_out[...], cot_bf)
        yield
        pre = pre + fvec[:, 0:1]
        root = math.sqrt(2.0 / math.pi)
        square = pre * pre
        share = 0.5 + 0.5 * jnp.tanh(pre * (root + (root * 0.044715) * square))
        act = pre * share
        slope = share + act * (1.0 - share) * (2.0 * root + (6.0 * root * 0.044715) * square)
        act = act.astype(BF16)
        dpre = (dact * slope).astype(BF16)
        yield
        output = middle + (mm(t_out[...], act) + bias_out)
        out_ref[here, :] = output.T.astype(BF16)
        dn3 = mm(w_in[...], dpre)
        grad_out[...] += mt(act, cot_bf)
        grad_in[...] += mt(n3, dpre)
        yield
        dmiddle = cot + norm_back(dn3, unit3, scale3, gain3)
        dattn = dmiddle.astype(BF16)
        sums[2] += lane_fold(dattn.astype(F32))
        sums[3] += lane_fold(dn3 * unit3)
        sums[4] += lane_fold(dn3)
        sums[5] += lane_fold(cot_bf.astype(F32))
        fsums[...] += lane_fold(dpre.astype(F32))
        yield
        dmixed = mm(w_proj[...], dattn).astype(BF16)
        grad_proj[...] += mt(mixed, dattn)
        dprobs = []
        for g in range(groups):
            lanes = slice(g * LANES, (g + 1) * LANES)
            scatter_heads(spread.at[1, part * groups + g], dmixed[:, lanes])
            dprobs.append(own_column(mm(qkv[2 * D :, lanes].T, spread[1, part * groups + g]), bits))
        yield
        dscores = []
        for prob, dprob in zip(probs, dprobs):
            dscore = prob * (dprob - jnp.sum(prob * dprob, axis=0, keepdims=True))
            dscores.append(all_columns(dscore, same))
        yield
        dq, dk, dv = [], [], []
        for g in range(groups):
            dq.append(blend(qkv[D : 2 * D, g * LANES : (g + 1) * LANES], dscores[g]) * SCALE)
            dk.append(gather_pairs(spread.at[0, part * groups + g], dscores[g]) * SCALE)
            dv.append(gather_pairs(spread.at[1, part * groups + g], tall_probs[g]))
        dqkv = [jnp.concatenate(d, axis=1) for d in (dq, dk, dv)]
        dqkv = jnp.concatenate(dqkv, axis=0).astype(BF16)
        dn2 = mm(w_qkv[...], dqkv)
        grad_qkv[...] += mt(n2, dqkv)
        yield
        dafter = dmiddle + norm_back(dn2, unit2, scale2, gain2)
        after_ref[:, here] = dafter
        branch_ref[:, here] = dafter.astype(BF16)
        sums[0] += lane_fold(dn2 * unit2)
        sums[1] += lane_fold(dn2)

    interleave([part_steps(part) for part in range(COLUMN_BLOCK // COLUMN_PART)])

    @pl.when(step == pl.num_programs(0) - 1)
    def _():
        grad_ref[...] = jnp.zeros_like(grad_ref)
        split_into(mat, grad_qkv[...])
        write_matrix(grad_ref, COL_LO, "qkv2", mat)
        split_into(mat, grad_proj[...])
        write_matrix(grad_ref, COL_LO, "proj2", mat)
        split_into(mat, grad_in[...])
        write_matrix(grad_ref, COL_LO, "mlp_in", mat)
        split_into(tall, grad_out[...])
        write_matrix(grad_ref, COL_LO, "mlp_out", tall)
        for k, name in enumerate(COLUMN_VECTORS):
            write_vector(grad_ref, COL_LO, name, sums[k])
        write_vector(grad_ref, COL_LO, "mlp_in_bias", fsums[...])


def column_call(dense, after_t, cotangent, counts):
    n = after_t.shape[1]
    feature = lambda r: pl.BlockSpec((r, COLUMN_BLOCK), lambda i: (0, i))
    token = pl.BlockSpec((COLUMN_BLOCK, D), lambda i: (i, 0))
    return call(
        column_kernel,
        (n // COLUMN_BLOCK,),
        [
            (dense, fixed_block(dense)),
            (after_t, feature(D)),
            (cotangent, token),
            (counts, feature(1)),
        ],
        [
            ((n, D), BF16, token),
            ((D, n), F32, feature(D)),
            ((D, n), BF16, feature(D)),
            (dense.shape, F32, whole_block(dense.shape)),
        ],
        [
            pltpu.VMEM((FF // LANES, D, LANES), F32),
            pltpu.VMEM((2, FF, LANES), F32),
            pltpu.VMEM((D, 3 * D), BF16),
            pltpu.VMEM((D, D), BF16),
            pltpu.VMEM((D, FF), BF16),
            pltpu.VMEM((FF, D), BF16),
            pltpu.VMEM((3 * D, D), BF16),
            pltpu.VMEM((D, D), BF16),
            pltpu.VMEM((FF, D), BF16),
            pltpu.VMEM((D, FF), BF16),
            pltpu.VMEM((D, LANES), F32),
            pltpu.VMEM((FF, LANES), F32),
            pltpu.VMEM((D, 3 * D), F32),
            pltpu.VMEM((D, D), F32),
            pltpu.VMEM((D, FF), F32),
            pltpu.VMEM((FF, D), F32),
            pltpu.VMEM((6, D, LANES), F32),
            pltpu.VMEM((FF, LANES), F32),
            pltpu.VMEM((2, COLUMN_BLOCK // LANES, D, HEADS * LANES), BF16),
        ],
        "column",
        40 * D * D * n,
        40,
    )


def window_backward_kernel(me_ref, band_ref, *refs, order, shard_rows, space):
    fused = space > 0
    if fused:
        slots_ref, refs = refs[0], refs[1:]
    (
        grad_ref,
        weights_ref,
        vec,
        column_ref,
        shifted_ref,
        qkv_ref,
        mixed_ref,
        prob_ref,
        out_ref,
        keep_ref,
        send_ref,
        total,
        wide,
        dense,
        mat,
        blocks,
        spread,
        grad_qkv,
        grad_proj,
        sums,
        sem,
    ) = refs
    step = pl.program_id(0)
    per_step = SLOT_BLOCK // LANES

    @pl.when(step == 0)
    def _():
        total[...] = jnp.zeros_like(total)
        sums[...] = jnp.zeros_like(sums)
        grad_qkv[...] = jnp.zeros_like(grad_qkv)
        grad_proj[...] = jnp.zeros_like(grad_proj)
        spread[...] = jnp.zeros_like(spread)

    if fused:
        grad = to_slots(grad_ref[...], slots_ref[...])
    else:
        grad = grad_ref[...]
    grad_proj[...] += mt(mixed_ref[...], grad)
    dmixed = mm(weights_ref[:, 3 * D :], grad).astype(BF16)
    qkv = qkv_ref[...]
    blank = jnp.zeros((LANES - KEYS, HEADS * LANES), BF16)
    dq, dk, dv, dprobs, dscores = [], [], [], {}, {}
    for turn in range(per_step + 2):
        if turn < per_step:
            lanes = slice(turn * LANES, (turn + 1) * LANES)
            scatter_heads(spread.at[0, turn % RING], qkv[:D, lanes])
            scatter_heads(spread.at[1, turn % RING], dmixed[:, lanes])
            dprobs[turn] = mm(qkv[2 * D :, lanes].T[:KEYS], spread[1, turn % RING])
        if 1 <= turn <= per_step:
            w = turn - 1
            heads = []
            for h in range(HEADS):
                prob = prob_ref[w, :, head_lanes(h)].astype(F32)
                dprob = dprobs[w][:, head_lanes(h)]
                heads.append(
                    (prob * (dprob - jnp.sum(prob * dprob, axis=0, keepdims=True))).astype(BF16)
                )
            dscores[w] = jnp.concatenate(heads, axis=1)
            band = band_of(band_ref, step * per_step + w, me_ref, space, pl.num_programs(0))
            for h in range(HEADS):
                spot = pl.ds(pl.multiple_of((band * HEADS + h) * KEYS, 8), KEYS)
                total[spot, :] += heads[h].astype(F32)
        if turn >= 2:
            w = turn - 2
            tall = jnp.concatenate([dscores[w], blank], axis=0)
            dq.append(blend(qkv[D : 2 * D, w * LANES : (w + 1) * LANES], tall) * SCALE)
            dk.append(gather_pairs(spread.at[0, w % RING], tall) * SCALE)
            tall = jnp.concatenate([prob_ref[w], blank], axis=0)
            dv.append(gather_pairs(spread.at[1, w % RING], tall))
    dqkv = jnp.concatenate([jnp.concatenate(d, axis=1) for d in (dq, dk, dv)], axis=0).astype(BF16)
    unit, scale = norm_parts(shifted_ref[...].astype(F32))
    grad_qkv[...] += mt((unit * vec[:, 0:1] + vec[:, 1:2]).astype(BF16), dqkv)
    dnormed = mm(weights_ref[:, : 3 * D], dqkv)
    dshifted = norm_back(dnormed, unit, scale, vec[:, 0:1])
    out_ref[...] = (join_windows(dshifted) if fused else dshifted).astype(BF16)
    for k, value in enumerate((dnormed * unit, dnormed, grad.astype(F32))):
        sums[k] += lane_fold(value)

    @pl.when(step == pl.num_programs(0) - 1)
    def _():
        for j in range(WIDE):
            wide[j * PITCH + USED : (j + 1) * PITCH, :] = jnp.zeros((PITCH - USED, LANES), F32)
        blank = jnp.zeros((WIN, LANES - KEYS), F32)

        def turn(k, _):
            for j in range(TURNS):
                pair, part = k * (TURNS // 2) + j // 2, j % 2
                spot = pl.ds(pl.multiple_of((k * TURNS + j) * KEYS, 8), KEYS)
                block = jnp.concatenate([total[spot, :].T[:WIN], blank], axis=1)
                for tile in range(WIN // 8):
                    wide[wide_rows(pair, part, tile), :] = block[tile * 8 : tile * 8 + 8]
            return 0

        lax.fori_loop(0, LAT_BANDS * HEADS // TURNS, turn, 0)
        dense[:COL_LO, :] = jnp.zeros((COL_LO, LANES), F32)
        write_bias(wide, dense, 0)
        covered = BIAS_ROW + DENSE * PERIODS
        dense[covered:, :] = jnp.zeros((dense.shape[0] - covered, LANES), F32)
        both = column_ref[COL_HI - COL_LO - 16 :, :]
        rows = lax.broadcasted_iota(jnp.int32, both.shape, 0) + (COL_HI - 16)
        lane = lane_ids(16)
        start = rows * LANES + lane < OFFSET["earth_bias"]
        dense[COL_LO : COL_HI - 16, :] = column_ref[: COL_HI - COL_LO - 16, :]
        dense[COL_HI - 16 : COL_HI, :] = jnp.where(start, both, dense[COL_HI - 16 : COL_HI, :])
        split_into(mat, grad_qkv[...])
        write_matrix(dense, 0, "qkv1", mat)
        split_into(mat, grad_proj[...])
        write_matrix(dense, 0, "proj1", mat)
        for k, name in enumerate(("norm1_gain", "norm1_shift", "proj1_bias")):
            write_vector(dense, 0, name, sums[k])
        shards, rows = blocks.shape[0], shard_rows
        for shard in range(shards):
            spot = position(me_ref[0] ^ shard, order)
            blocks[spot, :rows, :] = dense[shard * rows : (shard + 1) * rows, :].astype(BF16)
        first = pltpu.make_async_copy(blocks.at[pl.ds(0, shards // 2)], keep_ref, sem.at[0])
        second = pltpu.make_async_copy(
            blocks.at[pl.ds(shards // 2, shards // 2)], send_ref, sem.at[1]
        )
        first.start()
        second.start()
        first.wait()
        second.wait()


def window_backward_call(
    me, bands, order, shards, rows, slots, grad, weights, vec, column_grad, shifted, qkv, mixed, prob, space
):
    fused = space > 0
    padded = padded_rows(rows)
    n = shifted.shape[1]
    per_step = SLOT_BLOCK // LANES
    slot_block = lambda r: pl.BlockSpec((r, SLOT_BLOCK), lambda i, *_: (0, i))
    ins = [(me, None), (bands, None)]
    if fused:
        tight = pl.BlockSpec((1, TIGHT_BLOCK), lambda i, *_: (0, i))
        ins += [(slots, tight), (grad, fixed_block(grad))]
    else:
        ins += [(grad, slot_block(D))]
    ins += [
        (weights, fixed_block(weights)),
        (vec, fixed_block(vec)),
        (column_grad, fixed_block(column_grad)),
        (shifted, slot_block(D)),
        (qkv, slot_block(3 * D)),
        (mixed, slot_block(D)),
        (
            prob,
            pl.BlockSpec((per_step, KEYS, HEADS * LANES), lambda i, *_: (i, 0, 0)),
        ),
    ]
    flat_rows = max(shards * rows, BIAS_ROW + DENSE * PERIODS + 16)
    if fused:
        tight = pl.BlockSpec((D, TIGHT_BLOCK), lambda i, *_: (0, i))
        first = ((D, n // LANES * WIN), BF16, tight)
    else:
        first = ((D, n), BF16, slot_block(D))
    outs = [
        first,
        ((shards // 2, padded, LANES), BF16, pl.BlockSpec(memory_space=pl.ANY)),
        ((shards // 2, padded, LANES), BF16, pl.BlockSpec(memory_space=pl.ANY)),
    ]
    scratch = [
        pltpu.VMEM((LAT_BANDS * HEADS * KEYS, LANES), F32),
        pltpu.VMEM((WIDE * PITCH, LANES), F32),
        pltpu.VMEM((flat_rows, LANES), F32),
        pltpu.VMEM((5, D, LANES), F32),
        pltpu.VMEM((shards, padded, LANES), BF16),
        pltpu.VMEM((2, RING, D, HEADS * LANES), BF16),
        pltpu.VMEM((D, 3 * D), F32),
        pltpu.VMEM((D, D), F32),
        pltpu.VMEM((3, D, LANES), F32),
        pltpu.SemaphoreType.DMA((2,)),
    ]
    kernel = functools.partial(
        window_backward_kernel, order=order, shard_rows=rows, space=space
    )
    return call(kernel, (n // SLOT_BLOCK,), ins, outs, scratch, "window_backward", 24 * D * D * n, 40, scalars=2)


def finish_kernel(shift_ref, slots_ref, after_ref, out_ref):
    first = pl.program_id(0) * TOKEN_BLOCK
    back = from_slots(shift_ref[...], slots_ref[...], first, TOKEN_BLOCK)
    out_ref[...] = (after_ref[...] + back).T


def finish_call(grad_shifted, slots, after_t):
    n = after_t.shape[1]
    return call(
        finish_kernel,
        (n // TOKEN_BLOCK,),
        [
            (grad_shifted, fixed_block(grad_shifted)),
            (slots, fixed_block(slots)),
            (after_t, pl.BlockSpec((D, TOKEN_BLOCK), lambda i: (0, i))),
        ],
        [((n, D), F32, pl.BlockSpec((TOKEN_BLOCK, D), lambda i: (i, 0)))],
        [],
        "finish",
        D * n * slots.shape[1],
        24,
    )[0]


def body(block_input, cotangent, params, send_rows, window_band, level_count):
    model_width = block_input.shape[-1]
    rows_dev = block_input.shape[1] * block_input.shape[2]
    n_space, per_peer = send_rows.shape[1], send_rows.shape[3]
    devices = lax.axis_size(("dp", "space"))
    group = WIN // math.gcd(per_peer, WIN)
    if n_space % group:
        group = n_space
    fused = group == 1
    dest = n_space // group
    per_dest = group * per_peer // WIN
    member_groups = [[first + k for k in range(group)] for first in range(0, n_space, group)]
    place = lax.axis_index("space")
    index = lax.axis_index(("dp", "space"))
    me = index.astype(jnp.int32).reshape(1)
    bits = devices.bit_length() - 1
    order = [0] + list(range(bits - 1, 0, -1))

    def swap(value, *across):
        flip = sum(1 << bit for bit in across)
        return lax.ppermute(value, ("dp", "space"), [(k, k ^ flip) for k in range(devices)])

    def exchange(value):
        return lax.all_to_all(
            value, "space", split_axis=0, concat_axis=0, tiled=True, axis_index_groups=member_groups
        )

    def to_windows(rows):
        moved = exchange(rows[route_flat]).reshape(group, dest, per_peer, model_width)
        windows = moved.transpose(1, 0, 2, 3).reshape(-1, WIN, model_width)
        windows = jnp.pad(windows, ((0, 0), (0, LANES - WIN), (0, 0)))
        return windows.reshape(-1, model_width).T

    def from_windows(rows_t):
        rows = rows_t.T.reshape(-1, LANES, model_width)[:, :WIN]
        moved = rows.reshape(dest, group, per_peer, model_width).transpose(1, 0, 2, 3)
        rows = exchange(moved.reshape(rows_dev, model_width))
        return jnp.zeros((rows_dev, model_width), rows.dtype).at[route_flat].set(rows)

    flat_in = block_input[0].reshape(rows_dev, model_width)
    routes = send_rows[0, :, 0, :]
    route_flat = routes.reshape(-1)
    slots = routes.reshape(1, -1)
    if fused:
        bands = jnp.zeros((1, LANES), jnp.int32)
    else:
        all_bands = lax.all_gather(window_band[0], "space", axis=0)
        bands = lax.dynamic_slice(
            all_bands, ((place % group) * dest, (place // group) * per_dest), (dest, per_dest)
        ).reshape(1, -1)
        shifted = shifted_again = to_windows(flat_in)

    shard_rows = params.shape[0] // LANES
    padded = padded_rows(shard_rows)
    band_row = jnp.pad(window_band[0], (0, LANES - window_band.shape[1])).astype(BF16)
    own_rows = jnp.pad(params.reshape(shard_rows, LANES), ((0, padded - shard_rows), (0, 0)))
    row_id = lax.broadcasted_iota(jnp.int32, (padded, 1), 0)
    held = jnp.where(row_id == shard_rows, band_row[None, :], own_rows.astype(BF16))[None]
    near, far = order[-1], order[-2]
    direct = [swap(held, near), swap(held, far), swap(held, near, far)]
    held = jnp.concatenate([held] + direct, axis=0)
    for bit in reversed(order[3:-2]):
        held = jnp.concatenate([held, swap(held, bit)], axis=0)
    top, next_top = order[1], order[2]
    cut = padded // 16 * 8
    upper, lower = held[:, :cut], held[:, cut:]
    upper = jnp.concatenate([upper, swap(upper, next_top)], axis=0)
    lower = jnp.concatenate([lower, swap(lower, top)], axis=0)
    parts = [upper, swap(upper, top), lower, swap(lower, next_top)]
    if fused:
        _, slots = lax.optimization_barrier((parts, slots))
        shifted, shifted_again = shift_call(flat_in, slots)
    parts = parts + [swap(part, order[0]) for part in parts]
    few = devices // 8
    plan = []
    for core in range(2):
        base = core * 4 * few
        plan += [(4 * core, 0, base, 2 * few, 0), (4 * core + 1, 0, base + 2 * few, 2 * few, 0)]
        for part, spot in ((2, 0), (3, few)):
            plan += [
                (4 * core + part, 0, base + spot, few, cut),
                (4 * core + part, few, base + spot + 2 * few, few, cut),
            ]
    space = n_space if fused else 0
    first, qkv, mixed, prob, weights, column_rows, vec, table = window_forward_call(
        me, bands, parts, plan, order, devices, shard_rows, shifted, flat_in, slots, space
    )
    if fused:
        bands = table
    if fused:
        after_t = first
    else:
        after_t = (flat_in.astype(F32) + from_windows(first).astype(F32)).T
    counts = jnp.repeat(level_count[0], LEVELS).reshape(1, -1)
    output, grad_after, grad_branch, column_grad = column_call(
        column_rows, after_t, cotangent[0].reshape(rows_dev, model_width), counts
    )
    if not fused:
        grad_branch = to_windows(grad_branch.T)
    grad_shifted, keep, send = window_backward_call(
        me, bands, order, devices, shard_rows, slots, grad_branch, weights, vec, column_grad,
        shifted_again, qkv, mixed, prob, space
    )
    total = keep.astype(F32) + swap(send, order[0]).astype(F32)
    total, grad_shifted = lax.optimization_barrier((total, grad_shifted))
    if fused:
        input_grad = finish_call(grad_shifted, slots, grad_after)
    else:
        input_grad = grad_after.T + from_windows(grad_shifted).astype(F32)

    def fold(kept, sent, *across):
        return kept + swap(sent.astype(BF16), *across).astype(F32)

    upper = total[:, :cut]
    lower = total[:, cut:].reshape(2, 2, few, padded - cut, LANES)
    upper = fold(upper[: 2 * few], upper[2 * few :], top)
    lower = fold(lower[:, 0], lower[:, 1], next_top)
    upper, lower, input_grad = lax.optimization_barrier((upper, lower, input_grad))
    upper = fold(upper[:few], upper[few:], next_top)
    lower = fold(lower[0], lower[1], top)
    total = jnp.concatenate([upper, lower], axis=1)
    for bit in order[3:-2]:
        half = total.shape[0] // 2
        total = fold(total[:half], total[half:], bit)
    own = total[0]
    for k, across in ((1, (near,)), (2, (far,)), (3, (near, far))):
        own = fold(own, total[k], *across)
    total = own[:shard_rows]
    return (
        output.reshape(block_input.shape),
        input_grad.reshape(block_input.shape),
        total.reshape(-1),
    )


def solution(mesh):
    return jax.shard_map(
        body,
        mesh=mesh,
        in_specs=(
            P("dp", "space", None, None),
            P("dp", "space", None, None),
            P(("dp", "space")),
            P("dp", None, "space", None),
            P("dp", "space"),
            P("dp", "space"),
        ),
        out_specs=(P("dp", "space", None, None), P("dp", "space", None, None), P(("dp", "space"))),
        check_vma=False,
    )
```
